32 devices in a mesh: pb: 8 (over z, x), sa: 4 (over y, core).
Axes of the slice: x: 2, y: 2, z: 4, core: 2. Of those that a mesh axis runs over, the one named last changes fastest.
Arguments:
- question_states: bfloat16 [8, 4, 256, 768], P('pb', 'sa'), may hold values from -16 to 16
- question_ids: int32 [8, 4, 256], P('pb'), may hold values from 0 to 30521, as said below
- q_inner_weight: bfloat16 [768, 3072], P(None, 'sa'), may hold values from -0.21875 to 0.21875
- q_outer_weight: bfloat16 [3072, 768], P('sa'), may hold values from -0.109375 to 0.109375
- q_norm_gain: float32 [768], replicated, may hold values from 0.1 to 1.9
- sql_states: bfloat16 [4, 8, 256, 768], P('sa', 'pb'), may hold values from -16 to 16
- sql_ids: int32 [4, 8, 256], P('sa'), may hold values from 0 to 32099, as said below
- s_inner_weight: bfloat16 [768, 3072], P(None, 'pb'), may hold values from -0.21875 to 0.21875
- s_outer_weight: bfloat16 [3072, 768], P('pb'), may hold values from -0.109375 to 0.109375
- s_norm_gain: float32 [768], replicated, may hold values from 0.1 to 1.9
- positive_column: int32 [32], P('pb'), may hold values from 0 to 31, each once
Outputs:
- loss: float32 [], replicated
- q_inner_grad: float32 [768, 3072], P(None, 'sa')
- q_outer_grad: float32 [3072, 768], P('sa')
- q_gain_grad: float32 [768], replicated
- s_inner_grad: float32 [768, 3072], P(None, 'pb')
- s_outer_grad: float32 [3072, 768], P('pb')
- s_gain_grad: float32 [768], replicated
The draws below stay inside these ranges and needn't reach their ends.
Inputs may be any that keep to these rules, and one draw needn't show every extreme that they name: `question_ids`: each sequence is a run of nonzero ids followed by padding zeros, the run 3 * 64 long or longer. `sql_ids`: each sequence is a run of nonzero ids followed by padding zeros, the run 3 * 64 long or longer.
All inputs are finite; a program needn't handle non-finite values.
Results may differ from the reference program's by a relative error of at most 0.0051.
Values may be sent and summed in bfloat16 or wider, within the bound.
No kernel may reach another device: no remote copies, remote signals or barrier semaphores. Data moves between devices by JAX's collectives and lax.ppermute only.
A program may use at most 128 MiB of HBM per device.

```python
import math
import jax
import jax.numpy as jnp
from jax import lax

D = 768
FF = 3072
VOCAB_Q = 30522
VOCAB_S = 32100
SEQ = 256
G_Q = 4
G_S = 8
BATCH = 32
N_PB = 8
N_SA = 4


def rough_states(key, first, shape):
    values = jax.random.normal(jax.random.fold_in(key, first), shape, jnp.float32)
    return jnp.clip(values, -6.0, 6.0)


def draw_question_states(key, part):
    shape = (N_PB, G_Q, SEQ, D)
    states = rough_states(key, 1, shape)
    return states.astype(jnp.bfloat16)


def draw_sql_states(key, part):
    shape = (N_SA, G_S, SEQ, D)
    states = rough_states(key, 7, shape)
    return states.astype(jnp.bfloat16)


def padded_ids(key, first, shape, vocab):
    shortest = 3 * SEQ // 4
    lengths = jax.random.randint(jax.random.fold_in(key, first), shape[:2] + (1,), shortest, SEQ + 1)
    lengths = lengths.at[:, 0, :].set(SEQ)
    lengths = lengths.at[:, 1, :].set(shortest)
    tokens = jax.random.randint(jax.random.fold_in(key, first + 1), shape, 1, vocab)
    tokens = tokens.at[:, 0, 0].set(vocab - 1)
    places = jnp.arange(SEQ, dtype=jnp.int32)[None, None, :]
    return jnp.where(places < lengths, tokens, 0).astype(jnp.int32)


def draw_question_ids(key, part):
    return padded_ids(key, 3, (N_PB, G_Q, SEQ), VOCAB_Q)


def draw_sql_ids(key, part):
    return padded_ids(key, 5, (N_SA, G_S, SEQ), VOCAB_S)


def levels(rng, dims, split, smallest, high):
    level = 1.0
    for axis_at, blocks in split:
        draws = jax.random.uniform(jax.random.fold_in(jax.random.fold_in(rng, 6), axis_at), (blocks,), jnp.float32, smallest / len(split), high / len(split))
        level = level * jnp.repeat(jnp.exp(draws), dims[axis_at] // blocks).reshape((-1,) + (1,) * (len(dims) - 1 - axis_at))
    return level


def bell_draw(key, dims, scale, bound, pieces=(), kind=jnp.bfloat16):
    result = scale * jax.random.normal(key, dims, jnp.float32)
    if pieces:
        result = result * levels(key, dims, pieces, -0.22, 0.18)
    return jnp.clip(result, -bound, bound).astype(kind)


def setup_inputs(seed: int = 0) -> dict:
    key_of = jax.random.split(jax.random.key(seed), 12)
    question_states = draw_question_states(jax.random.fold_in(key_of[11], 71), 0)
    question_ids = draw_question_ids(jax.random.fold_in(key_of[11], 71), 0)
    q_inner_weight = bell_draw(key_of[2], (D, FF), D ** -0.5, 0.21875, ((1, 4),))
    q_outer_weight = bell_draw(key_of[3], (FF, D), FF ** -0.5, 0.109375, ((0, 4),))
    q_norm_gain = jnp.clip(1.0 + 0.18 * jax.random.normal(key_of[4], (D,), jnp.float32), 0.1, 1.9)
    sql_states = draw_sql_states(jax.random.fold_in(key_of[11], 71), 0)
    sql_ids = draw_sql_ids(jax.random.fold_in(key_of[11], 71), 0)
    s_inner_weight = bell_draw(key_of[7], (D, FF), D ** -0.5, 0.21875, ((1, 8),))
    s_outer_weight = bell_draw(key_of[8], (FF, D), FF ** -0.5, 0.109375, ((0, 8),))
    s_norm_gain = jnp.clip(1.0 + 0.18 * jax.random.normal(key_of[9], (D,), jnp.float32), 0.1, 1.9)
    positive_column = jax.random.permutation(key_of[10], BATCH).astype(jnp.int32)
    return dict(question_states=question_states, question_ids=question_ids, q_inner_weight=q_inner_weight, q_outer_weight=q_outer_weight, q_norm_gain=q_norm_gain, sql_states=sql_states, sql_ids=sql_ids, s_inner_weight=s_inner_weight, s_outer_weight=s_outer_weight, s_norm_gain=s_norm_gain, positive_column=positive_column)


HIGH = lax.Precision.HIGHEST

def apply_rms_norm(input_float, norm_gain_vector, root_mean_square):
    if root_mean_square:
        input_normalized = input_float * lax.rsqrt(lax.optimization_barrier(jnp.mean(input_float * input_float, axis=-1, keepdims=True)) + 1e-06)
    else:
        mean_removed = input_float - lax.optimization_barrier(jnp.mean(input_float, axis=-1, keepdims=True))
        input_normalized = mean_removed * lax.rsqrt(lax.optimization_barrier(jnp.mean(mean_removed * mean_removed, axis=-1, keepdims=True)) + 1e-05)
    return (input_normalized, (input_normalized * norm_gain_vector).astype(jnp.bfloat16))

def gelu_value(v):
    return 0.5 * v * (1.0 + lax.erf(v / math.sqrt(2.0)))

def gelu_slope(v):
    return 0.5 * (1.0 + lax.erf(v / math.sqrt(2.0))) + v * jnp.exp(-0.5 * v * v) / math.sqrt(2.0 * math.pi)

def pool_weights(ids):
    mask = (ids > 0).astype(jnp.float32)
    return mask / lax.optimization_barrier(jnp.sum(mask, axis=-1, keepdims=True))

def forward_block(states, ids, inner, norm_gain_vector, root_mean_square):
    count, length, width = states.shape
    input_float = states.astype(jnp.float32).reshape(count * length, width)
    input_normalized, normalized_rows = apply_rms_norm(input_float, norm_gain_vector, root_mean_square)
    pre = jnp.dot(normalized_rows, inner, preferred_element_type=jnp.float32)
    weights = pool_weights(ids)
    hidden = gelu_value(pre).reshape(count, length, -1)
    pooled = jnp.einsum('nt,ntf->nf', weights, hidden, precision=HIGH)
    resid = jnp.einsum('nt,ntd->nd', weights, input_float.reshape(count, length, width), precision=HIGH)
    return (pooled, resid)

def backward_block(states, ids, inner, norm_gain_vector, root_mean_square, hidden_grad):
    count, length, width = states.shape
    input_float = states.astype(jnp.float32).reshape(count * length, width)
    input_normalized, normalized_rows = apply_rms_norm(input_float, norm_gain_vector, root_mean_square)
    pre = jnp.dot(normalized_rows, inner, preferred_element_type=jnp.float32)
    weights = pool_weights(ids)
    slope = gelu_slope(pre).reshape(count, length, -1)
    dpre = (weights[:, :, None] * hidden_grad[:, None, :] * slope).reshape(count * length, -1).astype(jnp.bfloat16)
    inner_layer_grad = lax.dot_general(normalized_rows, dpre, (((0,), (0,)), ((), ())), preferred_element_type=jnp.float32)
    normalized_grad = lax.dot_general(dpre, inner, (((1,), (1,)), ((), ())), preferred_element_type=jnp.float32)
    return (inner_layer_grad, lax.optimization_barrier(jnp.sum(input_normalized * normalized_grad, axis=0)))

def tower_forward(states, ids, inner, outer, norm_gain_vector, root_mean_square):
    pooled, resid = lax.map(lambda pair: forward_block(pair[0], pair[1], inner, norm_gain_vector, root_mean_square), (states, ids))
    pooled = pooled.reshape(-1, pooled.shape[-1])
    embed = resid.reshape(-1, resid.shape[-1]) + jnp.dot(pooled, outer.astype(jnp.float32), precision=HIGH)
    return (pooled, embed)

def tower_backward(states, ids, inner, outer, norm_gain_vector, root_mean_square, pooled, embed_grad):
    outer_grad = lax.dot_general(pooled, embed_grad, (((0,), (0,)), ((), ())), precision=HIGH)
    hidden_grad = lax.dot_general(embed_grad, outer.astype(jnp.float32), (((1,), (1,)), ((), ())), precision=HIGH)
    hidden_grad = hidden_grad.reshape(states.shape[0], states.shape[1], -1)

    def step(carry, item):
        inner_layer_grad, gain_grad = backward_block(item[0], item[1], inner, norm_gain_vector, root_mean_square, item[2])
        return ((carry[0] + inner_layer_grad, carry[1] + gain_grad), None)
    start = (jnp.zeros(inner.shape, jnp.float32), jnp.zeros(norm_gain_vector.shape, jnp.float32))
    totals, _ = lax.scan(step, start, (states, ids, hidden_grad))
    return (totals[0], outer_grad, totals[1])

def reference(question_states, question_ids, q_inner_weight, q_outer_weight, q_norm_gain, sql_states, sql_ids, s_inner_weight, s_outer_weight, s_norm_gain, positive_column):
    scale = 1.0 / math.sqrt(D)
    q_pooled, q_embed = tower_forward(question_states, question_ids, q_inner_weight, q_outer_weight, q_norm_gain, False)
    s_pooled, s_embed = tower_forward(sql_states, sql_ids, s_inner_weight, s_outer_weight, s_norm_gain, True)
    score = scale * jnp.dot(q_embed, s_embed.T, precision=HIGH)
    count = score.shape[0]
    match = (positive_column[:, None] == jnp.arange(count, dtype=jnp.int32)[None, :]).astype(jnp.float32)
    row_max = lax.optimization_barrier(jnp.max(score, axis=1))
    row_lse = row_max + jnp.log(lax.optimization_barrier(jnp.sum(jnp.exp(score - row_max[:, None]), axis=1)))
    col_max = lax.optimization_barrier(jnp.max(score, axis=0))
    col_lse = col_max + jnp.log(lax.optimization_barrier(jnp.sum(jnp.exp(score - col_max[None, :]), axis=0)))
    row_pos = lax.optimization_barrier(jnp.sum(match * score, axis=1))
    col_pos = lax.optimization_barrier(jnp.sum(match * score, axis=0))
    loss = (jnp.sum(row_lse - row_pos) + jnp.sum(col_lse - col_pos)) / (2.0 * count)
    dscore = 0.5 * (jnp.exp(score - row_lse[:, None]) + jnp.exp(score - col_lse[None, :]) - 2.0 * match)
    q_grad = scale * jnp.dot(dscore, s_embed, precision=HIGH)
    s_grad = scale * jnp.dot(dscore.T, q_embed, precision=HIGH)
    q_inner, q_outer, q_gain = tower_backward(question_states, question_ids, q_inner_weight, q_outer_weight, q_norm_gain, False, q_pooled, q_grad)
    s_inner, s_outer, s_gain = tower_backward(sql_states, sql_ids, s_inner_weight, s_outer_weight, s_norm_gain, True, s_pooled, s_grad)
    return (loss, q_inner, q_outer, q_gain, s_inner, s_outer, s_gain)
```

```python
import math

import jax
import jax.numpy as jnp
from jax import lax
from jax.sharding import PartitionSpec as P

HIGH = lax.Precision.HIGHEST
F32 = jnp.float32
BF16 = jnp.bfloat16


def normalize(x, gain, root_mean_square):
    x = x.astype(F32)
    if root_mean_square:
        xhat = x * lax.rsqrt(jnp.mean(x * x, axis=-1, keepdims=True) + 1e-06)
    else:
        centered = x - jnp.mean(x, axis=-1, keepdims=True)
        xhat = centered * lax.rsqrt(jnp.mean(centered * centered, axis=-1, keepdims=True) + 1e-05)
    return (xhat * gain).astype(BF16)


def gelu_value(v):
    return 0.5 * v * (1.0 + lax.erf(v / math.sqrt(2.0)))


def gelu_slope(v):
    return 0.5 * (1.0 + lax.erf(v / math.sqrt(2.0))) + v * jnp.exp(-0.5 * v * v) / math.sqrt(
        2.0 * math.pi
    )


def pool_weights(ids):
    mask = (ids > 0).astype(F32)
    return mask / jnp.sum(mask, axis=-1, keepdims=True)


def swap(x, axis, step):
    size = lax.axis_size(axis)
    return lax.ppermute(x, axis, [(i, i ^ step) for i in range(size)])


def ordered(mine, other, bit, axis=0):
    return jnp.where(
        bit == 0,
        jnp.concatenate([mine, other], axis),
        jnp.concatenate([other, mine], axis),
    )


def bits_of(size):
    return [1 << i for i in range(size.bit_length() - 1)]


def bit_at(place, step):
    return jnp.where((place & step) != 0, 1, 0)


def pick_rows(table, place, count):
    return jnp.stack(
        [lax.dynamic_index_in_dim(table, place ^ k, 0, keepdims=False) for k in range(count)]
    )


def canonical(rows, place):
    count = rows.shape[0]
    for step in bits_of(count):
        shape = rows.shape
        parts = rows.reshape((count // (2 * step), 2, step) + shape[1:])
        rows = jnp.where((place & step) != 0, parts[:, ::-1], parts).reshape(shape)
    return rows


def cut(x, index, size, axis=0):
    return lax.dynamic_slice_in_dim(x, index * size, size, axis)


def per_device(
    question_states,
    question_ids,
    q_inner_weight,
    q_outer_weight,
    q_norm_gain,
    sql_states,
    sql_ids,
    s_inner_weight,
    s_outer_weight,
    s_norm_gain,
    positive_column,
):
    n_pb, n_sa = lax.axis_size("pb"), lax.axis_size("sa")
    p, a = lax.axis_index("pb"), lax.axis_index("sa")
    width = question_states.shape[-1]
    length = question_states.shape[-2]
    scale = 1.0 / math.sqrt(width)
    group = 4
    q_pool = pool_weights(question_ids[0])
    s_pool = pool_weights(sql_ids[0])
    pair_bit = bit_at(p, 1)

    own_q = question_states[0, 0]
    own_s = sql_states[0, 0]
    s_tokens = [own_s] + [swap(own_s, "pb", k) for k in range(1, group)]
    core = bit_at(a, 1)

    def fetch(weight, step):
        half = weight.shape[0] // 2
        mine = swap(cut(weight, core, half), "pb", step)
        return ordered(mine, swap(mine, "sa", 1), core)

    q_tokens = [own_q] + [None] * (n_sa - 1)
    for step in reversed(bits_of(n_sa)):
        for k in range(0, n_sa, 2 * step):
            q_tokens[k + step] = swap(q_tokens[k], "sa", step)
    far = range(group, n_pb, group)
    s_inners = [s_inner_weight] + [fetch(s_inner_weight, k) for k in far]
    s_outers = [s_outer_weight] + [fetch(s_outer_weight, k) for k in far]
    s_inner_all = jnp.concatenate(s_inners, 1)
    s_outer_all = jnp.concatenate(s_outers, 0)
    positive = lax.all_gather(positive_column, "pb", axis=0, tiled=True)

    q_pool_own = pick_rows(q_pool, a, n_sa)
    q_normed = [normalize(t, q_norm_gain, False) for t in q_tokens]
    q_rows = jnp.concatenate(q_normed, 0)
    q_pre = jnp.dot(q_rows, q_inner_weight, preferred_element_type=F32)
    q_pooled = jnp.sum(
        gelu_value(q_pre).reshape(n_sa, length, -1) * q_pool_own[:, :, None], axis=1
    )
    q_pooled = canonical(q_pooled, a)
    s_pool_own = pick_rows(s_pool, p, group)
    s_rows = jnp.concatenate([normalize(t, s_norm_gain, True) for t in s_tokens], 0)
    s_pre = jnp.dot(s_rows, s_inner_all, preferred_element_type=F32).reshape(group, length, -1)
    s_pooled = jnp.sum(gelu_value(s_pre) * s_pool_own[:, :, None], axis=1)
    s_pooled = canonical(s_pooled, p)
    q_self = jnp.sum(own_q.astype(F32) * q_pool_own[0][:, None], axis=0)
    s_self = jnp.sum(own_s.astype(F32) * s_pool_own[0][:, None], axis=0)

    q_outer_f = q_outer_weight.astype(F32)
    s_outer_f = s_outer_all.astype(F32)
    q_part = jnp.dot(q_pooled, q_outer_f, precision=HIGH)
    s_part = jnp.dot(s_pooled, s_outer_f, precision=HIGH)
    q_part = q_part + jnp.where(jnp.arange(n_sa)[:, None] == a, q_self[None], 0.0)
    s_part = s_part + jnp.where(jnp.arange(group)[:, None] == p % group, s_self[None], 0.0)

    q_pool_pair = swap(q_pool, "pb", 1)
    other_q = swap(own_q, "pb", 1)
    pair_tokens = [other_q] + [None] * (n_sa - 1)
    for step in reversed(bits_of(n_sa)):
        for k in range(0, n_sa, 2 * step):
            pair_tokens[k + step] = swap(pair_tokens[k], "sa", step)

    q_sum_steps = bits_of(n_sa)[1:]
    s_sum_steps = bits_of(group)
    for step in q_sum_steps:
        q_part = q_part + swap(q_part, "sa", step)
    for step in s_sum_steps:
        s_part = s_part + swap(s_part, "pb", step)
    for step in bits_of(n_pb):
        q_part = ordered(q_part, swap(q_part, "pb", step), bit_at(p, step))
    for step in bits_of(n_pb)[2:]:
        s_part = ordered(s_part, swap(s_part, "pb", step), bit_at(p, step))
    for step in reversed(bits_of(n_sa)):
        pass
    q_embed = q_part + swap(q_part, "sa", 1)
    s_embed = s_part
    for step in bits_of(n_sa):
        s_embed = ordered(s_embed, swap(s_embed, "sa", step), bit_at(a, step))

    q_pooled_all = lax.all_gather(q_pooled, "pb", axis=0, tiled=True)
    block = s_inner_weight.shape[1]
    s_pooled_own = [s_pooled[:, :block]] + [
        swap(s_pooled[:, (i + 1) * block : (i + 2) * block], "pb", k) for i, k in enumerate(far)
    ]
    s_pooled_own = canonical(jnp.stack(s_pooled_own), p // group).reshape(n_pb, block)
    s_pooled_all = lax.all_gather(s_pooled_own, "sa", axis=0, tiled=True)

    half = q_inner_weight.shape[1] // 2
    q_inner_half = cut(q_inner_weight, pair_bit, half, 1)
    q_outer_half = cut(q_outer_f, pair_bit, half, 0)
    q_all_rows = jnp.concatenate(
        [q_rows] + [normalize(t, q_norm_gain, False) for t in pair_tokens], 0
    )
    q_pool_all = jnp.concatenate([q_pool_own, pick_rows(q_pool_pair, a, n_sa)], 0)
    q_slope = gelu_slope(jnp.dot(q_all_rows, q_inner_half, preferred_element_type=F32))
    q_slope = q_slope.reshape(2 * n_sa, length, half) * q_pool_all[:, :, None]
    s_slope = gelu_slope(s_pre) * s_pool_own[:, :, None]

    score = scale * lax.dot_general(q_embed, s_embed, (((1,), (1,)), ((), ())), precision=HIGH)
    count = score.shape[0]
    match = (positive[:, None] == jnp.arange(count, dtype=jnp.int32)[None, :]).astype(F32)
    row_max = jnp.max(score, axis=1, keepdims=True)
    col_max = jnp.max(score, axis=0, keepdims=True)
    row_lse = row_max + jnp.log(jnp.sum(jnp.exp(score - row_max), axis=1, keepdims=True))
    col_lse = col_max + jnp.log(jnp.sum(jnp.exp(score - col_max), axis=0, keepdims=True))
    matched = jnp.sum(match * score)
    loss = (jnp.sum(row_lse) + jnp.sum(col_lse) - 2.0 * matched) / (2.0 * count)
    dscore = 0.5 * (jnp.exp(score - row_lse) + jnp.exp(score - col_lse) - 2.0 * match)
    q_grad = scale * jnp.dot(dscore, s_embed, precision=HIGH)
    s_grad = scale * lax.dot_general(dscore, q_embed, (((0,), (0,)), ((), ())), precision=HIGH)

    def hidden(grad, outer):
        return lax.dot_general(grad, outer, (((1,), (1,)), ((), ())), precision=HIGH)

    q_hidden = hidden(
        jnp.concatenate(
            [
                pick_rows(cut(q_grad, p, n_sa), a, n_sa),
                pick_rows(cut(q_grad, p ^ 1, n_sa), a, n_sa),
            ],
            0,
        ),
        q_outer_half,
    )
    s_hidden = hidden(pick_rows(cut(s_grad, a, n_pb), p, group), s_outer_f)
    q_dpre = (q_slope * q_hidden[:, None, :]).astype(BF16).reshape(-1, half)
    s_dpre = (s_slope * s_hidden[:, None, :]).astype(BF16).reshape(group * length, -1)
    contract = (((0,), (0,)), ((), ()))
    q_inner_part = lax.dot_general(q_all_rows, q_dpre, contract, preferred_element_type=F32)
    s_inner_part = lax.dot_general(s_rows, s_dpre, contract, preferred_element_type=F32)

    gains = jnp.stack(
        [
            jnp.sum(q_inner_part * q_inner_half.astype(F32), axis=1) / q_norm_gain,
            jnp.sum(s_inner_part * s_inner_all.astype(F32), axis=1) / s_norm_gain,
        ]
    )
    for step in bits_of(n_sa):
        gains = gains + swap(gains, "sa", step)
    for step in bits_of(n_pb):
        gains = gains + swap(gains, "pb", step)

    pairs = n_pb // 2
    q_chunk = width // pairs
    mine = p // 2
    q_total = cut(q_inner_part, mine, q_chunk)
    q_half_part = q_inner_part.astype(BF16)
    for k in range(1, pairs):
        q_total = q_total + swap(cut(q_half_part, mine ^ k, q_chunk), "pb", 2 * k).astype(F32)
    q_total = q_total.astype(BF16)
    chunks = [q_total] + [swap(q_total, "pb", 2 * k) for k in range(1, pairs)]
    others = [swap(c, "pb", 1) for c in chunks]
    q_inner_grad = jnp.zeros((width, 2 * half), F32)
    for k in range(pairs):
        rows = ordered(chunks[k], others[k], pair_bit, 1).astype(F32)
        q_inner_grad = lax.dynamic_update_slice_in_dim(q_inner_grad, rows, (mine ^ k) * q_chunk, 0)

    s_total = s_inner_part
    for step in bits_of(n_sa):
        size = s_total.shape[0] // 2
        bit = bit_at(a, step)
        keep = cut(s_total, bit, size)
        s_total = keep + swap(cut(s_total, 1 - bit, size).astype(BF16), "sa", step).astype(F32)
    s_sum = s_total[:, :block]
    for i, k in enumerate(far):
        piece = s_total[:, (i + 1) * block : (i + 2) * block].astype(BF16)
        s_sum = s_sum + swap(piece, "pb", k).astype(F32)
    s_sum = s_sum.astype(BF16)
    for step in reversed(bits_of(n_sa)):
        s_sum = ordered(s_sum, swap(s_sum, "sa", step), bit_at(a, step))
    s_inner_grad = s_sum.astype(F32)

    q_outer_grad = lax.dot_general(q_pooled_all, q_grad, contract, precision=HIGH)
    s_outer_grad = lax.dot_general(s_pooled_all, s_grad, contract, precision=HIGH)
    return (loss, q_inner_grad, q_outer_grad, gains[0], s_inner_grad, s_outer_grad, gains[1])


def solution(mesh):
    placed = (
        P("pb", "sa", None, None),
        P("pb", None, None),
        P(None, "sa"),
        P("sa", None),
        P(),
        P("sa", "pb", None, None),
        P("sa", None, None),
        P(None, "pb"),
        P("pb", None),
        P(),
        P("pb"),
    )
    return jax.shard_map(
        per_device,
        mesh=mesh,
        in_specs=placed,
        out_specs=(P(), P(None, "sa"), P("sa", None), P(), P(None, "pb"), P("pb", None), P()),
        check_vma=False,
    )
```

```python
import functools
import math

import jax
import jax.numpy as jnp
from jax import lax
from jax.experimental import pallas as pl
from jax.experimental.pallas import tpu as pltpu
from jax.sharding import PartitionSpec as P

HIGH = lax.Precision.HIGHEST
F32 = jnp.float32
BF16 = jnp.bfloat16
CONTRACT_FIRST = (((0,), (0,)), ((), ()))
CONTRACT_LAST = (((1,), (1,)), ((), ()))
GROUP = 4
VMEM_LIMIT = 48 * 1024 * 1024


def gelu_value(v):
    return 0.5 * v * (1.0 + lax.erf(v / math.sqrt(2.0)))


def gelu_slope(v):
    return 0.5 * (1.0 + lax.erf(v / math.sqrt(2.0))) + v * jnp.exp(-0.5 * v * v) / math.sqrt(
        2.0 * math.pi
    )


def swap(x, axis, step):
    size = lax.axis_size(axis)
    return lax.ppermute(x, axis, [(i, i ^ step) for i in range(size)])


def ordered(mine, other, bit, axis=0):
    return jnp.where(
        bit == 0,
        jnp.concatenate([mine, other], axis),
        jnp.concatenate([other, mine], axis),
    )


def bits_of(size):
    return [1 << i for i in range(size.bit_length() - 1)]


def bit_at(place, step):
    return jnp.where((place & step) != 0, 1, 0)


def canonical(rows, place):
    count = rows.shape[0]
    for step in bits_of(count):
        shape = rows.shape
        parts = rows.reshape((count // (2 * step), 2, step) + shape[1:])
        rows = jnp.where((place & step) != 0, parts[:, ::-1], parts).reshape(shape)
    return rows


def cut(x, index, size, axis=0):
    return lax.dynamic_slice_in_dim(x, index * size, size, axis)


def rounded(x):
    return lax.reduce_precision(x, 8, 7)


def split_rows(x):
    high = rounded(x)
    rest = x - high
    middle = rounded(rest)
    return jnp.concatenate([high, middle, rest - middle], 0).astype(BF16)


def exact_dot(x, weight, dims=(((1,), (0,)), ((), ()))):
    rows = x.shape[0]
    out = lax.dot_general(split_rows(x), weight, dims, preferred_element_type=F32)
    return out[:rows] + (out[rows : 2 * rows] + out[2 * rows :])


def two_parts(x):
    high = rounded(x)
    return jnp.concatenate([high, x - high], 0).astype(BF16)


def norm_kernel(q_ref, s_ref, q_gain, s_gain, q_out, s_out):
    x = s_ref[...].astype(F32)
    xhat = x * lax.rsqrt(jnp.mean(x * x, axis=-1, keepdims=True) + 1e-06)
    s_out[...] = (xhat * s_gain[...]).astype(BF16)
    x = q_ref[...].astype(F32)
    x = x - jnp.mean(x, axis=-1, keepdims=True)
    xhat = x * lax.rsqrt(jnp.mean(x * x, axis=-1, keepdims=True) + 1e-05)
    q_out[...] = (xhat * q_gain[...]).astype(BF16)


def normalize(own_q, own_s, q_gain, s_gain):
    return pl.pallas_call(
        norm_kernel,
        out_shape=(
            jax.ShapeDtypeStruct(own_q.shape, BF16),
            jax.ShapeDtypeStruct(own_s.shape, BF16),
        ),
        compiler_params=pltpu.CompilerParams(vmem_limit_bytes=VMEM_LIMIT),
    )(own_q, own_s, q_gain[None], s_gain[None])


def score_kernel(
    n_sa,
    n_pb,
    place,
    q_ref,
    s_ref,
    positive_ref,
    q_outer,
    s_outer,
    loss_ref,
    q_grad_ref,
    s_grad_ref,
    q_hidden,
    s_hidden,
):
    p, a = place[0], place[1]
    q, s = q_ref[...], s_ref[...]
    count, width = q.shape
    scale = 1.0 / math.sqrt(width)
    score = scale * lax.dot_general(q, s, CONTRACT_LAST, precision=HIGH, preferred_element_type=F32)
    columns = lax.broadcasted_iota(jnp.int32, (count, count), 1)
    match = (positive_ref[...] == columns).astype(F32)
    row_max = jnp.max(score, axis=1, keepdims=True)
    col_max = jnp.max(score, axis=0, keepdims=True)
    row_lse = row_max + jnp.log(jnp.sum(jnp.exp(score - row_max), axis=1, keepdims=True))
    col_lse = col_max + jnp.log(jnp.sum(jnp.exp(score - col_max), axis=0, keepdims=True))
    matched = jnp.sum(match * score, axis=1, keepdims=True)
    row_part = jnp.sum(row_lse - matched, axis=0, keepdims=True)
    col_part = jnp.sum(col_lse, axis=1, keepdims=True) - jnp.sum(matched, axis=0, keepdims=True)
    loss_ref[...] = (row_part + col_part) / (2.0 * count)
    dscore = 0.5 * (jnp.exp(score - row_lse) + jnp.exp(score - col_lse) - 2.0 * match)
    q_grad = scale * jnp.dot(dscore, s, precision=HIGH, preferred_element_type=F32)
    s_grad = scale * lax.dot_general(
        dscore, q, CONTRACT_FIRST, precision=HIGH, preferred_element_type=F32
    )
    q_grad_ref[...] = q_grad
    s_grad_ref[...] = s_grad

    def hidden(grad, places, outer):
        rows = places.shape[0]
        chosen = lax.broadcasted_iota(jnp.int32, (rows, count), 1) == places
        picked = jnp.dot(chosen.astype(F32), grad, precision=HIGH, preferred_element_type=F32)
        high = picked.astype(BF16)
        low = (picked - high.astype(F32)).astype(BF16)
        return lax.dot_general(
            high, outer, CONTRACT_LAST, preferred_element_type=F32
        ) + lax.dot_general(low, outer, CONTRACT_LAST, preferred_element_type=F32)

    index = lax.broadcasted_iota(jnp.int32, (2 * n_sa, 1), 0)
    pair = (index >= n_sa).astype(jnp.int32)
    q_hidden[...] = hidden(
        q_grad, (p ^ pair) * n_sa + (a ^ (index - pair * n_sa)), q_outer[...]
    )
    index = lax.broadcasted_iota(jnp.int32, (8, 1), 0)
    s_hidden[...] = hidden(s_grad, a * n_pb + (p ^ index), s_outer[...])


def scores(place, q_embed, s_embed, positive, q_outer, s_outer, n_sa, n_pb):
    shape = q_embed.shape
    whole = pl.BlockSpec(memory_space=pltpu.VMEM)
    return pl.pallas_call(
        functools.partial(score_kernel, n_sa, n_pb),
        in_specs=[pl.BlockSpec(memory_space=pltpu.SMEM)] + [whole] * 5,
        out_shape=(
            jax.ShapeDtypeStruct((1, 1), F32),
            jax.ShapeDtypeStruct(shape, F32),
            jax.ShapeDtypeStruct(shape, F32),
            jax.ShapeDtypeStruct((2 * n_sa, q_outer.shape[0]), F32),
            jax.ShapeDtypeStruct((8, s_outer.shape[0]), F32),
        ),
        compiler_params=pltpu.CompilerParams(vmem_limit_bytes=VMEM_LIMIT),
    )(place, q_embed, s_embed, positive, q_outer, s_outer)


def per_device(
    question_states,
    question_ids,
    q_inner_weight,
    q_outer_weight,
    q_norm_gain,
    sql_states,
    sql_ids,
    s_inner_weight,
    s_outer_weight,
    s_norm_gain,
    positive_column,
):
    n_pb, n_sa = lax.axis_size("pb"), lax.axis_size("sa")
    p, a = lax.axis_index("pb"), lax.axis_index("sa")
    width = question_states.shape[-1]
    length = question_states.shape[-2]
    block = s_inner_weight.shape[1]
    half = q_inner_weight.shape[1] // 2
    pair_bit = bit_at(p, 1)
    far = range(GROUP, n_pb, GROUP)

    piece_index = sum(bit_at(a, n_sa >> (i + 1)) << i for i in range(n_sa.bit_length() - 1))
    fold = width // block
    thin = width // n_sa // fold
    inner_piece = cut(s_inner_weight, piece_index, width // n_sa)
    inner_piece = jnp.concatenate([inner_piece[i * thin : (i + 1) * thin] for i in range(fold)], 1)
    piece = jnp.concatenate([inner_piece, cut(s_outer_weight, piece_index, block // n_sa)], 0)
    pieces = [swap(piece, "pb", k)[None] for k in far]

    own_q, own_s = question_states[0, 0], sql_states[0, 0]
    q_normed, s_normed = normalize(own_q, own_s, q_norm_gain, s_norm_gain)
    s_tokens = [s_normed] + [swap(s_normed, "pb", k) for k in range(1, GROUP)]
    q_tokens = [q_normed] + [None] * (n_sa - 1)
    for step in reversed(bits_of(n_sa)):
        for k in range(0, n_sa, 2 * step):
            q_tokens[k + step] = swap(q_tokens[k], "sa", step)
    for step in reversed(bits_of(n_sa)):
        pieces = [ordered(x, swap(x, "sa", step), bit_at(a, step)) for x in pieces]
    s_inners, s_outers = [s_inner_weight], [s_outer_weight]
    for x in pieces:
        inner = x[:, :thin].reshape(n_sa, thin, fold, block).transpose(0, 2, 1, 3)
        s_inners.append(inner.reshape(width, block))
        s_outers.append(x[:, thin:].reshape(block, width))
    s_inner_all = jnp.concatenate(s_inners, 1)
    s_outer_all = jnp.concatenate(s_outers, 0)

    q_lengths = jnp.sum((question_ids[0] > 0).astype(F32), axis=-1, keepdims=True)
    s_lengths = jnp.sum((sql_ids[0] > 0).astype(F32), axis=-1, keepdims=True)
    position = jnp.arange(length, dtype=jnp.int32).astype(F32)[None, :]

    def pool(lengths):
        return (position < lengths).astype(F32) / lengths

    q_pool = pool(canonical(q_lengths, a))
    s_pool = pool(canonical(s_lengths, p)[:GROUP])

    q_rows = jnp.concatenate(q_tokens, 0)
    q_pre = jnp.dot(q_rows, q_inner_weight, preferred_element_type=F32)
    q_pooled = jnp.sum(gelu_value(q_pre).reshape(n_sa, length, -1) * q_pool[:, :, None], axis=1)
    q_pooled = canonical(q_pooled, a)
    q_self = jnp.sum(own_q.astype(F32) * q_pool[0][:, None], axis=0)
    q_part = exact_dot(q_pooled, q_outer_weight)
    q_part = q_part + jnp.where(jnp.arange(n_sa)[:, None] == a, q_self[None], 0.0)
    for step in reversed(bits_of(n_sa)):
        q_part = q_part + swap(q_part, "sa", step)
    meta = jnp.concatenate(
        [positive_column.astype(F32)[:, None], q_lengths, jnp.zeros((n_sa, 126), F32)], 1
    )
    q_all = jnp.concatenate([q_part, q_pooled, meta], 1)
    pair_meta = None
    for step in bits_of(n_pb):
        other = swap(q_all, "pb", step)
        if step == 1:
            pair_meta = other
        q_all = ordered(q_all, other, bit_at(p, step))
    q_embed = q_all[:, :width]
    q_pooled_all = q_all[:, width : width + 2 * half]
    positive = q_all[:, width + 2 * half : width + 2 * half + 1].astype(jnp.int32)
    pair_lengths = pair_meta[:, width + 2 * half + 1 : width + 2 * half + 2]

    s_rows = jnp.concatenate(s_tokens, 0)
    s_pre = jnp.dot(s_rows, s_inner_all, preferred_element_type=F32).reshape(GROUP, length, -1)
    s_pooled = canonical(jnp.sum(gelu_value(s_pre) * s_pool[:, :, None], axis=1), p)
    s_self = jnp.sum(own_s.astype(F32) * s_pool[0][:, None], axis=0)
    s_part = exact_dot(s_pooled, s_outer_all)
    s_part = s_part + jnp.where(jnp.arange(GROUP)[:, None] == p % GROUP, s_self[None], 0.0)
    s_others = [swap(s_part, "pb", k) for k in range(1, GROUP)]
    s_part = (s_part + s_others[0]) + (s_others[1] + s_others[2])
    rows = [jnp.concatenate([s_part, s_pooled[:, :block]], 1)]
    for i, k in enumerate(far):
        pooled_far = s_pooled[:, (i + 1) * block : (i + 2) * block]
        rows.append(swap(jnp.concatenate([s_part, pooled_far], 1), "pb", k))
    s_all = canonical(jnp.stack(rows), p // GROUP).reshape(n_pb, width + block)
    s_all = s_all[None]
    for step in bits_of(n_sa):
        s_all = ordered(s_all, swap(s_all, "sa", step), bit_at(a, step))
    s_all = s_all.reshape(n_sa * n_pb, width + block)
    s_embed = s_all[:, :width]
    s_pooled_all = s_all[:, width:]

    pair_tokens = [swap(q_normed, "pb", 1)] + [None] * (n_sa - 1)
    for step in reversed(bits_of(n_sa)):
        for k in range(0, n_sa, 2 * step):
            pair_tokens[k + step] = swap(pair_tokens[k], "sa", step)
    q_inner_half = cut(q_inner_weight, pair_bit, half, 1)
    q_outer_half = cut(q_outer_weight, pair_bit, half, 0)
    q_both = jnp.concatenate([q_rows] + pair_tokens, 0)
    q_pool_both = jnp.concatenate([q_pool, pool(canonical(pair_lengths, a))], 0)

    place = jnp.stack([p, a]).astype(jnp.int32)
    loss, q_grad, s_grad, q_hidden, s_hidden = scores(
        place, q_embed, s_embed, positive, q_outer_half, s_outer_all, n_sa, n_pb
    )
    s_hidden = s_hidden[:GROUP]

    q_slope = gelu_slope(jnp.dot(q_both, q_inner_half, preferred_element_type=F32))
    q_slope = q_slope.reshape(2 * n_sa, length, half) * q_pool_both[:, :, None]
    s_slope = gelu_slope(s_pre) * s_pool[:, :, None]
    q_dpre = (q_slope * q_hidden[:, None, :]).astype(BF16).reshape(-1, half)
    s_dpre = (s_slope * s_hidden[:, None, :]).astype(BF16).reshape(GROUP * length, -1)
    q_inner_part = lax.dot_general(q_both, q_dpre, CONTRACT_FIRST, preferred_element_type=F32)
    s_inner_part = lax.dot_general(s_rows, s_dpre, CONTRACT_FIRST, preferred_element_type=F32)

    gains = jnp.stack(
        [
            jnp.sum(q_inner_part * q_inner_half.astype(F32), axis=1) / q_norm_gain,
            jnp.sum(s_inner_part * s_inner_all.astype(F32), axis=1) / s_norm_gain,
        ]
    )

    def pack(gains, columns):
        parts = two_parts(gains).reshape(-1, columns)
        return jnp.concatenate([parts, jnp.zeros((-parts.shape[0] % 16, columns), BF16)], 0)

    def unpack(rows):
        parts = rows[: 4 * width // rows.shape[1]].reshape(4, width).astype(F32)
        return parts[:2] + parts[2:]

    pairs = n_pb // 2
    q_chunk = width // pairs
    mine = p // 2
    q_half_part = q_inner_part.astype(BF16)
    packed = pack(gains, half)
    q_sent = []
    for k in range(1, pairs):
        chunk = cut(q_half_part, mine ^ k, q_chunk)
        q_sent.append(swap(jnp.concatenate([chunk, packed], 0), "pb", 2 * k))
    q_total = cut(q_inner_part, mine, q_chunk)
    sums = [unpack(packed)]
    for arrived in q_sent:
        q_total = q_total + arrived[:q_chunk].astype(F32)
        sums.append(unpack(arrived[q_chunk:]))
    while len(sums) > 1:
        sums = [sums[i] + sums[i + 1] for i in range(0, len(sums), 2)]
    gains = sums[0]
    q_total = q_total.astype(BF16)
    chunks = [q_total] + [swap(q_total, "pb", 2 * k) for k in range(1, pairs)]
    packed = pack(gains, half)
    first = swap(jnp.concatenate([q_total, packed], 0), "pb", 1)
    gains = unpack(packed) + unpack(first[q_chunk:])
    others = [first[:q_chunk]] + [swap(c, "pb", 1) for c in chunks[1:]]
    q_inner_grad = jnp.zeros((width, 2 * half), F32)
    for k in range(pairs):
        full = ordered(chunks[k], others[k], pair_bit, 1).astype(F32)
        q_inner_grad = lax.dynamic_update_slice_in_dim(q_inner_grad, full, (mine ^ k) * q_chunk, 0)

    s_total = s_inner_part
    for step in bits_of(n_sa):
        size = s_total.shape[0] // 2
        bit = bit_at(a, step)
        keep = cut(s_total, bit, size)
        s_total = keep + swap(cut(s_total, 1 - bit, size).astype(BF16), "sa", step).astype(F32)
    s_sum = s_total[:, :block]
    for i, k in enumerate(far):
        far_part = s_total[:, (i + 1) * block : (i + 2) * block].astype(BF16)
        s_sum = s_sum + swap(far_part, "pb", k).astype(F32)
    s_sum = s_sum.astype(BF16)
    for step in reversed(bits_of(n_sa)):
        size = s_sum.shape[0]
        packed = pack(gains, block)
        arrived = swap(jnp.concatenate([s_sum, packed], 0), "sa", step)
        gains = unpack(packed) + unpack(arrived[size:])
        s_sum = ordered(s_sum, arrived[:size], bit_at(a, step))
    s_inner_grad = s_sum.astype(F32)

    q_outer_grad = lax.dot_general(q_pooled_all, q_grad, CONTRACT_FIRST, precision=HIGH)
    s_outer_grad = lax.dot_general(s_pooled_all, s_grad, CONTRACT_FIRST, precision=HIGH)
    return (
        loss[0, 0],
        q_inner_grad,
        q_outer_grad,
        gains[0],
        s_inner_grad,
        s_outer_grad,
        gains[1],
    )


def solution(mesh):
    placed = (
        P("pb", "sa", None, None),
        P("pb", None, None),
        P(None, "sa"),
        P("sa", None),
        P(),
        P("sa", "pb", None, None),
        P("sa", None, None),
        P(None, "pb"),
        P("pb", None),
        P(),
        P("pb"),
    )
    return jax.shard_map(
        per_device,
        mesh=mesh,
        in_specs=placed,
        out_specs=(P(), P(None, "sa"), P("sa", None), P(), P(None, "pb"), P("pb", None), P()),
        check_vma=False,
    )
```

```python
import functools
import math

import jax
import jax.numpy as jnp
from jax import lax
from jax.experimental import pallas as pl
from jax.experimental.pallas import tpu as pltpu
from jax.sharding import PartitionSpec as P

HIGH = lax.Precision.HIGHEST
F32 = jnp.float32
BF16 = jnp.bfloat16
CONTRACT_FIRST = (((0,), (0,)), ((), ()))
CONTRACT_LAST = (((1,), (1,)), ((), ()))
GROUP = 4
PARTS = 4
GAIN_ROWS = 16
ROOT_HALF = 1.0 / math.sqrt(2.0)
VMEM = pl.BlockSpec(memory_space=pltpu.VMEM)
SMEM = pl.BlockSpec(memory_space=pltpu.SMEM)
HBM = pl.BlockSpec(memory_space=pltpu.HBM)
LOAD = "load"


def call(body, in_specs, out_shape, scratch=(), limit=16, flops=0, bytes_accessed=0):
    loads = [i for i, spec in enumerate(in_specs) if spec is LOAD]
    n_in, n_own = len(in_specs), len(out_shape) + len(scratch)

    def kernel(*refs):
        ins, rest = list(refs[:n_in]), refs[n_in:]
        copies = []
        for j, i in enumerate(loads):
            buffer = rest[n_own + j]
            copies.append(pltpu.make_async_copy(ins[i], buffer, rest[-1].at[j]))
            ins[i] = buffer
        for copy in copies:
            copy.start()
        for copy in copies:
            copy.wait()
        body(*ins, *rest[:n_own])

    def run(*args):
        buffers = [pltpu.VMEM(args[i].shape, args[i].dtype) for i in loads]
        if loads:
            buffers.append(pltpu.SemaphoreType.DMA((len(loads),)))
        return pl.pallas_call(
            kernel,
            in_specs=[HBM if spec is LOAD else spec for spec in in_specs],
            out_shape=tuple(jax.ShapeDtypeStruct(s, t) for s, t in out_shape),
            out_specs=tuple(VMEM for _ in out_shape),
            scratch_shapes=list(scratch) + buffers,
            cost_estimate=pl.CostEstimate(
                flops=flops, bytes_accessed=bytes_accessed, transcendentals=0
            ),
            compiler_params=pltpu.CompilerParams(vmem_limit_bytes=limit * 1024 * 1024),
        )(*args)

    return run


def gelu_value(v):
    return 0.5 * v * (1.0 + lax.erf(v * ROOT_HALF))


def gelu_slope(v):
    return 0.5 * (1.0 + lax.erf(v * ROOT_HALF)) + v * jnp.exp(-0.5 * v * v) * (
        1.0 / math.sqrt(2.0 * math.pi)
    )


def swap(x, axis, step):
    size = lax.axis_size(axis)
    return lax.ppermute(x, axis, [(i, i ^ step) for i in range(size)])


def ordered(mine, other, bit, axis=0):
    return jnp.where(
        bit == 0,
        jnp.concatenate([mine, other], axis),
        jnp.concatenate([other, mine], axis),
    )


def bits_of(size):
    return [1 << i for i in range(size.bit_length() - 1)]


def bit_at(place, step):
    return jnp.where((place & step) != 0, 1, 0)


def canonical(rows, place):
    rows = list(rows)
    for step in bits_of(len(rows)):
        odd = (place & step) != 0
        for k in range(len(rows)):
            if not k & step:
                first, second = rows[k], rows[k + step]
                rows[k] = jnp.where(odd, second, first)
                rows[k + step] = jnp.where(odd, first, second)
    return jnp.concatenate(rows, 0)


def together(*values):
    return lax.optimization_barrier(values)


def pack(gains, columns):
    high = lax.reduce_precision(gains, 8, 7)
    parts = jnp.concatenate([high, gains - high], 0).astype(BF16).reshape(-1, columns)
    return jnp.concatenate([parts, jnp.zeros((-parts.shape[0] % 16, columns), BF16)], 0)


def unpack(rows, width):
    parts = rows[: 4 * width // rows.shape[1]].reshape(4, width).astype(F32)
    return parts[:2] + parts[2:]


def column_tiles(size):
    tile = 256 if size % 256 == 0 else size
    return [slice(c, c + tile) for c in range(0, size, tile)]


def run_mask(rows, offset, length):
    return lax.broadcasted_iota(jnp.int32, (rows, 1), 0) + offset < length


def product(x, weight):
    return jnp.dot(x, weight, preferred_element_type=F32)


def rms_rows(x_ref, gain, out):
    x = x_ref[...].astype(F32)
    xhat = x * lax.rsqrt(jnp.mean(x * x, axis=-1, keepdims=True) + 1e-06)
    out[...] = (xhat * gain[...][None, :]).astype(BF16)


def prepare_kernel(
    fold,
    place,
    q_hbm,
    s_hbm,
    q_gain,
    s_gain,
    inner,
    outer,
    q_out,
    s_out,
    piece,
    q_ref,
    s_ref,
    sems,
):
    thin = inner.shape[0] // PARTS // fold
    block = inner.shape[1]
    rows = outer.shape[0] // PARTS
    index = place[2]
    tokens = [
        pltpu.make_async_copy(s_hbm, s_ref, sems.at[0]),
        pltpu.make_async_copy(q_hbm, q_ref, sems.at[1]),
    ]
    copies = []
    for i in range(fold):
        first = pl.multiple_of(index * (thin * fold) + i * thin, 16)
        copies.append(
            pltpu.make_async_copy(
                inner.at[pl.ds(first, thin), :],
                piece.at[pl.ds(0, thin), pl.ds(i * block, block)],
                sems.at[2 + i],
            )
        )
    copies.append(
        pltpu.make_async_copy(
            outer.at[pl.ds(pl.multiple_of(index * rows, 16), rows), :],
            piece.at[pl.ds(thin, rows), :],
            sems.at[2 + fold],
        )
    )
    for copy in tokens + copies:
        copy.start()
    tokens[0].wait()
    rms_rows(s_ref, s_gain, s_out)
    tokens[1].wait()
    x = q_ref[...].astype(F32)
    x = x - jnp.mean(x, axis=-1, keepdims=True)
    xhat = x * lax.rsqrt(jnp.mean(x * x, axis=-1, keepdims=True) + 1e-05)
    q_out[...] = (xhat * q_gain[...][None, :]).astype(BF16)
    for copy in copies:
        copy.wait()


def norm_only_kernel(q_ref, s_ref, q_gain, s_gain, q_out, s_out):
    rms_rows(s_ref, s_gain, s_out)
    x = q_ref[...].astype(F32)
    x = x - jnp.mean(x, axis=-1, keepdims=True)
    xhat = x * lax.rsqrt(jnp.mean(x * x, axis=-1, keepdims=True) + 1e-05)
    q_out[...] = (xhat * q_gain[...][None, :]).astype(BF16)


def prepare(place, own_q, own_s, q_gain, s_gain, inner, outer):
    width, block = inner.shape
    fold = width // block
    thin = width // PARTS // fold
    rows = block // PARTS
    if block % 128 == 0:
        return call(
            functools.partial(prepare_kernel, fold),
            [SMEM] + [HBM] * 2 + [LOAD] * 2 + [HBM] * 2,
            [(own_q.shape, BF16), (own_s.shape, BF16), ((thin + rows, width), BF16)],
            [
                pltpu.VMEM(own_q.shape, BF16),
                pltpu.VMEM(own_s.shape, BF16),
                pltpu.SemaphoreType.DMA((fold + 3,)),
            ],
        )(place, own_q, own_s, q_gain, s_gain, inner, outer)
    piece = lax.dynamic_slice_in_dim(inner, place[2] * (thin * fold), thin * fold, 0)
    piece = jnp.concatenate([piece[i * thin : (i + 1) * thin] for i in range(fold)], 1)
    other = lax.dynamic_slice_in_dim(outer, place[2] * rows, rows, 0)
    normed = call(norm_only_kernel, [VMEM] * 4, [(own_q.shape, BF16), (own_s.shape, BF16)])(
        own_q, own_s, q_gain, s_gain
    )
    return *normed, jnp.concatenate([piece, other], 0)


def gather_rows(token_refs, rows, sems):
    copies = []
    first = 0
    for i, token in enumerate(token_refs):
        count = token.shape[0]
        copies.append(pltpu.make_async_copy(token, rows.at[pl.ds(first, count), :], sems.at[i]))
        first += count
    for copy in copies:
        copy.start()
    for copy in copies:
        copy.wait()


def forward_kernel(n, far, axis, *refs):
    place, lengths, own = refs[:3]
    token_refs, refs = refs[3 : 3 + n], refs[3 + n :]
    inners, outers = [refs[0]], [refs[1]]
    pieces = refs[2 : 2 + PARTS * far]
    refs = refs[2 + PARTS * far :]
    pooled, part, rows = refs[:3]
    gather_rows(token_refs, rows, refs[-1])
    me = place[axis]
    y, core = place[3], place[4]
    places = (
        core * 2 + y,
        core * 2 + (1 - y),
        (1 - core) * 2 + y,
        (1 - core) * 2 + (1 - y),
    )
    for f in range(far):
        inner, outer = refs[3 + 2 * f : 5 + 2 * f]
        block = inner.shape[1]
        fold = inner.shape[0] // block
        thin = inner.shape[0] // PARTS // fold
        deep = block // PARTS
        for j in range(PARTS):
            piece = pieces[PARTS * f + j]
            for i in range(fold):
                first = pl.multiple_of(places[j] * (thin * fold) + i * thin, 16)
                inner[pl.ds(first, thin), :] = piece[:thin, i * block : (i + 1) * block]
            first = pl.multiple_of(places[j] * deep, 16)
            outer[pl.ds(first, deep), :] = piece[thin:, :]
        inners.append(inner)
        outers.append(outer)
    total = part.shape[0]
    span = own.shape[0]
    index = lax.broadcasted_iota(jnp.int32, (total, 1), 0)
    base = 0
    for inner in inners:
        for columns in column_tiles(inner.shape[1]):
            weight = inner[:, columns]
            tile = jnp.zeros((total, weight.shape[1]), F32)
            for k in range(total):
                length = lengths[me ^ k]
                value = gelu_value(product(rows[k * span : (k + 1) * span, :], weight))
                value = jnp.where(run_mask(span, 0, length), value, 0.0)
                row = jnp.sum(value, axis=0, keepdims=True) / length.astype(F32)
                tile = jnp.where(index == ((me ^ k) & (total - 1)), row, tile)
            pooled[:, base + columns.start : base + columns.stop] = tile
        base += inner.shape[1]
    x = own[...].astype(F32)
    length = lengths[me]
    x = jnp.where(run_mask(span, 0, length), x, 0.0)
    own_row = jnp.sum(x, axis=0, keepdims=True) / length.astype(F32)
    result = jnp.where(index == (me & (total - 1)), own_row, 0.0)
    base = 0
    for outer in outers:
        units = pooled[:, base : base + outer.shape[0]]
        high = units.astype(BF16)
        rest = units - high.astype(F32)
        middle = rest.astype(BF16)
        low = (rest - middle.astype(F32)).astype(BF16)
        weight = outer[...]
        result = result + (
            product(high, weight) + (product(middle, weight) + product(low, weight))
        )
        base += outer.shape[0]
    part[...] = result


def forward(place, lengths, own, tokens, inner, outer, pieces, axis):
    width, units = inner.shape
    far = len(pieces) // PARTS
    rows = sum(t.shape[0] for t in tokens)
    count = rows // own.shape[0]
    return call(
        functools.partial(forward_kernel, len(tokens), far, axis),
        [SMEM] * 2 + [LOAD] + [HBM] * len(tokens) + [LOAD] * (2 + len(pieces)),
        [((count, units * (1 + far)), F32), ((count, width), F32), ((rows, width), BF16)]
        + [((width, units), BF16), ((units, width), BF16)] * far,
        [pltpu.SemaphoreType.DMA((len(tokens),))],
        flops=3 * 10**9,
        bytes_accessed=3 * 10**6,
    )(place, lengths, own, *tokens, inner, outer, *pieces)


def slope_kernel(n, axis, span, gathered, place, lengths, *refs):
    token_refs = refs[:n]
    if gathered:
        weights, out, rows = refs[n:-3], refs[-3], refs[-2]
        gather_rows(token_refs, rows, refs[-1])
    else:
        weights, out, rows = refs[n:-1], refs[-1], token_refs[0]
    me = place[axis] & (lengths.shape[0] - 1)
    base = 0
    for weight in weights:
        for columns in column_tiles(weight.shape[1]):
            w = weight[:, columns]
            for k in range(out.shape[0] // span):
                length = lengths[me ^ k]
                part = slice(k * span, (k + 1) * span)
                value = gelu_slope(product(rows[part, :], w)) * (1.0 / length.astype(F32))
                value = jnp.where(run_mask(span, 0, length), value, 0.0)
                out[part, base + columns.start : base + columns.stop] = value
        base += weight.shape[1]


def slopes(place, lengths, tokens, weights, axis, span):
    gathered = len(tokens) > 1
    rows = sum(t.shape[0] for t in tokens)
    width, units = weights[0].shape[0], sum(w.shape[1] for w in weights)
    return call(
        functools.partial(slope_kernel, len(tokens), axis, span, gathered),
        [SMEM] * 2 + [HBM if gathered else VMEM] * len(tokens) + [VMEM] * len(weights),
        [((rows, units), F32)] + [((rows, width), BF16)] * gathered,
        [pltpu.SemaphoreType.DMA((len(tokens),))] * gathered,
        flops=3 * rows * units * width,
        bytes_accessed=3 * 10**6,
    )(place, lengths, *tokens, *weights)


def inner_gradient(row_refs, slope_refs, hidden, weights, gain, total, span):
    base = 0
    gains = jnp.zeros((total.shape[0], 128), F32)
    for weight in weights:
        for columns in column_tiles(weight.shape[1]):
            part = slice(base + columns.start, base + columns.stop)
            result = 0.0
            k = 0
            for rows, slope in zip(row_refs, slope_refs):
                for first in range(0, rows.shape[0], span):
                    dpre = slope[first : first + span, part] * hidden[k : k + 1, part]
                    result = result + lax.dot_general(
                        rows[first : first + span, :],
                        dpre.astype(BF16),
                        CONTRACT_FIRST,
                        preferred_element_type=F32,
                    )
                    k += 1
            total[:, part] = result
            shares = result * weight[:, columns].astype(F32)
            lanes = shares.shape[1]
            if lanes % 128:
                shares = jnp.concatenate(
                    [shares, jnp.zeros((shares.shape[0], -lanes % 128), F32)], 1
                )
            for c in range(0, shares.shape[1], 128):
                gains = gains + shares[:, c : c + 128]
        base += weight.shape[1]
    return jnp.sum(gains.T, axis=0, keepdims=True) / gain[...][None, :]


def q_backward_kernel(pairs, span, place, *refs):
    rows, pair_rows, own_slope, pair_slope, hidden, weight, gain = refs[:7]
    sends, (keep, gains, total) = refs[7 : 6 + pairs], refs[6 + pairs :]
    gains[...] = inner_gradient(
        [rows, pair_rows], [own_slope, pair_slope], hidden, [weight], gain, total, span
    )
    mine = place[0] // 2
    size = keep.shape[0]
    keep[...] = total[pl.ds(pl.multiple_of(mine * size, 16), size), :]
    for k in range(1, pairs):
        first = pl.multiple_of((mine ^ k) * size, 16)
        sends[k - 1][...] = total[pl.ds(first, size), :].astype(BF16)


def q_backward(place, rows, slope, pair_rows, pair_slope, hidden, weight, gain, pairs, span):
    width, units = weight.shape
    size = width // pairs
    return call(
        functools.partial(q_backward_kernel, pairs, span),
        [SMEM] + [VMEM] * 6 + [LOAD],
        [((size, units), BF16)] * (pairs - 1) + [((size, units), F32), ((1, width), F32)],
        [pltpu.VMEM((width, units), F32)],
        flops=4 * 10**9,
        bytes_accessed=3 * 10**6,
    )(place, rows, pair_rows, slope, pair_slope, hidden, weight, gain)


def s_backward_kernel(span, axis, place, lengths, *refs):
    rows, hidden = refs[:2]
    weights = refs[2:-7]
    gain, q_gains, send, keep, gains, total, slope = refs[-7:]
    slope_kernel(1, axis, span, False, place, lengths, rows, *weights, slope)
    s_gains = inner_gradient([rows], [slope], hidden, weights, gain, total, span)
    core = place[4]
    size = keep.shape[0]
    keep[...] = total[pl.ds(pl.multiple_of(core * size, 16), size), :]
    first = pl.multiple_of((1 - core) * size, 16)
    send[...] = total[pl.ds(first, size), :].astype(BF16)
    index = lax.broadcasted_iota(jnp.int32, (GAIN_ROWS, 1), 0)
    packed = jnp.zeros((GAIN_ROWS, total.shape[0]), F32)
    for i, row in enumerate((q_gains[...], s_gains)):
        high = row.astype(BF16).astype(F32)
        packed = jnp.where(index == i, high, packed)
        packed = jnp.where(index == i + 2, row - high, packed)
    gains[...] = packed.astype(BF16)


def s_backward(place, lengths, rows, hidden, weights, gain, q_gains, axis, span):
    width = weights[0].shape[0]
    units = sum(w.shape[1] for w in weights)
    return call(
        functools.partial(s_backward_kernel, span, axis),
        [SMEM] * 2 + [VMEM] * 2 + [LOAD] + [VMEM] * (len(weights) - 1) + [LOAD, VMEM],
        [
            ((width // 2, units), BF16),
            ((width // 2, units), F32),
            ((GAIN_ROWS, width), BF16),
        ],
        [pltpu.VMEM((width, units), F32), pltpu.VMEM((rows.shape[0], units), F32)],
        flops=6 * 10**9,
        bytes_accessed=3 * 10**6,
    )(place, lengths, rows, hidden, *weights, gain, q_gains)


def score_kernel(
    n_sa, n_pb, width, place, q_ref, s_ref, q_outer, *refs
):
    s_outers = refs[:-5]
    loss_ref, q_grad_ref, s_grad_ref, q_hidden, s_hidden = refs[-5:]
    p, a = place[0], place[1]
    q, s = q_ref[:, :width], s_ref[:, :width]
    positive = q_ref[:, q_ref.shape[1] - 128 : q_ref.shape[1] - 127].astype(jnp.int32)
    count = q.shape[0]
    scale = 1.0 / math.sqrt(width)
    score = scale * lax.dot_general(q, s, CONTRACT_LAST, precision=HIGH, preferred_element_type=F32)
    columns = lax.broadcasted_iota(jnp.int32, (count, count), 1)
    match = (positive == columns).astype(F32)
    row_max = jnp.max(score, axis=1, keepdims=True)
    col_max = jnp.max(score, axis=0, keepdims=True)
    row_lse = row_max + jnp.log(jnp.sum(jnp.exp(score - row_max), axis=1, keepdims=True))
    col_lse = col_max + jnp.log(jnp.sum(jnp.exp(score - col_max), axis=0, keepdims=True))
    matched = jnp.sum(match * score, axis=1, keepdims=True)
    row_part = jnp.sum(row_lse - matched, axis=0, keepdims=True)
    col_part = jnp.sum(col_lse, axis=1, keepdims=True) - jnp.sum(matched, axis=0, keepdims=True)
    loss_ref[...] = (row_part + col_part) / (2.0 * count)
    dscore = 0.5 * (jnp.exp(score - row_lse) + jnp.exp(score - col_lse) - 2.0 * match)
    q_grad = scale * jnp.dot(dscore, s, precision=HIGH, preferred_element_type=F32)
    s_grad = scale * lax.dot_general(
        dscore, q, CONTRACT_FIRST, precision=HIGH, preferred_element_type=F32
    )
    q_grad_ref[...] = q_grad
    s_grad_ref[...] = s_grad

    def hidden(grad, places, outers, out):
        rows = places.shape[0]
        chosen = lax.broadcasted_iota(jnp.int32, (rows, count), 1) == places
        picked = jnp.dot(chosen.astype(F32), grad, precision=HIGH, preferred_element_type=F32)
        high = picked.astype(BF16)
        low = (picked - high.astype(F32)).astype(BF16)
        base = 0
        for outer in outers:
            weight = outer[...]
            result = lax.dot_general(high, weight, CONTRACT_LAST, preferred_element_type=F32)
            result += lax.dot_general(low, weight, CONTRACT_LAST, preferred_element_type=F32)
            out[:, base : base + weight.shape[0]] = result
            base += weight.shape[0]

    index = lax.broadcasted_iota(jnp.int32, (2 * n_sa, 1), 0)
    pair = (index >= n_sa).astype(jnp.int32)
    hidden(q_grad, (p ^ pair) * n_sa + (a ^ (index - pair * n_sa)), [q_outer], q_hidden)
    index = lax.broadcasted_iota(jnp.int32, (8, 1), 0)
    hidden(s_grad, a * n_pb + (p ^ index), s_outers, s_hidden)


def scores(place, q_all, s_all, q_outer, s_outers, n_sa, n_pb, width):
    shape = (q_all.shape[0], width)
    units = sum(w.shape[0] for w in s_outers)
    return call(
        functools.partial(score_kernel, n_sa, n_pb, width),
        [SMEM] + [VMEM] * 3 + [LOAD] + [VMEM] * (len(s_outers) - 1),
        [
            ((1, 1), F32),
            (shape, F32),
            (shape, F32),
            ((2 * n_sa, q_outer.shape[0]), F32),
            ((8, units), F32),
        ],
    )(place, q_all, s_all, q_outer, *s_outers)


def assemble_kernel(pairs, place, *refs):
    out = refs[-1]
    chunks, (own_other, first, rest) = refs[:pairs], refs[pairs:-1]
    rows, half = own_other.shape
    mine = place[0] // 2
    even = place[0] % 2 == 0
    for k in range(pairs):
        a = chunks[k][:rows, :].astype(F32)
        b = own_other if k == 0 else first if k == 1 else rest.at[pl.ds((k - 2) * rows, rows), :]
        b = b[...].astype(F32)
        where = pl.ds(pl.multiple_of((mine ^ k) * rows, 8), rows)
        out[where, :half] = jnp.where(even, a, b)
        out[where, half:] = jnp.where(even, b, a)


def assemble(place, chunks, own_other, first, rest):
    rows, half = own_other.shape
    pairs = len(chunks)
    return call(
        functools.partial(assemble_kernel, pairs),
        [SMEM] + [LOAD] * (pairs + 3),
        [((rows * pairs, 2 * half), F32)],
    )(place, *chunks, own_other, first, rest)[0]


def per_device(
    question_states,
    question_ids,
    q_inner_weight,
    q_outer_weight,
    q_norm_gain,
    sql_states,
    sql_ids,
    s_inner_weight,
    s_outer_weight,
    s_norm_gain,
    positive_column,
):
    n_pb, n_sa = lax.axis_size("pb"), lax.axis_size("sa")
    p, a = lax.axis_index("pb"), lax.axis_index("sa")
    width, length = question_states.shape[-1], question_states.shape[-2]
    block = s_inner_weight.shape[1]
    units = q_inner_weight.shape[1]
    half = units // 2
    pairs = n_pb // 2
    far = range(GROUP, n_pb, GROUP)
    y, core = bit_at(a, 2), bit_at(a, 1)
    place = jnp.stack([p, a, core * 2 + y, y, core]).astype(jnp.int32)

    own_q, own_s = question_states[0, 0], sql_states[0, 0]
    q_normed, s_normed, piece = prepare(
        place, own_q, own_s, q_norm_gain, s_norm_gain, s_inner_weight, s_outer_weight
    )
    top = n_sa // 2
    mine = [swap(piece, "pb", k) for k in far]
    beside = [swap(piece, "sa", 1) for piece in mine]
    from_x, from_z = swap(s_normed, "pb", 1), swap(s_normed, "pb", 2)
    pair_token = swap(q_normed, "pb", 1)
    q_far = swap(q_normed, "sa", top)
    pair_bit = bit_at(p, 1)
    q_inner_half = lax.dynamic_slice_in_dim(q_inner_weight, pair_bit * half, half, 1)
    q_outer_half = lax.dynamic_slice_in_dim(q_outer_weight, pair_bit * half, half, 0)
    q_lengths = jnp.sum((question_ids[0] > 0).astype(jnp.int32), axis=-1)
    s_lengths = jnp.sum((sql_ids[0] > 0).astype(jnp.int32), axis=-1)
    (
        from_x,
        from_z,
        mine,
        beside,
        q_far,
        pair_token,
        s_late,
        q_inner_half,
        q_outer_half,
        q_lengths,
        s_lengths,
    ) = together(
        from_x,
        from_z,
        mine,
        beside,
        q_far,
        pair_token,
        s_normed,
        q_inner_half,
        q_outer_half,
        q_lengths,
        s_lengths,
    )

    across = [swap(piece, "sa", 2) for piece in mine]
    from_xz = swap(s_late, "pb", 3)
    q_tokens = [q_normed] + [None] * (n_sa - 1)
    q_tokens[top] = q_far
    for step in reversed(bits_of(n_sa)):
        for k in range(0, n_sa, 2 * step):
            if q_tokens[k + step] is None:
                q_tokens[k + step] = swap(q_tokens[k], "sa", step)

    q_pooled, q_part, q_rows = forward(
        place, q_lengths, own_q, q_tokens, q_inner_weight, q_outer_weight, [], 1
    )
    (own_slope,) = slopes(place, q_lengths, [q_rows], [q_inner_half], 1, length)
    q_steps = list(reversed(bits_of(n_sa)))
    for step in q_steps[:-1]:
        q_part = q_part + swap(q_part, "sa", step)
    from_xz, across, q_part, own_slope, pair_late = together(
        from_xz, across, q_part, own_slope, pair_token
    )
    pair_far = swap(pair_late, "sa", top)

    pieces = []
    for one, two, three in zip(mine, across, beside):
        pieces += [one, two, three, swap(two, "sa", 1)]
    s_tokens = [s_normed, from_x, from_z, from_xz]
    q_part = q_part + swap(q_part, "sa", q_steps[-1])
    meta = jnp.stack([positive_column, q_lengths], 1).astype(F32)
    meta = jnp.concatenate([meta, jnp.zeros((n_sa, 126), F32)], 1)
    q_all = jnp.concatenate([q_part, q_pooled, meta], 1)
    s_pooled, s_part, s_rows, *far_weights = forward(
        place, s_lengths, own_s, s_tokens, s_inner_weight, s_outer_weight, pieces, 0
    )
    s_inners = [s_inner_weight] + far_weights[0::2]
    s_outers = [s_outer_weight] + far_weights[1::2]
    s_part, q_all = together(s_part, q_all)

    s_others = [swap(s_part, "pb", k) for k in range(1, GROUP)]
    pair_meta = swap(q_all, "pb", 1)
    q_all = ordered(q_all, pair_meta, pair_bit)
    pair_lengths = pair_meta[:, width + units + 1].astype(jnp.int32)
    s_part = (s_part + s_others[0]) + (s_others[1] + s_others[2])
    s_part, q_all = together(s_part, q_all)

    s_sent = [jnp.concatenate([s_part, s_pooled[:, :block]], 1)]
    for i, k in enumerate(far):
        pooled_far = s_pooled[:, (i + 1) * block : (i + 2) * block]
        s_sent.append(swap(jnp.concatenate([s_part, pooled_far], 1), "pb", k))
    q_all = ordered(q_all, swap(q_all, "pb", 2), bit_at(p, 2))
    s_all = canonical(s_sent, p // GROUP)[None]
    s_all, q_all = together(s_all, q_all)
    pair_tokens = [pair_token] + [None] * (n_sa - 1)
    pair_tokens[top] = pair_far
    for step in reversed(bits_of(n_sa)):
        for k in range(0, n_sa, 2 * step):
            if pair_tokens[k + step] is None:
                pair_tokens[k + step] = swap(pair_tokens[k], "sa", step)
    for step in bits_of(n_pb)[2:]:
        q_all = ordered(q_all, swap(q_all, "pb", step), bit_at(p, step))
    for step in reversed(bits_of(n_sa)):
        s_all = ordered(s_all, swap(s_all, "sa", step), bit_at(a, step))
    order = [
        sum(((i >> b) & 1) << (n_sa.bit_length() - 2 - b) for b in range(n_sa.bit_length() - 1))
        for i in range(n_sa)
    ]
    s_all = jnp.concatenate([s_all[order[i]] for i in range(n_sa)], 0)
    pair_slope, pair_rows = slopes(place, pair_lengths, pair_tokens, [q_inner_half], 1, length)
    q_all, s_all, pair_slope = together(q_all, s_all, pair_slope)

    loss, q_grad, s_grad, q_hidden, s_hidden = scores(
        place, q_all, s_all, q_outer_half, s_outers, n_sa, n_pb, width
    )

    *q_sends, q_keep, q_gains = q_backward(
        place,
        q_rows,
        own_slope,
        pair_rows,
        pair_slope,
        q_hidden,
        q_inner_half,
        q_norm_gain,
        pairs,
        length,
    )
    q_arrived = [swap(x, "pb", 2 * k) for k, x in enumerate(q_sends, 1)]
    s_hidden, q_gains = together(s_hidden, q_gains)
    s_send, s_keep, packed = s_backward(
        place, s_lengths, s_rows, s_hidden, s_inners, s_norm_gain, q_gains, 0, length
    )

    def outer_gradient(pooled, grad):
        high = lax.reduce_precision(pooled, 8, 7)
        top = lax.reduce_precision(grad, 8, 7)
        left = jnp.concatenate([high, pooled - high, high], 0).astype(BF16)
        right = jnp.concatenate([top, top, grad - top], 0).astype(BF16)
        return lax.dot_general(left, right, CONTRACT_FIRST, preferred_element_type=F32)

    q_outer_grad = outer_gradient(q_all[:, width : width + units], q_grad)
    s_outer_grad = outer_gradient(s_all[:, width:], s_grad)
    q_arrived, s_send, s_keep, packed, q_outer_grad, s_outer_grad = together(
        q_arrived, s_send, s_keep, packed, q_outer_grad, s_outer_grad
    )
    s_beside = swap(s_send, "sa", 1)

    q_total = q_keep
    for x in q_arrived:
        q_total = q_total + x.astype(F32)
    q_total = q_total.astype(BF16)
    rows = q_total.shape[0]
    packed = jnp.concatenate(jnp.split(packed, width // half, 1), 0)
    sent = jnp.concatenate([q_total, packed], 0)
    arrivals = [swap(sent, "pb", 2 * k) for k in range(1, pairs)]
    own_other = swap(q_total, "pb", 1)
    size = width // 2
    s_total = s_keep + s_beside.astype(F32)
    for step in bits_of(n_sa)[1:]:
        size = size // 2
        bit = bit_at(a, step)
        away = lax.dynamic_slice_in_dim(s_total, (1 - bit) * size, size, 0).astype(BF16)
        arrived = swap(away, "sa", step)
        s_total = lax.dynamic_slice_in_dim(s_total, bit * size, size, 0)
        s_total = s_total + arrived.astype(F32)
    first = swap(arrivals[0][:rows], "pb", 1)
    arrivals, own_other, first, s_total = together(arrivals, own_other, first, s_total)

    chunks = [q_total] + list(arrivals)

    def gain_sums(tail):
        tail = jnp.concatenate(jnp.split(tail, width // half, 0), 1)
        return tail[:2].astype(F32) + tail[2:4].astype(F32)

    sums = [gain_sums(packed)] + [gain_sums(x[rows:]) for x in arrivals]
    while len(sums) > 1:
        sums = [sums[i] + sums[i + 1] for i in range(0, len(sums), 2)]
    gains = sums[0]
    packed = pack(gains, half)
    rest = swap(jnp.concatenate([x[:rows] for x in chunks[2:]] + [packed], 0), "pb", 1)
    s_sum = s_total[:, :block]
    for i, k in enumerate(far):
        far_part = s_total[:, (i + 1) * block : (i + 2) * block].astype(BF16)
        s_sum = s_sum + swap(far_part, "pb", k).astype(F32)
    rest, s_sum = together(rest, s_sum)
    gains = unpack(packed, width) + unpack(rest[(pairs - 2) * rows :], width)
    q_inner_grad = assemble(place, chunks, own_other, first, rest)

    s_sum = s_sum.astype(BF16)
    for step in reversed(bits_of(n_sa)):
        size = s_sum.shape[0]
        packed = pack(gains, block)
        if step == 1:
            s_sum, q_inner_grad = together(s_sum, q_inner_grad)
        arrived = swap(jnp.concatenate([s_sum, packed], 0), "sa", step)
        gains = unpack(packed, width) + unpack(arrived[size:], width)
        s_sum = ordered(s_sum, arrived[:size], bit_at(a, step))
    s_inner_grad = s_sum.astype(F32)

    return (
        loss[0, 0],
        q_inner_grad,
        q_outer_grad,
        gains[0],
        s_inner_grad,
        s_outer_grad,
        gains[1],
    )


def solution(mesh):
    placed = (
        P("pb", "sa", None, None),
        P("pb", None, None),
        P(None, "sa"),
        P("sa", None),
        P(),
        P("sa", "pb", None, None),
        P("sa", None, None),
        P(None, "pb"),
        P("pb", None),
        P(),
        P("pb"),
    )
    return jax.shard_map(
        per_device,
        mesh=mesh,
        in_specs=placed,
        out_specs=(P(), P(None, "sa"), P("sa", None), P(), P(None, "pb"), P("pb", None), P()),
        check_vma=False,
    )
```

```python
import functools
import math

import jax
import jax.numpy as jnp
from jax import lax
from jax.experimental import pallas as pl
from jax.experimental.pallas import tpu as pltpu
from jax.sharding import PartitionSpec as P

HIGH = lax.Precision.HIGHEST
F32 = jnp.float32
BF16 = jnp.bfloat16
CONTRACT_FIRST = (((0,), (0,)), ((), ()))
CONTRACT_LAST = (((1,), (1,)), ((), ()))
GROUP = 4
PARTS = 4
GAIN_ROWS = 16
ROOT_HALF = 1.0 / math.sqrt(2.0)
VMEM = pl.BlockSpec(memory_space=pltpu.VMEM)
SMEM = pl.BlockSpec(memory_space=pltpu.SMEM)
HBM = pl.BlockSpec(memory_space=pltpu.HBM)
LOAD = "load"


def call(body, in_specs, out_shape, scratch=(), limit=16, flops=0, bytes_accessed=0, outs=None):
    loads = [i for i, spec in enumerate(in_specs) if spec is LOAD]
    n_in, n_own = len(in_specs), len(out_shape) + len(scratch)

    def kernel(*refs):
        ins, rest = list(refs[:n_in]), refs[n_in:]
        copies = []
        for j, i in enumerate(loads):
            buffer = rest[n_own + j]
            copies.append(pltpu.make_async_copy(ins[i], buffer, rest[-1].at[j]))
            ins[i] = buffer
        for copy in copies:
            copy.start()
        for copy in copies:
            copy.wait()
        body(*ins, *rest[:n_own])

    def run(*args):
        buffers = [pltpu.VMEM(args[i].shape, args[i].dtype) for i in loads]
        if loads:
            buffers.append(pltpu.SemaphoreType.DMA((len(loads),)))
        return pl.pallas_call(
            kernel,
            in_specs=[HBM if spec is LOAD else spec for spec in in_specs],
            out_shape=tuple(jax.ShapeDtypeStruct(s, t) for s, t in out_shape),
            out_specs=tuple(outs or [VMEM] * len(out_shape)),
            scratch_shapes=list(scratch) + buffers,
            cost_estimate=pl.CostEstimate(
                flops=flops, bytes_accessed=bytes_accessed, transcendentals=0
            ),
            compiler_params=pltpu.CompilerParams(vmem_limit_bytes=limit * 1024 * 1024),
        )(*args)

    return run


def gelu_value(v):
    return 0.5 * v * (1.0 + lax.erf(v * ROOT_HALF))


def gelu_slope(v):
    return 0.5 * (1.0 + lax.erf(v * ROOT_HALF)) + v * jnp.exp(-0.5 * v * v) * (
        1.0 / math.sqrt(2.0 * math.pi)
    )


def swap(x, axis, step):
    size = lax.axis_size(axis)
    return lax.ppermute(x, axis, [(i, i ^ step) for i in range(size)])


def ordered(mine, other, bit, axis=0):
    return jnp.where(
        bit == 0,
        jnp.concatenate([mine, other], axis),
        jnp.concatenate([other, mine], axis),
    )


def bits_of(size):
    return [1 << i for i in range(size.bit_length() - 1)]


def bit_at(place, step):
    return jnp.where((place & step) != 0, 1, 0)


def canonical(rows, place):
    rows = list(rows)
    for step in bits_of(len(rows)):
        odd = (place & step) != 0
        for k in range(len(rows)):
            if not k & step:
                first, second = rows[k], rows[k + step]
                rows[k] = jnp.where(odd, second, first)
                rows[k + step] = jnp.where(odd, first, second)
    return jnp.concatenate(rows, 0)


def together(*values):
    return lax.optimization_barrier(values)


def pack(gains, columns):
    high = lax.reduce_precision(gains, 8, 7)
    parts = jnp.concatenate([high, gains - high], 0).astype(BF16).reshape(-1, columns)
    return jnp.concatenate([parts, jnp.zeros((-parts.shape[0] % 16, columns), BF16)], 0)


def unpack(rows, width):
    parts = rows[: 4 * width // rows.shape[1]].reshape(4, width).astype(F32)
    return parts[:2] + parts[2:]


def column_tiles(size):
    tile = 256 if size % 256 == 0 else size
    return [slice(c, c + tile) for c in range(0, size, tile)]


def run_mask(rows, offset, length):
    return lax.broadcasted_iota(jnp.int32, (rows, 1), 0) + offset < length


def product(x, weight):
    return jnp.dot(x, weight, preferred_element_type=F32)


def rms_rows(x_ref, gain, out):
    x = x_ref[...].astype(F32)
    xhat = x * lax.rsqrt(jnp.mean(x * x, axis=-1, keepdims=True) + 1e-06)
    out[...] = (xhat * gain[...][None, :]).astype(BF16)


def prepare_kernel(
    fold,
    place,
    q_hbm,
    s_hbm,
    q_gain,
    s_gain,
    inner,
    outer,
    q_out,
    s_out,
    piece,
    q_ref,
    s_ref,
    sems,
):
    thin = inner.shape[0] // PARTS // fold
    block = inner.shape[1]
    rows = outer.shape[0] // PARTS
    index = place[2]
    tokens = [
        pltpu.make_async_copy(s_hbm, s_ref, sems.at[0]),
        pltpu.make_async_copy(q_hbm, q_ref, sems.at[1]),
    ]
    copies = []
    for i in range(fold):
        first = pl.multiple_of(index * (thin * fold) + i * thin, 16)
        copies.append(
            pltpu.make_async_copy(
                inner.at[pl.ds(first, thin), :],
                piece.at[pl.ds(0, thin), pl.ds(i * block, block)],
                sems.at[2 + i],
            )
        )
    copies.append(
        pltpu.make_async_copy(
            outer.at[pl.ds(pl.multiple_of(index * rows, 16), rows), :],
            piece.at[pl.ds(thin, rows), :],
            sems.at[2 + fold],
        )
    )
    for copy in tokens + copies:
        copy.start()
    tokens[0].wait()
    rms_rows(s_ref, s_gain, s_out)
    tokens[1].wait()
    x = q_ref[...].astype(F32)
    x = x - jnp.mean(x, axis=-1, keepdims=True)
    xhat = x * lax.rsqrt(jnp.mean(x * x, axis=-1, keepdims=True) + 1e-05)
    q_out[...] = (xhat * q_gain[...][None, :]).astype(BF16)
    for copy in copies:
        copy.wait()


def norm_only_kernel(q_ref, s_ref, q_gain, s_gain, q_out, s_out):
    rms_rows(s_ref, s_gain, s_out)
    x = q_ref[...].astype(F32)
    x = x - jnp.mean(x, axis=-1, keepdims=True)
    xhat = x * lax.rsqrt(jnp.mean(x * x, axis=-1, keepdims=True) + 1e-05)
    q_out[...] = (xhat * q_gain[...][None, :]).astype(BF16)


def prepare(place, own_q, own_s, q_gain, s_gain, inner, outer):
    width, block = inner.shape
    fold = width // block
    thin = width // PARTS // fold
    rows = block // PARTS
    if block % 128 == 0:
        return call(
            functools.partial(prepare_kernel, fold),
            [SMEM] + [HBM] * 2 + [LOAD] * 2 + [HBM] * 2,
            [(own_q.shape, BF16), (own_s.shape, BF16), ((thin + rows, width), BF16)],
            [
                pltpu.VMEM(own_q.shape, BF16),
                pltpu.VMEM(own_s.shape, BF16),
                pltpu.SemaphoreType.DMA((fold + 3,)),
            ],
            limit=60,
        )(place, own_q, own_s, q_gain, s_gain, inner, outer)
    piece = lax.dynamic_slice_in_dim(inner, place[2] * (thin * fold), thin * fold, 0)
    piece = jnp.concatenate([piece[i * thin : (i + 1) * thin] for i in range(fold)], 1)
    other = lax.dynamic_slice_in_dim(outer, place[2] * rows, rows, 0)
    normed = call(norm_only_kernel, [VMEM] * 4, [(own_q.shape, BF16), (own_s.shape, BF16)])(
        own_q, own_s, q_gain, s_gain
    )
    return *normed, jnp.concatenate([piece, other], 0)


def gather_rows(token_refs, rows, sems):
    copies = []
    first = 0
    for i, token in enumerate(token_refs):
        count = token.shape[0]
        copies.append(pltpu.make_async_copy(token, rows.at[pl.ds(first, count), :], sems.at[i]))
        first += count
    for copy in copies:
        copy.start()
    for copy in copies:
        copy.wait()


def forward_kernel(n, far, axis, *refs):
    place, lengths, own = refs[:3]
    token_refs, refs = refs[3 : 3 + n], refs[3 + n :]
    inners, outers = [refs[0]], [refs[1]]
    pieces = refs[2 : 2 + PARTS * far]
    refs = refs[2 + PARTS * far :]
    pooled, part = refs[:2]
    results, (buffers, sems) = refs[2 : 3 + 2 * far], (refs[3 + 2 * far : -1], refs[-1])
    rows = buffers[0]
    gather_rows(token_refs, rows, sems)
    leaving = [pltpu.make_async_copy(x, y, sems.at[i]) for i, (x, y) in enumerate(zip(buffers, results))]
    leaving[0].start()
    me = place[axis]
    y, core = place[3], place[4]
    places = (
        core * 2 + y,
        core * 2 + (1 - y),
        (1 - core) * 2 + y,
        (1 - core) * 2 + (1 - y),
    )
    for f in range(far):
        inner, outer = buffers[1 + 2 * f : 3 + 2 * f]
        block = inner.shape[1]
        fold = inner.shape[0] // block
        thin = inner.shape[0] // PARTS // fold
        deep = block // PARTS
        for j in range(PARTS):
            piece = pieces[PARTS * f + j]
            for i in range(fold):
                first = pl.multiple_of(places[j] * (thin * fold) + i * thin, 16)
                inner[pl.ds(first, thin), :] = piece[:thin, i * block : (i + 1) * block]
            first = pl.multiple_of(places[j] * deep, 16)
            outer[pl.ds(first, deep), :] = piece[thin:, :]
        inners.append(inner)
        outers.append(outer)
    for copy in leaving[1:]:
        copy.start()
    total = part.shape[0]
    span = own.shape[0]
    index = lax.broadcasted_iota(jnp.int32, (total, 1), 0)
    base = 0
    for inner in inners:
        for columns in column_tiles(inner.shape[1]):
            weight = inner[:, columns]
            tile = jnp.zeros((total, weight.shape[1]), F32)
            for k in range(total):
                length = lengths[me ^ k]
                value = gelu_value(product(rows[k * span : (k + 1) * span, :], weight))
                value = jnp.where(run_mask(span, 0, length), value, 0.0)
                row = jnp.sum(value, axis=0, keepdims=True) / length.astype(F32)
                tile = jnp.where(index == ((me ^ k) & (total - 1)), row, tile)
            pooled[:, base + columns.start : base + columns.stop] = tile
        base += inner.shape[1]
    x = own[...].astype(F32)
    length = lengths[me]
    x = jnp.where(run_mask(span, 0, length), x, 0.0)
    own_row = jnp.sum(x, axis=0, keepdims=True) / length.astype(F32)
    result = jnp.where(index == (me & (total - 1)), own_row, 0.0)
    base = 0
    for outer in outers:
        units = pooled[:, base : base + outer.shape[0]]
        high = units.astype(BF16)
        rest = units - high.astype(F32)
        middle = rest.astype(BF16)
        low = (rest - middle.astype(F32)).astype(BF16)
        weight = outer[...]
        result = result + (
            product(high, weight) + (product(middle, weight) + product(low, weight))
        )
        base += outer.shape[0]
    part[...] = result
    for copy in leaving:
        copy.wait()


def forward(place, lengths, own, tokens, inner, outer, pieces, axis):
    width, units = inner.shape
    far = len(pieces) // PARTS
    rows = sum(t.shape[0] for t in tokens)
    count = rows // own.shape[0]
    large = [(rows, width)] + [(width, units), (units, width)] * far
    return call(
        functools.partial(forward_kernel, len(tokens), far, axis),
        [SMEM] * 2 + [LOAD] + [HBM] * len(tokens) + [LOAD] * (2 + len(pieces)),
        [((count, units * (1 + far)), F32), ((count, width), F32)] + [(x, BF16) for x in large],
        [pltpu.VMEM(x, BF16) for x in large]
        + [pltpu.SemaphoreType.DMA((max(len(tokens), len(large)),))],
        flops=3 * 10**9,
        bytes_accessed=3 * 10**6,
        limit=60 if far else 24,
        outs=[VMEM] * 2 + [HBM] * len(large),
    )(place, lengths, own, *tokens, inner, outer, *pieces)


def slope_kernel(n, axis, span, gathered, place, lengths, *refs):
    token_refs = refs[:n]
    if gathered:
        weights, out, rows = refs[n:-3], refs[-3], refs[-2]
        gather_rows(token_refs, rows, refs[-1])
    else:
        weights, out, rows = refs[n:-1], refs[-1], token_refs[0]
    me = place[axis] & (lengths.shape[0] - 1)
    base = 0
    for weight in weights:
        for columns in column_tiles(weight.shape[1]):
            w = weight[:, columns]
            for k in range(out.shape[0] // span):
                length = lengths[me ^ k]
                part = slice(k * span, (k + 1) * span)
                value = gelu_slope(product(rows[part, :], w)) * (1.0 / length.astype(F32))
                value = jnp.where(run_mask(span, 0, length), value, 0.0)
                out[part, base + columns.start : base + columns.stop] = value
        base += weight.shape[1]


def slopes(place, lengths, tokens, weights, axis, span):
    gathered = len(tokens) > 1
    rows = sum(t.shape[0] for t in tokens)
    width, units = weights[0].shape[0], sum(w.shape[1] for w in weights)
    return call(
        functools.partial(slope_kernel, len(tokens), axis, span, gathered),
        [SMEM] * 2 + [HBM if gathered else VMEM] * len(tokens) + [VMEM] * len(weights),
        [((rows, units), F32)] + [((rows, width), BF16)] * gathered,
        [pltpu.SemaphoreType.DMA((len(tokens),))] * gathered,
        flops=3 * rows * units * width,
        bytes_accessed=3 * 10**6,
    )(place, lengths, *tokens, *weights)


def inner_gradient(row_refs, slope_refs, hidden, weights, gain, total, span):
    base = 0
    gains = jnp.zeros((total.shape[0], 128), F32)
    for weight in weights:
        for columns in column_tiles(weight.shape[1]):
            part = slice(base + columns.start, base + columns.stop)
            result = 0.0
            k = 0
            for rows, slope in zip(row_refs, slope_refs):
                for first in range(0, rows.shape[0], span):
                    dpre = slope[first : first + span, part] * hidden[k : k + 1, part]
                    result = result + lax.dot_general(
                        rows[first : first + span, :],
                        dpre.astype(BF16),
                        CONTRACT_FIRST,
                        preferred_element_type=F32,
                    )
                    k += 1
            total[:, part] = result
            shares = result * weight[:, columns].astype(F32)
            lanes = shares.shape[1]
            if lanes % 128:
                shares = jnp.concatenate(
                    [shares, jnp.zeros((shares.shape[0], -lanes % 128), F32)], 1
                )
            for c in range(0, shares.shape[1], 128):
                gains = gains + shares[:, c : c + 128]
        base += weight.shape[1]
    return jnp.sum(gains.T, axis=0, keepdims=True) / gain[...][None, :]


def q_backward_kernel(pairs, span, place, *refs):
    rows, pair_rows, own_slope, pair_slope, hidden, weight, gain = refs[:7]
    sends, (keep, gains, total) = refs[7 : 6 + pairs], refs[6 + pairs :]
    gains[...] = inner_gradient(
        [rows, pair_rows], [own_slope, pair_slope], hidden, [weight], gain, total, span
    )
    mine = place[0] // 2
    size = keep.shape[0]
    keep[...] = total[pl.ds(pl.multiple_of(mine * size, 16), size), :]
    for k in range(1, pairs):
        first = pl.multiple_of((mine ^ k) * size, 16)
        sends[k - 1][...] = total[pl.ds(first, size), :].astype(BF16)


def q_backward(place, rows, slope, pair_rows, pair_slope, hidden, weight, gain, pairs, span):
    width, units = weight.shape
    size = width // pairs
    return call(
        functools.partial(q_backward_kernel, pairs, span),
        [SMEM] + [VMEM] * 6 + [LOAD],
        [((size, units), BF16)] * (pairs - 1) + [((size, units), F32), ((1, width), F32)],
        [pltpu.VMEM((width, units), F32)],
        flops=4 * 10**9,
        bytes_accessed=3 * 10**6,
    )(place, rows, pair_rows, slope, pair_slope, hidden, weight, gain)


def s_backward_kernel(span, axis, place, lengths, *refs):
    rows, hidden = refs[:2]
    weights = refs[2:-7]
    gain, q_gains, send, keep, gains, total, slope = refs[-7:]
    slope_kernel(1, axis, span, False, place, lengths, rows, *weights, slope)
    s_gains = inner_gradient([rows], [slope], hidden, weights, gain, total, span)
    core = place[4]
    size = keep.shape[0]
    keep[...] = total[pl.ds(pl.multiple_of(core * size, 16), size), :]
    first = pl.multiple_of((1 - core) * size, 16)
    send[...] = total[pl.ds(first, size), :].astype(BF16)
    index = lax.broadcasted_iota(jnp.int32, (GAIN_ROWS, 1), 0)
    packed = jnp.zeros((GAIN_ROWS, total.shape[0]), F32)
    for i, row in enumerate((q_gains[...], s_gains)):
        high = row.astype(BF16).astype(F32)
        packed = jnp.where(index == i, high, packed)
        packed = jnp.where(index == i + 2, row - high, packed)
    gains[...] = packed.astype(BF16)


def s_backward(place, lengths, rows, hidden, weights, gain, q_gains, axis, span):
    width = weights[0].shape[0]
    units = sum(w.shape[1] for w in weights)
    return call(
        functools.partial(s_backward_kernel, span, axis),
        [SMEM] * 2 + [VMEM] * 2 + [LOAD] + [VMEM] * (len(weights) - 1) + [LOAD, VMEM],
        [
            ((width // 2, units), BF16),
            ((width // 2, units), F32),
            ((GAIN_ROWS, width), BF16),
        ],
        [pltpu.VMEM((width, units), F32), pltpu.VMEM((rows.shape[0], units), F32)],
        flops=6 * 10**9,
        bytes_accessed=3 * 10**6,
    )(place, lengths, rows, hidden, *weights, gain, q_gains)


def score_kernel(
    n_sa, n_pb, width, place, q_ref, s_ref, q_outer, *refs
):
    s_outers = refs[:-5]
    loss_ref, q_grad_ref, s_grad_ref, q_hidden, s_hidden = refs[-5:]
    p, a = place[0], place[1]
    q, s = q_ref[:, :width], s_ref[:, :width]
    positive = q_ref[:, q_ref.shape[1] - 128 : q_ref.shape[1] - 127].astype(jnp.int32)
    count = q.shape[0]
    scale = 1.0 / math.sqrt(width)
    score = scale * lax.dot_general(q, s, CONTRACT_LAST, precision=HIGH, preferred_element_type=F32)
    columns = lax.broadcasted_iota(jnp.int32, (count, count), 1)
    match = (positive == columns).astype(F32)
    row_max = jnp.max(score, axis=1, keepdims=True)
    col_max = jnp.max(score, axis=0, keepdims=True)
    row_lse = row_max + jnp.log(jnp.sum(jnp.exp(score - row_max), axis=1, keepdims=True))
    col_lse = col_max + jnp.log(jnp.sum(jnp.exp(score - col_max), axis=0, keepdims=True))
    matched = jnp.sum(match * score, axis=1, keepdims=True)
    row_part = jnp.sum(row_lse - matched, axis=0, keepdims=True)
    col_part = jnp.sum(col_lse, axis=1, keepdims=True) - jnp.sum(matched, axis=0, keepdims=True)
    loss_ref[...] = (row_part + col_part) / (2.0 * count)
    dscore = 0.5 * (jnp.exp(score - row_lse) + jnp.exp(score - col_lse) - 2.0 * match)
    q_grad = scale * jnp.dot(dscore, s, precision=HIGH, preferred_element_type=F32)
    s_grad = scale * lax.dot_general(
        dscore, q, CONTRACT_FIRST, precision=HIGH, preferred_element_type=F32
    )
    q_grad_ref[...] = q_grad
    s_grad_ref[...] = s_grad

    def hidden(grad, places, outers, out):
        rows = places.shape[0]
        chosen = lax.broadcasted_iota(jnp.int32, (rows, count), 1) == places
        picked = jnp.dot(chosen.astype(F32), grad, precision=HIGH, preferred_element_type=F32)
        high = picked.astype(BF16)
        low = (picked - high.astype(F32)).astype(BF16)
        base = 0
        for outer in outers:
            weight = outer[...]
            result = lax.dot_general(high, weight, CONTRACT_LAST, preferred_element_type=F32)
            result += lax.dot_general(low, weight, CONTRACT_LAST, preferred_element_type=F32)
            out[:, base : base + weight.shape[0]] = result
            base += weight.shape[0]

    index = lax.broadcasted_iota(jnp.int32, (2 * n_sa, 1), 0)
    pair = (index >= n_sa).astype(jnp.int32)
    hidden(q_grad, (p ^ pair) * n_sa + (a ^ (index - pair * n_sa)), [q_outer], q_hidden)
    index = lax.broadcasted_iota(jnp.int32, (8, 1), 0)
    hidden(s_grad, a * n_pb + (p ^ index), s_outers, s_hidden)


def scores(place, q_all, s_all, q_outer, s_outers, n_sa, n_pb, width):
    shape = (q_all.shape[0], width)
    units = sum(w.shape[0] for w in s_outers)
    return call(
        functools.partial(score_kernel, n_sa, n_pb, width),
        [SMEM] + [VMEM] * 3 + [LOAD] + [VMEM] * (len(s_outers) - 1),
        [
            ((1, 1), F32),
            (shape, F32),
            (shape, F32),
            ((2 * n_sa, q_outer.shape[0]), F32),
            ((8, units), F32),
        ],
    )(place, q_all, s_all, q_outer, *s_outers)


def assemble_kernel(pairs, place, *refs):
    out = refs[-1]
    chunks, (own_other, first, rest) = refs[:pairs], refs[pairs:-1]
    rows, half = own_other.shape
    mine = place[0] // 2
    even = place[0] % 2 == 0
    for k in range(pairs):
        a = chunks[k][:rows, :].astype(F32)
        b = own_other if k == 0 else first if k == 1 else rest.at[pl.ds((k - 2) * rows, rows), :]
        b = b[...].astype(F32)
        where = pl.ds(pl.multiple_of((mine ^ k) * rows, 8), rows)
        out[where, :half] = jnp.where(even, a, b)
        out[where, half:] = jnp.where(even, b, a)


def assemble(place, chunks, own_other, first, rest):
    rows, half = own_other.shape
    pairs = len(chunks)
    return call(
        functools.partial(assemble_kernel, pairs),
        [SMEM] + [LOAD] * (pairs + 3),
        [((rows * pairs, 2 * half), F32)],
        flops=60 * 10**9,
        bytes_accessed=6 * 10**6,
    )(place, *chunks, own_other, first, rest)[0]


def per_device(
    question_states,
    question_ids,
    q_inner_weight,
    q_outer_weight,
    q_norm_gain,
    sql_states,
    sql_ids,
    s_inner_weight,
    s_outer_weight,
    s_norm_gain,
    positive_column,
):
    n_pb, n_sa = lax.axis_size("pb"), lax.axis_size("sa")
    p, a = lax.axis_index("pb"), lax.axis_index("sa")
    width, length = question_states.shape[-1], question_states.shape[-2]
    block = s_inner_weight.shape[1]
    units = q_inner_weight.shape[1]
    half = units // 2
    pairs = n_pb // 2
    far = range(GROUP, n_pb, GROUP)
    y, core = bit_at(a, 2), bit_at(a, 1)
    place = jnp.stack([p, a, core * 2 + y, y, core]).astype(jnp.int32)

    own_q, own_s = question_states[0, 0], sql_states[0, 0]
    q_normed, s_normed, piece = prepare(
        place, own_q, own_s, q_norm_gain, s_norm_gain, s_inner_weight, s_outer_weight
    )
    top = n_sa // 2
    mine = [swap(piece, "pb", k) for k in far]
    beside = [swap(piece, "sa", 1) for piece in mine]
    from_x, from_z = swap(s_normed, "pb", 1), swap(s_normed, "pb", 2)
    pair_token = swap(q_normed, "pb", 1)
    q_far = swap(q_normed, "sa", top)
    pair_bit = bit_at(p, 1)
    q_inner_half = lax.dynamic_slice_in_dim(q_inner_weight, pair_bit * half, half, 1)
    q_outer_half = lax.dynamic_slice_in_dim(q_outer_weight, pair_bit * half, half, 0)
    q_lengths = jnp.sum((question_ids[0] > 0).astype(jnp.int32), axis=-1)
    s_lengths = jnp.sum((sql_ids[0] > 0).astype(jnp.int32), axis=-1)
    (
        from_x,
        from_z,
        mine,
        beside,
        q_far,
        pair_token,
        s_late,
        q_inner_half,
        q_outer_half,
        q_lengths,
        s_lengths,
    ) = together(
        from_x,
        from_z,
        mine,
        beside,
        q_far,
        pair_token,
        s_normed,
        q_inner_half,
        q_outer_half,
        q_lengths,
        s_lengths,
    )

    across = [swap(piece, "sa", 2) for piece in mine]
    from_xz = swap(s_late, "pb", 3)
    q_tokens = [q_normed] + [None] * (n_sa - 1)
    q_tokens[top] = q_far
    for step in reversed(bits_of(n_sa)):
        for k in range(0, n_sa, 2 * step):
            if q_tokens[k + step] is None:
                q_tokens[k + step] = swap(q_tokens[k], "sa", step)

    q_pooled, q_part, q_rows = forward(
        place, q_lengths, own_q, q_tokens, q_inner_weight, q_outer_weight, [], 1
    )
    (own_slope,) = slopes(place, q_lengths, [q_rows], [q_inner_half], 1, length)
    q_steps = list(reversed(bits_of(n_sa)))
    for step in q_steps[:-1]:
        q_part = q_part + swap(q_part, "sa", step)
    from_xz, across, q_part, own_slope, pair_late = together(
        from_xz, across, q_part, own_slope, pair_token
    )
    pair_far = swap(pair_late, "sa", top)

    pieces = []
    for one, two, three in zip(mine, across, beside):
        pieces += [one, two, three, swap(two, "sa", 1)]
    s_tokens = [s_normed, from_x, from_z, from_xz]
    q_part = q_part + swap(q_part, "sa", q_steps[-1])
    meta = jnp.stack([positive_column, q_lengths], 1).astype(F32)
    meta = jnp.concatenate([meta, jnp.zeros((n_sa, 126), F32)], 1)
    q_all = jnp.concatenate([q_part, q_pooled, meta], 1)
    s_pooled, s_part, s_rows, *far_weights = forward(
        place, s_lengths, own_s, s_tokens, s_inner_weight, s_outer_weight, pieces, 0
    )
    s_inners = [s_inner_weight] + far_weights[0::2]
    s_outers = [s_outer_weight] + far_weights[1::2]
    s_part, q_all = together(s_part, q_all)

    s_others = [swap(s_part, "pb", k) for k in range(1, GROUP)]
    pair_meta = swap(q_all, "pb", 1)
    q_all = ordered(q_all, pair_meta, pair_bit)
    pair_lengths = pair_meta[:, width + units + 1].astype(jnp.int32)
    s_part = (s_part + s_others[0]) + (s_others[1] + s_others[2])
    s_part, q_all, pair_far = together(s_part, q_all, pair_far)

    s_sent = [jnp.concatenate([s_part, s_pooled[:, :block]], 1)]
    for i, k in enumerate(far):
        pooled_far = s_pooled[:, (i + 1) * block : (i + 2) * block]
        s_sent.append(swap(jnp.concatenate([s_part, pooled_far], 1), "pb", k))
    q_all = ordered(q_all, swap(q_all, "pb", 2), bit_at(p, 2))
    s_all = canonical(s_sent, p // GROUP)[None]
    pair_tokens = [pair_token] + [None] * (n_sa - 1)
    pair_tokens[top] = pair_far
    for step in reversed(bits_of(n_sa)):
        for k in range(0, n_sa, 2 * step):
            if pair_tokens[k + step] is None:
                pair_tokens[k + step] = swap(pair_tokens[k], "sa", step)
    s_all, q_all, pair_tokens = together(s_all, q_all, pair_tokens)
    for step in bits_of(n_pb)[2:]:
        q_all = ordered(q_all, swap(q_all, "pb", step), bit_at(p, step))
    pair_slope, pair_rows = slopes(place, pair_lengths, pair_tokens, [q_inner_half], 1, length)
    for step in reversed(bits_of(n_sa)):
        if step == 1:
            s_all, pair_slope = together(s_all, pair_slope)
        s_all = ordered(s_all, swap(s_all, "sa", step), bit_at(a, step))
    order = [
        sum(((i >> b) & 1) << (n_sa.bit_length() - 2 - b) for b in range(n_sa.bit_length() - 1))
        for i in range(n_sa)
    ]
    s_all = jnp.concatenate([s_all[order[i]] for i in range(n_sa)], 0)
    loss, q_grad, s_grad, q_hidden, s_hidden = scores(
        place, q_all, s_all, q_outer_half, s_outers, n_sa, n_pb, width
    )

    *q_sends, q_keep, q_gains = q_backward(
        place,
        q_rows,
        own_slope,
        pair_rows,
        pair_slope,
        q_hidden,
        q_inner_half,
        q_norm_gain,
        pairs,
        length,
    )
    q_arrived = [swap(x, "pb", 2 * k) for k, x in enumerate(q_sends, 1)]
    s_hidden, q_gains = together(s_hidden, q_gains)
    s_send, s_keep, packed = s_backward(
        place, s_lengths, s_rows, s_hidden, s_inners, s_norm_gain, q_gains, 0, length
    )

    def outer_gradient(pooled, grad):
        high = lax.reduce_precision(pooled, 8, 7)
        top = lax.reduce_precision(grad, 8, 7)
        left = jnp.concatenate([high, pooled - high, high], 0).astype(BF16)
        right = jnp.concatenate([top, top, grad - top], 0).astype(BF16)
        return lax.dot_general(left, right, CONTRACT_FIRST, preferred_element_type=F32)

    q_outer_grad = outer_gradient(q_all[:, width : width + units], q_grad)
    s_outer_grad = outer_gradient(s_all[:, width:], s_grad)
    strips = 6
    strip = s_send.shape[0] // strips
    s_beside = [swap(s_send[i * strip : (i + 1) * strip], "sa", 1) for i in range(strips)]
    s_total = s_keep + jnp.concatenate(s_beside, 0).astype(F32)
    q_arrived, s_total, packed, q_outer_grad, s_outer_grad = together(
        q_arrived, s_total, packed, q_outer_grad, s_outer_grad
    )

    q_total = q_keep
    for x in q_arrived:
        q_total = q_total + x.astype(F32)
    q_total = q_total.astype(BF16)
    rows = q_total.shape[0]

    def with_gains(x, gains):
        packed = pack(gains, x.shape[1])
        return jnp.concatenate([x, packed], 0), unpack(packed, width)

    def arrived_gains(x, rows):
        return x[:rows], unpack(x[rows:], width)

    gains = packed[:2].astype(F32) + packed[2:4].astype(F32)
    sent, gains = with_gains(q_total, gains)
    arrivals = [swap(sent, "pb", 2 * k) for k in range(1, pairs)]
    own_other = swap(q_total, "pb", 1)
    first = swap(arrivals[0][:rows], "pb", 1)
    size = width // 2
    for step in bits_of(n_sa)[1:]:
        size = size // 2
        bit = bit_at(a, step)
        away = lax.dynamic_slice_in_dim(s_total, (1 - bit) * size, size, 0).astype(BF16)
        arrived = swap(away, "sa", step)
        s_total = lax.dynamic_slice_in_dim(s_total, bit * size, size, 0)
        s_total = s_total + arrived.astype(F32)
    arrivals, own_other, first, s_total = together(arrivals, own_other, first, s_total)

    sums = [gains] + [arrived_gains(x, rows)[1] for x in arrivals]
    while len(sums) > 1:
        sums = [sums[i] + sums[i + 1] for i in range(0, len(sums), 2)]
    gains = sums[0] + swap(sums[0], "pb", 1)
    chunks = [q_total] + list(arrivals)
    rest = swap(jnp.concatenate([x[:rows] for x in chunks[2:]], 0), "pb", 1)
    q_inner_grad = assemble(place, chunks, own_other, first, rest)
    s_sum = s_total[:, :block]
    for i, k in enumerate(far):
        far_part = s_total[:, (i + 1) * block : (i + 2) * block].astype(BF16)
        s_sum = s_sum + swap(far_part, "pb", k).astype(F32)
    s_sum, gains = together(s_sum.astype(BF16), gains)

    for step in reversed(bits_of(n_sa)):
        size = s_sum.shape[0]
        sent, gains = with_gains(s_sum, gains)
        arrived, more = arrived_gains(swap(sent, "sa", step), size)
        gains = gains + more
        s_sum = ordered(s_sum, arrived, bit_at(a, step))
    s_inner_grad = s_sum.astype(F32)

    return (
        loss[0, 0],
        q_inner_grad,
        q_outer_grad,
        gains[0],
        s_inner_grad,
        s_outer_grad,
        gains[1],
    )


def solution(mesh):
    placed = (
        P("pb", "sa", None, None),
        P("pb", None, None),
        P(None, "sa"),
        P("sa", None),
        P(),
        P("sa", "pb", None, None),
        P("sa", None, None),
        P(None, "pb"),
        P("pb", None),
        P(),
        P("pb"),
    )
    return jax.shard_map(
        per_device,
        mesh=mesh,
        in_specs=placed,
        out_specs=(P(), P(None, "sa"), P("sa", None), P(), P(None, "pb"), P("pb", None), P()),
        check_vma=False,
    )
```

```python
import functools
import math

import jax
import jax.numpy as jnp
from jax import lax
from jax.experimental import pallas as pl
from jax.experimental.pallas import tpu as pltpu
from jax.sharding import PartitionSpec as P

HIGH = lax.Precision.HIGHEST
F32 = jnp.float32
BF16 = jnp.bfloat16
CONTRACT_FIRST = (((0,), (0,)), ((), ()))
CONTRACT_LAST = (((1,), (1,)), ((), ()))
GROUP = 4
PARTS = 4
GAIN_ROWS = 16
ROOT_HALF = 1.0 / math.sqrt(2.0)
VMEM = pl.BlockSpec(memory_space=pltpu.VMEM)
SMEM = pl.BlockSpec(memory_space=pltpu.SMEM)
HBM = pl.BlockSpec(memory_space=pltpu.HBM)
LOAD = "load"
LATE = "late"


def call(body, in_specs, out_shape, scratch=(), limit=16, flops=0, bytes_accessed=0, outs=None, aliases=None, staged=False):
    loads = [i for i, spec in enumerate(in_specs) if spec in (LOAD, LATE)]
    n_in, n_own = len(in_specs), len(out_shape) + len(scratch)

    def kernel(*refs):
        ins, rest = list(refs[:n_in]), refs[n_in:]
        copies = {}
        for j, i in enumerate(loads):
            buffer = rest[n_own + j]
            copies[i] = pltpu.make_async_copy(ins[i], buffer, rest[-1].at[j])
            ins[i] = buffer
        for wanted in (LOAD, LATE):
            for i in loads:
                if in_specs[i] is wanted:
                    copies[i].start()

        def arrive(wanted):
            for i in loads:
                if in_specs[i] is wanted:
                    copies[i].wait()

        if staged:
            body(arrive, *ins, *rest[:n_own])
        else:
            arrive(LOAD)
            body(*ins, *rest[:n_own])

    def run(*args):
        buffers = [pltpu.VMEM(args[i].shape, args[i].dtype) for i in loads]
        if loads:
            buffers.append(pltpu.SemaphoreType.DMA((len(loads),)))
        return pl.pallas_call(
            kernel,
            in_specs=[HBM if spec in (LOAD, LATE) else spec for spec in in_specs],
            out_shape=tuple(jax.ShapeDtypeStruct(s, t) for s, t in out_shape),
            out_specs=tuple(outs or [VMEM] * len(out_shape)),
            scratch_shapes=list(scratch) + buffers,
            input_output_aliases=aliases or {},
            cost_estimate=pl.CostEstimate(
                flops=flops, bytes_accessed=bytes_accessed, transcendentals=0
            ),
            compiler_params=pltpu.CompilerParams(vmem_limit_bytes=limit * 1024 * 1024),
        )(*args)

    return run


def gelu_value(v):
    return 0.5 * v * (1.0 + lax.erf(v * ROOT_HALF))


def gelu_slope(v):
    return 0.5 * (1.0 + lax.erf(v * ROOT_HALF)) + v * jnp.exp(-0.5 * v * v) * (
        1.0 / math.sqrt(2.0 * math.pi)
    )


def swap(x, axis, step):
    size = lax.axis_size(axis)
    return lax.ppermute(x, axis, [(i, i ^ step) for i in range(size)])


def ordered(mine, other, bit, axis=0):
    return jnp.where(
        bit == 0,
        jnp.concatenate([mine, other], axis),
        jnp.concatenate([other, mine], axis),
    )


def bits_of(size):
    return [1 << i for i in range(size.bit_length() - 1)]


def bit_at(place, step):
    return jnp.where((place & step) != 0, 1, 0)


def canonical(rows, place):
    rows = list(rows)
    for step in bits_of(len(rows)):
        odd = (place & step) != 0
        for k in range(len(rows)):
            if not k & step:
                first, second = rows[k], rows[k + step]
                rows[k] = jnp.where(odd, second, first)
                rows[k + step] = jnp.where(odd, first, second)
    return jnp.concatenate(rows, 0)


def together(*values):
    return lax.optimization_barrier(values)


def pack(gains, columns):
    high = lax.reduce_precision(gains, 8, 7)
    parts = jnp.concatenate([high, gains - high], 0).astype(BF16).reshape(-1, columns)
    return jnp.concatenate([parts, jnp.zeros((-parts.shape[0] % 16, columns), BF16)], 0)


def unpack(rows, width):
    parts = rows[: 4 * width // rows.shape[1]].reshape(4, width).astype(F32)
    return parts[:2] + parts[2:]


def column_tiles(size):
    tile = 256 if size % 256 == 0 else size
    return [slice(c, c + tile) for c in range(0, size, tile)]


def run_mask(rows, offset, length):
    return lax.broadcasted_iota(jnp.int32, (rows, 1), 0) + offset < length


def product(x, weight):
    return jnp.dot(x, weight, preferred_element_type=F32)


def rms_rows(x_ref, gain, out):
    x = x_ref[...].astype(F32)
    xhat = x * lax.rsqrt(jnp.mean(x * x, axis=-1, keepdims=True) + 1e-06)
    out[...] = (xhat * gain[...][None, :]).astype(BF16)


def prepare_kernel(
    fold,
    place,
    q_hbm,
    s_hbm,
    q_gain,
    s_gain,
    inner,
    outer,
    q_out,
    s_out,
    piece,
    q_ref,
    s_ref,
    sems,
):
    thin = inner.shape[0] // PARTS // fold
    block = inner.shape[1]
    rows = outer.shape[0] // PARTS
    index = place[2]
    tokens = [
        pltpu.make_async_copy(s_hbm, s_ref, sems.at[0]),
        pltpu.make_async_copy(q_hbm, q_ref, sems.at[1]),
    ]
    copies = []
    for i in range(fold):
        first = pl.multiple_of(index * (thin * fold) + i * thin, 16)
        copies.append(
            pltpu.make_async_copy(
                inner.at[pl.ds(first, thin), :],
                piece.at[pl.ds(0, thin), pl.ds(i * block, block)],
                sems.at[2 + i],
            )
        )
    copies.append(
        pltpu.make_async_copy(
            outer.at[pl.ds(pl.multiple_of(index * rows, 16), rows), :],
            piece.at[pl.ds(thin, rows), :],
            sems.at[2 + fold],
        )
    )
    for copy in tokens + copies:
        copy.start()
    tokens[0].wait()
    rms_rows(s_ref, s_gain, s_out)
    tokens[1].wait()
    x = q_ref[...].astype(F32)
    x = x - jnp.mean(x, axis=-1, keepdims=True)
    xhat = x * lax.rsqrt(jnp.mean(x * x, axis=-1, keepdims=True) + 1e-05)
    q_out[...] = (xhat * q_gain[...][None, :]).astype(BF16)
    for copy in copies:
        copy.wait()


def norm_only_kernel(q_ref, s_ref, q_gain, s_gain, q_out, s_out):
    rms_rows(s_ref, s_gain, s_out)
    x = q_ref[...].astype(F32)
    x = x - jnp.mean(x, axis=-1, keepdims=True)
    xhat = x * lax.rsqrt(jnp.mean(x * x, axis=-1, keepdims=True) + 1e-05)
    q_out[...] = (xhat * q_gain[...][None, :]).astype(BF16)


def prepare(place, own_q, own_s, q_gain, s_gain, inner, outer):
    width, block = inner.shape
    fold = width // block
    thin = width // PARTS // fold
    rows = block // PARTS
    if block % 128 == 0:
        return call(
            functools.partial(prepare_kernel, fold),
            [SMEM] + [HBM] * 2 + [LOAD] * 2 + [HBM] * 2,
            [(own_q.shape, BF16), (own_s.shape, BF16), ((thin + rows, width), BF16)],
            [
                pltpu.VMEM(own_q.shape, BF16),
                pltpu.VMEM(own_s.shape, BF16),
                pltpu.SemaphoreType.DMA((fold + 3,)),
            ],
            limit=60,
        )(place, own_q, own_s, q_gain, s_gain, inner, outer)
    piece = lax.dynamic_slice_in_dim(inner, place[2] * (thin * fold), thin * fold, 0)
    piece = jnp.concatenate([piece[i * thin : (i + 1) * thin] for i in range(fold)], 1)
    other = lax.dynamic_slice_in_dim(outer, place[2] * rows, rows, 0)
    normed = call(norm_only_kernel, [VMEM] * 4, [(own_q.shape, BF16), (own_s.shape, BF16)])(
        own_q, own_s, q_gain, s_gain
    )
    return *normed, jnp.concatenate([piece, other], 0)


def gather_rows(token_refs, rows, sems):
    copies = []
    first = 0
    for i, token in enumerate(token_refs):
        count = token.shape[0]
        copies.append(pltpu.make_async_copy(token, rows.at[pl.ds(first, count), :], sems.at[i]))
        first += count
    for copy in copies:
        copy.start()
    return copies


def forward_kernel(n, far, axis, arrive, place, lengths, positive, own, *refs):
    token_refs, refs = refs[:n], refs[n:]
    inners, outers = [refs[0]], [refs[1]]
    pieces = refs[2 : 2 + PARTS * far]
    refs = refs[2 + PARTS * far :]
    width = own.shape[1]
    if far:
        part, *outs = refs[: 2 + far]
        refs = refs[2 + far :]
    else:
        part, outs, refs = refs[0], [refs[0]], refs[1:]
    start = 0 if far else width
    results, buffers, sems = refs[: 1 + 2 * far], refs[1 + 2 * far : -1], refs[-1]
    rows = buffers[0]
    gathered = gather_rows(token_refs, rows, sems)
    leaving = [
        pltpu.make_async_copy(x, y, sems.at[i]) for i, (x, y) in enumerate(zip(buffers, results))
    ]
    arrive(LOAD)
    for copy in gathered:
        copy.wait()
    leaving[0].start()
    me = place[axis]
    span = own.shape[0]
    total = rows.shape[0] // span
    index = lax.broadcasted_iota(jnp.int32, (total, 1), 0)

    def pool(inner, out):
        for columns in column_tiles(inner.shape[1]):
            weight = inner[:, columns]
            tile = jnp.zeros((total, weight.shape[1]), F32)
            for k in range(total):
                length = lengths[me ^ k]
                value = gelu_value(product(rows[k * span : (k + 1) * span, :], weight))
                value = jnp.where(run_mask(span, 0, length), value, 0.0)
                row = jnp.sum(value, axis=0, keepdims=True) / length.astype(F32)
                tile = jnp.where(index == ((me ^ k) & (total - 1)), row, tile)
            out[:, start + columns.start : start + columns.stop] = tile

    pool(inners[0], outs[0])
    arrive(LATE)
    y, core = place[3], place[4]
    places = (
        core * 2 + y,
        core * 2 + (1 - y),
        (1 - core) * 2 + y,
        (1 - core) * 2 + (1 - y),
    )
    for f in range(far):
        inner, outer = buffers[1 + 2 * f : 3 + 2 * f]
        block = inner.shape[1]
        fold = inner.shape[0] // block
        thin = inner.shape[0] // PARTS // fold
        deep = block // PARTS
        for j in range(PARTS):
            piece = pieces[PARTS * f + j]
            for i in range(fold):
                first = pl.multiple_of(places[j] * (thin * fold) + i * thin, 16)
                inner[pl.ds(first, thin), :] = piece[:thin, i * block : (i + 1) * block]
            first = pl.multiple_of(places[j] * deep, 16)
            outer[pl.ds(first, deep), :] = piece[thin:, :]
        inners.append(inner)
        outers.append(outer)
    for copy in leaving[1:]:
        copy.start()
    for inner, out in zip(inners[1:], outs[1:]):
        pool(inner, out)
    x = own[...].astype(F32)
    length = lengths[me]
    x = jnp.where(run_mask(span, 0, length), x, 0.0)
    own_row = jnp.sum(x, axis=0, keepdims=True) / length.astype(F32)
    result = jnp.where(index == (me & (total - 1)), own_row, 0.0)
    for outer, out in zip(outers, outs):
        units = out[:, start : start + outer.shape[0]]
        high = units.astype(BF16)
        rest = units - high.astype(F32)
        middle = rest.astype(BF16)
        low = (rest - middle.astype(F32)).astype(BF16)
        weight = outer[...]
        result = result + (
            product(high, weight) + (product(middle, weight) + product(low, weight))
        )
    part[:, :width] = result
    if positive is not None:
        lane = lax.broadcasted_iota(jnp.int32, (total, 128), 1)
        row = lax.broadcasted_iota(jnp.int32, (total, 128), 0)
        meta = jnp.zeros((total, 128), F32)
        for k in range(total):
            pair = jnp.where(lane == 0, positive[k], jnp.where(lane == 1, lengths[k], 0))
            meta = jnp.where(row == k, pair.astype(F32), meta)
        part[:, part.shape[1] - 128 :] = meta
    for copy in leaving:
        copy.wait()


def forward(place, lengths, positive, own, tokens, inner, outer, pieces, axis):
    width, units = inner.shape
    far = len(pieces) // PARTS
    rows = sum(t.shape[0] for t in tokens)
    count = rows // own.shape[0]
    large = [(rows, width)] + [(width, units), (units, width)] * far
    columns = width + units + 128
    body = functools.partial(forward_kernel, len(tokens), far, axis)
    if far:
        return call(
            lambda arrive, place, lengths, *refs: body(arrive, place, lengths, None, *refs),
            [SMEM] * 2 + [LOAD] + [HBM] * len(tokens) + [LOAD] * 2 + [LATE] * len(pieces),
            [((count, width), F32)]
            + [((count, units), F32)] * (1 + far)
            + [(x, BF16) for x in large],
            [pltpu.VMEM(x, BF16) for x in large]
            + [pltpu.SemaphoreType.DMA((max(len(tokens), len(large)),))],
            flops=3 * 10**9,
            bytes_accessed=3 * 10**6,
            limit=62,
            outs=[VMEM] * (2 + far) + [HBM] * len(large),
            staged=True,
        )(place, lengths, own, *tokens, inner, outer, *pieces)
    return call(
        body,
        [SMEM] * 3 + [LOAD] + [HBM] * len(tokens) + [LOAD] * 2,
        [((count, columns), F32)] + [(x, BF16) for x in large],
        [pltpu.VMEM(x, BF16) for x in large] + [pltpu.SemaphoreType.DMA((len(tokens),))],
        flops=3 * 10**9,
        bytes_accessed=3 * 10**6,
        limit=24,
        outs=[VMEM] + [HBM] * len(large),
        staged=True,
    )(place, lengths, positive, own, *tokens, inner, outer)


def slope_kernel(n, axis, span, gathered, place, lengths, *refs):
    token_refs = refs[:n]
    if gathered:
        weights, out, rows = refs[n:-3], refs[-3], refs[-2]
        for copy in gather_rows(token_refs, rows, refs[-1]):
            copy.wait()
    else:
        weights, out, rows = refs[n:-1], refs[-1], token_refs[0]
    me = place[axis] & (lengths.shape[0] - 1)
    base = 0
    for weight in weights:
        for columns in column_tiles(weight.shape[1]):
            w = weight[:, columns]
            for k in range(out.shape[0] // span):
                length = lengths[me ^ k]
                part = slice(k * span, (k + 1) * span)
                value = gelu_slope(product(rows[part, :], w)) * (1.0 / length.astype(F32))
                value = jnp.where(run_mask(span, 0, length), value, 0.0)
                out[part, base + columns.start : base + columns.stop] = value
        base += weight.shape[1]


def slopes(place, lengths, tokens, weights, axis, span):
    gathered = len(tokens) > 1
    rows = sum(t.shape[0] for t in tokens)
    width, units = weights[0].shape[0], sum(w.shape[1] for w in weights)
    return call(
        functools.partial(slope_kernel, len(tokens), axis, span, gathered),
        [SMEM] * 2 + [HBM if gathered else VMEM] * len(tokens) + [VMEM] * len(weights),
        [((rows, units), F32)] + [((rows, width), BF16)] * gathered,
        [pltpu.SemaphoreType.DMA((len(tokens),))] * gathered,
        flops=3 * rows * units * width,
        bytes_accessed=3 * 10**6,
    )(place, lengths, *tokens, *weights)


def inner_gradient(row_refs, slope_refs, hidden, weights, gain, total, span):
    base = 0
    gains = jnp.zeros((total.shape[0], 128), F32)
    for weight in weights:
        for columns in column_tiles(weight.shape[1]):
            part = slice(base + columns.start, base + columns.stop)
            result = 0.0
            k = 0
            for rows, slope in zip(row_refs, slope_refs):
                for first in range(0, rows.shape[0], span):
                    dpre = slope[first : first + span, part] * hidden[k : k + 1, part]
                    result = result + lax.dot_general(
                        rows[first : first + span, :],
                        dpre.astype(BF16),
                        CONTRACT_FIRST,
                        preferred_element_type=F32,
                    )
                    k += 1
            total[:, part] = result
            shares = result * weight[:, columns].astype(F32)
            lanes = shares.shape[1]
            if lanes % 128:
                shares = jnp.concatenate(
                    [shares, jnp.zeros((shares.shape[0], -lanes % 128), F32)], 1
                )
            for c in range(0, shares.shape[1], 128):
                gains = gains + shares[:, c : c + 128]
        base += weight.shape[1]
    return jnp.sum(gains.T, axis=0, keepdims=True) / gain[...][None, :]


def q_backward_kernel(pairs, span, place, *refs):
    rows, pair_rows, own_slope, pair_slope, hidden, weight, gain = refs[:7]
    sends, (keep, gains, total) = refs[7 : 6 + pairs], refs[6 + pairs :]
    gains[...] = inner_gradient(
        [rows, pair_rows], [own_slope, pair_slope], hidden, [weight], gain, total, span
    )
    mine = place[0] // 2
    size = keep.shape[0]
    keep[...] = total[pl.ds(pl.multiple_of(mine * size, 16), size), :]
    for k in range(1, pairs):
        first = pl.multiple_of((mine ^ k) * size, 16)
        sends[k - 1][...] = total[pl.ds(first, size), :].astype(BF16)


def q_backward(place, rows, slope, pair_rows, pair_slope, hidden, weight, gain, pairs, span):
    width, units = weight.shape
    size = width // pairs
    return call(
        functools.partial(q_backward_kernel, pairs, span),
        [SMEM] + [VMEM] * 6 + [LOAD],
        [((size, units), BF16)] * (pairs - 1) + [((size, units), F32), ((1, width), F32)],
        [pltpu.VMEM((width, units), F32)],
        flops=4 * 10**9,
        bytes_accessed=3 * 10**6,
    )(place, rows, pair_rows, slope, pair_slope, hidden, weight, gain)


def s_backward_kernel(span, axis, place, lengths, *refs):
    rows, hidden = refs[:2]
    weights = refs[2:-7]
    gain, q_gains, send, keep, gains, total, slope = refs[-7:]
    slope_kernel(1, axis, span, False, place, lengths, rows, *weights, slope)
    s_gains = inner_gradient([rows], [slope], hidden, weights, gain, total, span)
    core = place[4]
    size = keep.shape[0]
    keep[...] = total[pl.ds(pl.multiple_of(core * size, 16), size), :]
    first = pl.multiple_of((1 - core) * size, 16)
    send[...] = total[pl.ds(first, size), :].astype(BF16)
    index = lax.broadcasted_iota(jnp.int32, (GAIN_ROWS, 1), 0)
    packed = jnp.zeros((GAIN_ROWS, total.shape[0]), F32)
    for i, row in enumerate((q_gains[...], s_gains)):
        high = row.astype(BF16).astype(F32)
        packed = jnp.where(index == i, high, packed)
        packed = jnp.where(index == i + 2, row - high, packed)
    gains[...] = packed.astype(BF16)


def s_backward(place, lengths, rows, hidden, weights, gain, q_gains, axis, span):
    width = weights[0].shape[0]
    units = sum(w.shape[1] for w in weights)
    return call(
        functools.partial(s_backward_kernel, span, axis),
        [SMEM] * 2 + [VMEM] * 2 + [LOAD] + [VMEM] * (len(weights) - 1) + [LOAD, VMEM],
        [
            ((width // 2, units), BF16),
            ((width // 2, units), F32),
            ((GAIN_ROWS, width), BF16),
        ],
        [pltpu.VMEM((width, units), F32), pltpu.VMEM((rows.shape[0], units), F32)],
        flops=6 * 10**9,
        bytes_accessed=3 * 10**6,
    )(place, lengths, rows, hidden, *weights, gain, q_gains)


def score_kernel(
    n_sa, n_pb, width, place, q_ref, s_ref, q_outer, *refs
):
    s_outers = refs[:-5]
    loss_ref, q_grad_ref, s_grad_ref, q_hidden, s_hidden = refs[-5:]
    p, a = place[0], place[1]
    q, s = q_ref[:, :width], s_ref[:, :width]
    positive = q_ref[:, q_ref.shape[1] - 128 : q_ref.shape[1] - 127].astype(jnp.int32)
    count = q.shape[0]
    scale = 1.0 / math.sqrt(width)
    score = scale * lax.dot_general(q, s, CONTRACT_LAST, precision=HIGH, preferred_element_type=F32)
    columns = lax.broadcasted_iota(jnp.int32, (count, count), 1)
    match = (positive == columns).astype(F32)
    row_max = jnp.max(score, axis=1, keepdims=True)
    col_max = jnp.max(score, axis=0, keepdims=True)
    row_lse = row_max + jnp.log(jnp.sum(jnp.exp(score - row_max), axis=1, keepdims=True))
    col_lse = col_max + jnp.log(jnp.sum(jnp.exp(score - col_max), axis=0, keepdims=True))
    matched = jnp.sum(match * score, axis=1, keepdims=True)
    row_part = jnp.sum(row_lse - matched, axis=0, keepdims=True)
    col_part = jnp.sum(col_lse, axis=1, keepdims=True) - jnp.sum(matched, axis=0, keepdims=True)
    loss_ref[...] = (row_part + col_part) / (2.0 * count)
    dscore = 0.5 * (jnp.exp(score - row_lse) + jnp.exp(score - col_lse) - 2.0 * match)
    q_grad = scale * jnp.dot(dscore, s, precision=HIGH, preferred_element_type=F32)
    s_grad = scale * lax.dot_general(
        dscore, q, CONTRACT_FIRST, precision=HIGH, preferred_element_type=F32
    )
    q_grad_ref[...] = q_grad
    s_grad_ref[...] = s_grad

    def hidden(grad, places, outers, out):
        rows = places.shape[0]
        chosen = lax.broadcasted_iota(jnp.int32, (rows, count), 1) == places
        picked = jnp.dot(chosen.astype(F32), grad, precision=HIGH, preferred_element_type=F32)
        high = picked.astype(BF16)
        low = (picked - high.astype(F32)).astype(BF16)
        base = 0
        for outer in outers:
            weight = outer[...]
            result = lax.dot_general(high, weight, CONTRACT_LAST, preferred_element_type=F32)
            result += lax.dot_general(low, weight, CONTRACT_LAST, preferred_element_type=F32)
            out[:, base : base + weight.shape[0]] = result
            base += weight.shape[0]

    index = lax.broadcasted_iota(jnp.int32, (2 * n_sa, 1), 0)
    pair = (index >= n_sa).astype(jnp.int32)
    hidden(q_grad, (p ^ pair) * n_sa + (a ^ (index - pair * n_sa)), [q_outer], q_hidden)
    index = lax.broadcasted_iota(jnp.int32, (8, 1), 0)
    hidden(s_grad, a * n_pb + (p ^ index), s_outers, s_hidden)


def scores(place, q_all, s_all, q_outer, s_outers, n_sa, n_pb, width):
    shape = (q_all.shape[0], width)
    units = sum(w.shape[0] for w in s_outers)
    return call(
        functools.partial(score_kernel, n_sa, n_pb, width),
        [SMEM] + [VMEM] * 3 + [LOAD] + [VMEM] * (len(s_outers) - 1),
        [
            ((1, 1), F32),
            (shape, F32),
            (shape, F32),
            ((2 * n_sa, q_outer.shape[0]), F32),
            ((8, units), F32),
        ],
    )(place, q_all, s_all, q_outer, *s_outers)


def assemble_kernel(first, own_rows, packed, continued, place, *refs):
    out, buffer, sems = refs[-3:]
    refs = refs[1:-3] if continued else refs[:-3]
    count = len(refs) - 1 if packed else len(refs) // 2
    chunks, others = refs[:count], refs[count:]
    mine = place[0] // 2
    even = place[0] % 2 == 0
    copies = []
    for k in range(count):
        half = chunks[k].shape[1]
        a = chunks[k][:own_rows, :].astype(F32)
        b = others[0][k * own_rows : (k + 1) * own_rows, :] if packed else others[k][...]
        b = b.astype(F32)
        buffer[k, :, :half] = jnp.where(even, a, b)
        buffer[k, :, half:] = jnp.where(even, b, a)
        place_of = pl.multiple_of((mine ^ (first + k)) * own_rows, 8)
        copies.append(
            pltpu.make_async_copy(buffer.at[k], out.at[pl.ds(place_of, own_rows), :], sems.at[k])
        )
        copies[-1].start()
    for copy in copies:
        copy.wait()


def assemble(place, chunks, others, first, rows, shape, packed=False, earlier=None):
    before = [] if earlier is None else [earlier]
    return call(
        functools.partial(assemble_kernel, first, rows, packed, bool(before)),
        [SMEM] + [HBM] * len(before) + [LOAD] * (len(chunks) + len(others)),
        [(shape, F32)],
        [
            pltpu.VMEM((len(chunks), rows, shape[1]), F32),
            pltpu.SemaphoreType.DMA((len(chunks),)),
        ],
        flops=2 * 10**9,
        bytes_accessed=3 * 10**6,
        outs=[HBM],
        aliases={1: 0} if before else {},
    )(place, *before, *chunks, *others)[0]


def per_device(
    question_states,
    question_ids,
    q_inner_weight,
    q_outer_weight,
    q_norm_gain,
    sql_states,
    sql_ids,
    s_inner_weight,
    s_outer_weight,
    s_norm_gain,
    positive_column,
):
    n_pb, n_sa = lax.axis_size("pb"), lax.axis_size("sa")
    p, a = lax.axis_index("pb"), lax.axis_index("sa")
    width, length = question_states.shape[-1], question_states.shape[-2]
    block = s_inner_weight.shape[1]
    units = q_inner_weight.shape[1]
    half = units // 2
    pairs = n_pb // 2
    far = range(GROUP, n_pb, GROUP)
    y, core = bit_at(a, 2), bit_at(a, 1)
    place = jnp.stack([p, a, core * 2 + y, y, core]).astype(jnp.int32)

    own_q, own_s = question_states[0, 0], sql_states[0, 0]
    q_normed, s_normed, piece = prepare(
        place, own_q, own_s, q_norm_gain, s_norm_gain, s_inner_weight, s_outer_weight
    )
    top = n_sa // 2
    mine = [swap(piece, "pb", k) for k in far]
    beside = [swap(piece, "sa", 1) for piece in mine]
    from_x, from_z = swap(s_normed, "pb", 1), swap(s_normed, "pb", 2)
    q_far = swap(q_normed, "sa", top)
    pair_bit = bit_at(p, 1)
    q_inner_half = lax.dynamic_slice_in_dim(q_inner_weight, pair_bit * half, half, 1)
    q_outer_half = lax.dynamic_slice_in_dim(q_outer_weight, pair_bit * half, half, 0)
    q_lengths = jnp.sum((question_ids[0] > 0).astype(jnp.int32), axis=-1)
    s_lengths = jnp.sum((sql_ids[0] > 0).astype(jnp.int32), axis=-1)
    (
        from_x,
        from_z,
        mine,
        beside,
        q_far,
        q_late,
        q_inner_half,
        q_outer_half,
        q_lengths,
        s_lengths,
    ) = together(
        from_x,
        from_z,
        mine,
        beside,
        q_far,
        q_normed,
        q_inner_half,
        q_outer_half,
        q_lengths,
        s_lengths,
    )

    across = [swap(piece, "sa", 2) for piece in mine]
    from_xz = swap(from_x, "pb", 2)
    pair_token = swap(q_late, "pb", 1)
    q_tokens = [q_normed] + [None] * (n_sa - 1)
    q_tokens[top] = q_far
    for step in reversed(bits_of(n_sa)):
        for k in range(0, n_sa, 2 * step):
            if q_tokens[k + step] is None:
                q_tokens[k + step] = swap(q_tokens[k], "sa", step)

    q_all, q_rows = forward(
        place, q_lengths, positive_column, own_q, q_tokens, q_inner_weight, q_outer_weight, [], 1
    )
    in_part = jnp.arange(q_all.shape[1], dtype=jnp.int32)[None, :] < width

    def add_part(x, step):
        return jnp.where(in_part, x + swap(x, "sa", step), x)

    (own_slope,) = slopes(place, q_lengths, [q_rows], [q_inner_half], 1, length)
    q_steps = list(reversed(bits_of(n_sa)))
    for step in q_steps[:-1]:
        q_all = add_part(q_all, step)
    from_xz, across, q_all, own_slope, pair_token = together(
        from_xz, across, q_all, own_slope, pair_token
    )
    pair_far = swap(pair_token, "sa", top)

    pieces = []
    for one, two, three in zip(mine, across, beside):
        pieces += [one, two, three, swap(two, "sa", 1)]
    s_tokens = [s_normed, from_x, from_z, from_xz]
    q_all = add_part(q_all, q_steps[-1])
    s_part, *s_rest = forward(
        place, s_lengths, None, own_s, s_tokens, s_inner_weight, s_outer_weight, pieces, 0
    )
    s_pooled, s_rows, far_weights = (
        s_rest[: 1 + len(far)],
        s_rest[1 + len(far)],
        s_rest[2 + len(far) :],
    )
    s_inners = [s_inner_weight] + far_weights[0::2]
    s_outers = [s_outer_weight] + far_weights[1::2]
    s_part, q_all = together(s_part, q_all)

    s_others = [swap(s_part, "pb", k) for k in range(1, GROUP)]
    pair_meta = swap(q_all, "pb", 1)
    q_all = ordered(q_all, pair_meta, pair_bit)
    pair_lengths = pair_meta[:, width + units + 1].astype(jnp.int32)
    s_part = (s_part + s_others[0]) + (s_others[1] + s_others[2])
    s_part, q_all, pair_lengths = together(s_part, q_all, pair_lengths)

    s_sent = [jnp.concatenate([s_part, s_pooled[0]], 1)]
    for i, k in enumerate(far, 1):
        s_sent.append(swap(jnp.concatenate([s_part, s_pooled[i]], 1), "pb", k))
    q_all = ordered(q_all, swap(q_all, "pb", 2), bit_at(p, 2))
    s_all = canonical(s_sent, p // GROUP)[None]
    pair_beside = swap(pair_token, "sa", 1)
    s_all, q_all, pair_far, pair_beside = together(s_all, q_all, pair_far, pair_beside)
    pair_tokens = [[pair_token], [pair_beside]] + [None] * (n_sa - 2)
    pair_tokens[top] = [pair_far]
    for step in reversed(bits_of(n_sa)):
        for k in range(0, n_sa, 2 * step):
            if pair_tokens[k + step] is None:
                cuts = 4 if step == 1 else 1
                pair_tokens[k + step] = [
                    swap(x, "sa", step) for x in jnp.split(pair_tokens[k][0], cuts, axis=0)
                ]
    pair_tokens = [x for parts in pair_tokens for x in parts]
    for step in bits_of(n_pb)[2:]:
        q_all = ordered(q_all, swap(q_all, "pb", step), bit_at(p, step))
    pair_slope, pair_rows = slopes(place, pair_lengths, pair_tokens, [q_inner_half], 1, length)
    for step in reversed(bits_of(n_sa)):
        if step == 1:
            s_all, pair_slope = together(s_all, pair_slope)
        s_all = ordered(s_all, swap(s_all, "sa", step), bit_at(a, step))
    order = [
        sum(((i >> b) & 1) << (n_sa.bit_length() - 2 - b) for b in range(n_sa.bit_length() - 1))
        for i in range(n_sa)
    ]
    s_all = jnp.concatenate([s_all[order[i]] for i in range(n_sa)], 0)
    loss, q_grad, s_grad, q_hidden, s_hidden = scores(
        place, q_all, s_all, q_outer_half, s_outers, n_sa, n_pb, width
    )

    *q_sends, q_keep, q_gains = q_backward(
        place,
        q_rows,
        own_slope,
        pair_rows,
        pair_slope,
        q_hidden,
        q_inner_half,
        q_norm_gain,
        pairs,
        length,
    )
    q_arrived = [swap(x, "pb", 2 * k) for k, x in enumerate(q_sends, 1)]
    s_hidden, q_gains = together(s_hidden, q_gains)
    s_send, s_keep, packed = s_backward(
        place, s_lengths, s_rows, s_hidden, s_inners, s_norm_gain, q_gains, 0, length
    )

    def outer_gradient(pooled, grad):
        high = lax.reduce_precision(pooled, 8, 7)
        top = lax.reduce_precision(grad, 8, 7)
        left = jnp.concatenate([high, pooled - high, high], 0).astype(BF16)
        right = jnp.concatenate([top, top, grad - top], 0).astype(BF16)
        return lax.dot_general(left, right, CONTRACT_FIRST, preferred_element_type=F32)

    q_outer_grad = outer_gradient(q_all[:, width : width + units], q_grad)
    s_outer_grad = outer_gradient(s_all[:, width:], s_grad)
    strips = 6
    strip = s_send.shape[0] // strips
    s_beside = [swap(s_send[i * strip : (i + 1) * strip], "sa", 1) for i in range(strips)]
    s_total = s_keep + jnp.concatenate(s_beside, 0).astype(F32)
    q_arrived, s_total, packed, q_outer_grad, s_outer_grad = together(
        q_arrived, s_total, packed, q_outer_grad, s_outer_grad
    )

    q_total = q_keep
    for x in q_arrived:
        q_total = q_total + x.astype(F32)
    q_total = q_total.astype(BF16)
    rows = q_total.shape[0]

    def with_gains(x, gains):
        packed = pack(gains, x.shape[1])
        return jnp.concatenate([x, packed], 0), unpack(packed, width)

    def arrived_gains(x, rows):
        return x[:rows], unpack(x[rows:], width)

    gains = packed[:2].astype(F32) + packed[2:4].astype(F32)
    sent, gains = with_gains(q_total, gains)
    arrivals = [swap(sent, "pb", 2 * k) for k in range(1, pairs)]
    own_other = swap(q_total, "pb", 1)
    first = swap(arrivals[0][:rows], "pb", 1)
    size = width // 2
    for step in bits_of(n_sa)[1:]:
        size = size // 2
        bit = bit_at(a, step)
        away = lax.dynamic_slice_in_dim(s_total, (1 - bit) * size, size, 0).astype(BF16)
        arrived = swap(away, "sa", step)
        s_total = lax.dynamic_slice_in_dim(s_total, bit * size, size, 0)
        s_total = s_total + arrived.astype(F32)
    arrivals, own_other, first, s_total = together(arrivals, own_other, first, s_total)

    sums = [gains] + [arrived_gains(x, rows)[1] for x in arrivals]
    while len(sums) > 1:
        sums = [sums[i] + sums[i + 1] for i in range(0, len(sums), 2)]
    gains = sums[0] + swap(sums[0], "pb", 1)
    chunks = [q_total] + list(arrivals)
    rest = swap(jnp.concatenate([x[:rows] for x in chunks[2:]], 0), "pb", 1)
    shape = (width, 2 * half)
    q_inner_grad = assemble(place, chunks[:2], [own_other, first], 0, rows, shape)
    s_sum = s_total[:, :block]
    for i, k in enumerate(far):
        far_part = s_total[:, (i + 1) * block : (i + 2) * block].astype(BF16)
        s_sum = s_sum + swap(far_part, "pb", k).astype(F32)
    s_sum, gains, q_inner_grad, rest = together(s_sum.astype(BF16), gains, q_inner_grad, rest)
    q_inner_grad = assemble(place, chunks[2:], [rest], 2, rows, shape, True, q_inner_grad)

    for step in reversed(bits_of(n_sa)):
        size = s_sum.shape[0]
        if step == 1:
            s_sum, q_inner_grad = together(s_sum, q_inner_grad)
        sent, gains = with_gains(s_sum, gains)
        arrived, more = arrived_gains(swap(sent, "sa", step), size)
        gains = gains + more
        s_sum = ordered(s_sum, arrived, bit_at(a, step))
    s_inner_grad = s_sum.astype(F32)

    return (
        loss[0, 0],
        q_inner_grad,
        q_outer_grad,
        gains[0],
        s_inner_grad,
        s_outer_grad,
        gains[1],
    )


def solution(mesh):
    placed = (
        P("pb", "sa", None, None),
        P("pb", None, None),
        P(None, "sa"),
        P("sa", None),
        P(),
        P("sa", "pb", None, None),
        P("sa", None, None),
        P(None, "pb"),
        P("pb", None),
        P(),
        P("pb"),
    )
    return jax.shard_map(
        per_device,
        mesh=mesh,
        in_specs=placed,
        out_specs=(P(), P(None, "sa"), P("sa", None), P(), P(None, "pb"), P("pb", None), P()),
        check_vma=False,
    )
```

```python
import functools
import math

import jax
import jax.numpy as jnp
from jax import lax
from jax.experimental import pallas as pl
from jax.experimental.pallas import tpu as pltpu
from jax.sharding import PartitionSpec as P

HIGH = lax.Precision.HIGHEST
F32 = jnp.float32
BF16 = jnp.bfloat16
CONTRACT_FIRST = (((0,), (0,)), ((), ()))
CONTRACT_LAST = (((1,), (1,)), ((), ()))
GROUP = 4
PARTS = 4
GAIN_ROWS = 16
ROOT_HALF = 1.0 / math.sqrt(2.0)
VMEM = pl.BlockSpec(memory_space=pltpu.VMEM)
SMEM = pl.BlockSpec(memory_space=pltpu.SMEM)
HBM = pl.BlockSpec(memory_space=pltpu.HBM)
LOAD = "load"
LATE = "late"


def call(body, in_specs, out_shape, scratch=(), limit=16, flops=0, bytes_accessed=0, outs=None, aliases=None, staged=False):
    loads = [i for i, spec in enumerate(in_specs) if spec in (LOAD, LATE)]
    n_in, n_own = len(in_specs), len(out_shape) + len(scratch)

    def kernel(*refs):
        ins, rest = list(refs[:n_in]), refs[n_in:]
        copies = {}
        for j, i in enumerate(loads):
            buffer = rest[n_own + j]
            copies[i] = pltpu.make_async_copy(ins[i], buffer, rest[-1].at[j])
            ins[i] = buffer

        def start(wanted):
            for i in loads:
                if in_specs[i] is wanted:
                    copies[i].start()

        def arrive(wanted):
            for i in loads:
                if in_specs[i] is wanted:
                    copies[i].wait()

        if staged:
            body(start, arrive, *ins, *rest[:n_own])
        else:
            start(LOAD)
            arrive(LOAD)
            body(*ins, *rest[:n_own])

    def run(*args):
        buffers = [pltpu.VMEM(args[i].shape, args[i].dtype) for i in loads]
        if loads:
            buffers.append(pltpu.SemaphoreType.DMA((len(loads),)))
        return pl.pallas_call(
            kernel,
            in_specs=[HBM if spec in (LOAD, LATE) else spec for spec in in_specs],
            out_shape=tuple(jax.ShapeDtypeStruct(s, t) for s, t in out_shape),
            out_specs=tuple(outs or [VMEM] * len(out_shape)),
            scratch_shapes=list(scratch) + buffers,
            input_output_aliases=aliases or {},
            cost_estimate=pl.CostEstimate(
                flops=flops, bytes_accessed=bytes_accessed, transcendentals=0
            ),
            compiler_params=pltpu.CompilerParams(vmem_limit_bytes=limit * 1024 * 1024),
        )(*args)

    return run


def gelu_value(v):
    return 0.5 * v * (1.0 + lax.erf(v * ROOT_HALF))


def gelu_slope(v):
    return 0.5 * (1.0 + lax.erf(v * ROOT_HALF)) + v * jnp.exp(-0.5 * v * v) * (
        1.0 / math.sqrt(2.0 * math.pi)
    )


def swap(x, axis, step):
    size = lax.axis_size(axis)
    return lax.ppermute(x, axis, [(i, i ^ step) for i in range(size)])


def ordered(mine, other, bit, axis=0):
    return jnp.where(
        bit == 0,
        jnp.concatenate([mine, other], axis),
        jnp.concatenate([other, mine], axis),
    )


def bits_of(size):
    return [1 << i for i in range(size.bit_length() - 1)]


def bit_at(place, step):
    return jnp.where((place & step) != 0, 1, 0)


def canonical(rows, place):
    rows = list(rows)
    for step in bits_of(len(rows)):
        odd = (place & step) != 0
        for k in range(len(rows)):
            if not k & step:
                first, second = rows[k], rows[k + step]
                rows[k] = jnp.where(odd, second, first)
                rows[k + step] = jnp.where(odd, first, second)
    return jnp.concatenate(rows, 0)


def together(*values):
    return lax.optimization_barrier(values)


def pack(gains, columns):
    high = lax.reduce_precision(gains, 8, 7)
    parts = jnp.concatenate([high, gains - high], 0).astype(BF16).reshape(-1, columns)
    return jnp.concatenate([parts, jnp.zeros((-parts.shape[0] % 16, columns), BF16)], 0)


def unpack(rows, width):
    parts = rows[: 4 * width // rows.shape[1]].reshape(4, width).astype(F32)
    return parts[:2] + parts[2:]


def column_tiles(size):
    tile = 256 if size % 256 == 0 else size
    return [slice(c, c + tile) for c in range(0, size, tile)]


def run_mask(rows, offset, length):
    return lax.broadcasted_iota(jnp.int32, (rows, 1), 0) + offset < length


def product(x, weight):
    return jnp.dot(x, weight, preferred_element_type=F32)


def rms_rows(x_ref, gain, out):
    x = x_ref[...].astype(F32)
    xhat = x * lax.rsqrt(jnp.mean(x * x, axis=-1, keepdims=True) + 1e-06)
    out[...] = (xhat * gain[...][None, :]).astype(BF16)


def prepare_kernel(
    fold,
    start,
    arrive,
    place,
    q_hbm,
    s_hbm,
    q_gain,
    s_gain,
    inner,
    outer,
    q_out,
    s_out,
    piece,
    q_ref,
    s_ref,
    sems,
):
    thin = inner.shape[0] // PARTS // fold
    block = inner.shape[1]
    rows = outer.shape[0] // PARTS
    index = place[2]
    tokens = [
        pltpu.make_async_copy(s_hbm, s_ref, sems.at[0]),
        pltpu.make_async_copy(q_hbm, q_ref, sems.at[1]),
    ]
    copies = []
    for i in range(fold):
        first = pl.multiple_of(index * (thin * fold) + i * thin, 16)
        copies.append(
            pltpu.make_async_copy(
                inner.at[pl.ds(first, thin), :],
                piece.at[pl.ds(0, thin), pl.ds(i * block, block)],
                sems.at[2 + i],
            )
        )
    copies.append(
        pltpu.make_async_copy(
            outer.at[pl.ds(pl.multiple_of(index * rows, 16), rows), :],
            piece.at[pl.ds(thin, rows), :],
            sems.at[2 + fold],
        )
    )
    for copy in tokens:
        copy.start()
    start(LOAD)
    for copy in copies:
        copy.start()
    arrive(LOAD)
    tokens[0].wait()
    rms_rows(s_ref, s_gain, s_out)
    tokens[1].wait()
    x = q_ref[...].astype(F32)
    x = x - jnp.mean(x, axis=-1, keepdims=True)
    xhat = x * lax.rsqrt(jnp.mean(x * x, axis=-1, keepdims=True) + 1e-05)
    q_out[...] = (xhat * q_gain[...][None, :]).astype(BF16)
    for copy in copies:
        copy.wait()


def norm_only_kernel(q_ref, s_ref, q_gain, s_gain, q_out, s_out):
    rms_rows(s_ref, s_gain, s_out)
    x = q_ref[...].astype(F32)
    x = x - jnp.mean(x, axis=-1, keepdims=True)
    xhat = x * lax.rsqrt(jnp.mean(x * x, axis=-1, keepdims=True) + 1e-05)
    q_out[...] = (xhat * q_gain[...][None, :]).astype(BF16)


def prepare(place, own_q, own_s, q_gain, s_gain, inner, outer):
    width, block = inner.shape
    fold = width // block
    thin = width // PARTS // fold
    rows = block // PARTS
    if block % 128 == 0:
        return call(
            functools.partial(prepare_kernel, fold),
            [SMEM] + [HBM] * 2 + [LOAD] * 2 + [HBM] * 2,
            [(own_q.shape, BF16), (own_s.shape, BF16), ((thin + rows, width), BF16)],
            [
                pltpu.VMEM(own_q.shape, BF16),
                pltpu.VMEM(own_s.shape, BF16),
                pltpu.SemaphoreType.DMA((fold + 3,)),
            ],
            limit=60,
            staged=True,
        )(place, own_q, own_s, q_gain, s_gain, inner, outer)
    piece = lax.dynamic_slice_in_dim(inner, place[2] * (thin * fold), thin * fold, 0)
    piece = jnp.concatenate([piece[i * thin : (i + 1) * thin] for i in range(fold)], 1)
    other = lax.dynamic_slice_in_dim(outer, place[2] * rows, rows, 0)
    normed = call(norm_only_kernel, [VMEM] * 4, [(own_q.shape, BF16), (own_s.shape, BF16)])(
        own_q, own_s, q_gain, s_gain
    )
    return *normed, jnp.concatenate([piece, other], 0)


def gather_rows(token_refs, rows, sems):
    copies = []
    first = 0
    for i, token in enumerate(token_refs):
        count = token.shape[0]
        copies.append(pltpu.make_async_copy(token, rows.at[pl.ds(first, count), :], sems.at[i]))
        first += count
    for copy in copies:
        copy.start()
    return copies


def forward_kernel(n, far, axis, start, arrive, place, lengths, positive, own, *refs):
    token_refs, refs = refs[:n], refs[n:]
    inners, outers = [refs[0]], [refs[1]]
    pieces = refs[2 : 2 + PARTS * far]
    refs = refs[2 + PARTS * far :]
    width = own.shape[1]
    if far:
        part, *outs = refs[: 2 + far]
        refs = refs[2 + far :]
    else:
        part, outs, refs = refs[0], [refs[0]], refs[1:]
    offset = 0 if far else width
    results, buffers, sems = refs[: 1 + 2 * far], refs[1 + 2 * far : -1], refs[-1]
    rows = buffers[0]
    start(LOAD)
    gathered = gather_rows(token_refs, rows, sems)
    start(LATE)
    leaving = [
        pltpu.make_async_copy(x, y, sems.at[i]) for i, (x, y) in enumerate(zip(buffers, results))
    ]
    arrive(LOAD)
    for copy in gathered:
        copy.wait()
    leaving[0].start()
    me = place[axis]
    span = own.shape[0]
    total = rows.shape[0] // span
    index = lax.broadcasted_iota(jnp.int32, (total, 1), 0)

    def pool(inner, out):
        for columns in column_tiles(inner.shape[1]):
            weight = inner[:, columns]
            tile = jnp.zeros((total, weight.shape[1]), F32)
            for k in range(total):
                length = lengths[me ^ k]
                value = gelu_value(product(rows[k * span : (k + 1) * span, :], weight))
                value = jnp.where(run_mask(span, 0, length), value, 0.0)
                row = jnp.sum(value, axis=0, keepdims=True) / length.astype(F32)
                tile = jnp.where(index == ((me ^ k) & (total - 1)), row, tile)
            out[:, offset + columns.start : offset + columns.stop] = tile

    pool(inners[0], outs[0])
    arrive(LATE)
    y, core = place[3], place[4]
    places = (
        core * 2 + y,
        core * 2 + (1 - y),
        (1 - core) * 2 + y,
        (1 - core) * 2 + (1 - y),
    )
    for f in range(far):
        inner, outer = buffers[1 + 2 * f : 3 + 2 * f]
        block = inner.shape[1]
        fold = inner.shape[0] // block
        thin = inner.shape[0] // PARTS // fold
        deep = block // PARTS
        for j in range(PARTS):
            piece = pieces[PARTS * f + j]
            for i in range(fold):
                first = pl.multiple_of(places[j] * (thin * fold) + i * thin, 16)
                inner[pl.ds(first, thin), :] = piece[:thin, i * block : (i + 1) * block]
            first = pl.multiple_of(places[j] * deep, 16)
            outer[pl.ds(first, deep), :] = piece[thin:, :]
        inners.append(inner)
        outers.append(outer)
    for copy in leaving[1:]:
        copy.start()
    for inner, out in zip(inners[1:], outs[1:]):
        pool(inner, out)
    x = own[...].astype(F32)
    length = lengths[me]
    x = jnp.where(run_mask(span, 0, length), x, 0.0)
    own_row = jnp.sum(x, axis=0, keepdims=True) / length.astype(F32)
    result = jnp.where(index == (me & (total - 1)), own_row, 0.0)
    for outer, out in zip(outers, outs):
        units = out[:, offset : offset + outer.shape[0]]
        high = units.astype(BF16)
        rest = units - high.astype(F32)
        middle = rest.astype(BF16)
        low = (rest - middle.astype(F32)).astype(BF16)
        weight = outer[...]
        result = result + (
            product(high, weight) + (product(middle, weight) + product(low, weight))
        )
    part[:, :width] = result
    if positive is not None:
        lane = lax.broadcasted_iota(jnp.int32, (total, 128), 1)
        row = lax.broadcasted_iota(jnp.int32, (total, 128), 0)
        meta = jnp.zeros((total, 128), F32)
        for k in range(total):
            pair = jnp.where(lane == 0, positive[k], jnp.where(lane == 1, lengths[k], 0))
            meta = jnp.where(row == k, pair.astype(F32), meta)
        part[:, part.shape[1] - 128 :] = meta
    for copy in leaving:
        copy.wait()


def forward(place, lengths, positive, own, tokens, inner, outer, pieces, axis):
    width, units = inner.shape
    far = len(pieces) // PARTS
    rows = sum(t.shape[0] for t in tokens)
    count = rows // own.shape[0]
    large = [(rows, width)] + [(width, units), (units, width)] * far
    columns = width + units + 128
    body = functools.partial(forward_kernel, len(tokens), far, axis)
    if far:
        return call(
            lambda start, arrive, place, lengths, *refs: body(
                start, arrive, place, lengths, None, *refs
            ),
            [SMEM] * 2 + [LATE] + [HBM] * len(tokens) + [LOAD, LATE] + [LATE] * len(pieces),
            [((count, width), F32)]
            + [((count, units), F32)] * (1 + far)
            + [(x, BF16) for x in large],
            [pltpu.VMEM(x, BF16) for x in large]
            + [pltpu.SemaphoreType.DMA((max(len(tokens), len(large)),))],
            flops=3 * 10**9,
            bytes_accessed=3 * 10**6,
            limit=62,
            outs=[VMEM] * (2 + far) + [HBM] * len(large),
            staged=True,
        )(place, lengths, own, *tokens, inner, outer, *pieces)
    return call(
        body,
        [SMEM] * 3 + [LATE] + [HBM] * len(tokens) + [LOAD, LATE],
        [((count, columns), F32)] + [(x, BF16) for x in large],
        [pltpu.VMEM(x, BF16) for x in large] + [pltpu.SemaphoreType.DMA((len(tokens),))],
        flops=3 * 10**9,
        bytes_accessed=3 * 10**6,
        limit=24,
        outs=[VMEM] + [HBM] * len(large),
        staged=True,
    )(place, lengths, positive, own, *tokens, inner, outer)


def slope_kernel(n, axis, span, gathered, place, lengths, *refs):
    token_refs = refs[:n]
    if gathered:
        weights, out, rows = refs[n:-3], refs[-3], refs[-2]
        for copy in gather_rows(token_refs, rows, refs[-1]):
            copy.wait()
    else:
        weights, out, rows = refs[n:-1], refs[-1], token_refs[0]
    me = place[axis] & (lengths.shape[0] - 1)
    base = 0
    for weight in weights:
        for columns in column_tiles(weight.shape[1]):
            w = weight[:, columns]
            for k in range(out.shape[0] // span):
                length = lengths[me ^ k]
                part = slice(k * span, (k + 1) * span)
                value = gelu_slope(product(rows[part, :], w)) * (1.0 / length.astype(F32))
                value = jnp.where(run_mask(span, 0, length), value, 0.0)
                out[part, base + columns.start : base + columns.stop] = value
        base += weight.shape[1]


def slopes(place, lengths, tokens, weights, axis, span):
    gathered = len(tokens) > 1
    rows = sum(t.shape[0] for t in tokens)
    width, units = weights[0].shape[0], sum(w.shape[1] for w in weights)
    return call(
        functools.partial(slope_kernel, len(tokens), axis, span, gathered),
        [SMEM] * 2 + [HBM if gathered else VMEM] * len(tokens) + [VMEM] * len(weights),
        [((rows, units), F32)] + [((rows, width), BF16)] * gathered,
        [pltpu.SemaphoreType.DMA((len(tokens),))] * gathered,
        flops=3 * rows * units * width,
        bytes_accessed=3 * 10**6,
    )(place, lengths, *tokens, *weights)


def inner_gradient(row_refs, slope_refs, hidden, weights, gain, total, span, arrive=None):
    base = 0
    gains = jnp.zeros((total.shape[0], 128), F32)
    for weight in weights:
        for columns in column_tiles(weight.shape[1]):
            part = slice(base + columns.start, base + columns.stop)
            result = 0.0
            k = 0
            for rows, slope in zip(row_refs, slope_refs):
                for first in range(0, rows.shape[0], span):
                    dpre = slope[first : first + span, part] * hidden[k : k + 1, part]
                    result = result + lax.dot_general(
                        rows[first : first + span, :],
                        dpre.astype(BF16),
                        CONTRACT_FIRST,
                        preferred_element_type=F32,
                    )
                    k += 1
            total[:, part] = result
            shares = result * weight[:, columns].astype(F32)
            lanes = shares.shape[1]
            if lanes % 128:
                shares = jnp.concatenate(
                    [shares, jnp.zeros((shares.shape[0], -lanes % 128), F32)], 1
                )
            for c in range(0, shares.shape[1], 128):
                gains = gains + shares[:, c : c + 128]
        base += weight.shape[1]
    if arrive is not None:
        arrive(LOAD)
    return jnp.sum(gains.T, axis=0, keepdims=True) / gain[...][None, :]


def q_backward_kernel(pairs, span, start, arrive, place, *refs):
    start(LOAD)
    rows, pair_rows, own_slope, pair_slope, hidden, weight, gain = refs[:7]
    sends, (keep, gains, total) = refs[7 : 6 + pairs], refs[6 + pairs :]
    gains[...] = inner_gradient(
        [rows, pair_rows], [own_slope, pair_slope], hidden, [weight], gain, total, span, arrive
    )
    mine = place[0] // 2
    size = keep.shape[0]
    keep[...] = total[pl.ds(pl.multiple_of(mine * size, 16), size), :]
    for k in range(1, pairs):
        first = pl.multiple_of((mine ^ k) * size, 16)
        sends[k - 1][...] = total[pl.ds(first, size), :].astype(BF16)


def q_backward(place, rows, slope, pair_rows, pair_slope, hidden, weight, gain, pairs, span):
    width, units = weight.shape
    size = width // pairs
    return call(
        functools.partial(q_backward_kernel, pairs, span),
        [SMEM] + [VMEM] * 6 + [LOAD],
        [((size, units), BF16)] * (pairs - 1) + [((size, units), F32), ((1, width), F32)],
        [pltpu.VMEM((width, units), F32)],
        flops=4 * 10**9,
        bytes_accessed=3 * 10**6,
        staged=True,
    )(place, rows, pair_rows, slope, pair_slope, hidden, weight, gain)


def s_backward_kernel(span, axis, place, lengths, *refs):
    rows, hidden = refs[:2]
    weights = refs[2:-7]
    gain, q_gains, send, keep, gains, total, slope = refs[-7:]
    slope_kernel(1, axis, span, False, place, lengths, rows, *weights, slope)
    s_gains = inner_gradient([rows], [slope], hidden, weights, gain, total, span)
    core = place[4]
    size = keep.shape[0]
    keep[...] = total[pl.ds(pl.multiple_of(core * size, 16), size), :]
    first = pl.multiple_of((1 - core) * size, 16)
    send[...] = total[pl.ds(first, size), :].astype(BF16)
    index = lax.broadcasted_iota(jnp.int32, (GAIN_ROWS, 1), 0)
    packed = jnp.zeros((GAIN_ROWS, total.shape[0]), F32)
    for i, row in enumerate((q_gains[...], s_gains)):
        high = row.astype(BF16).astype(F32)
        packed = jnp.where(index == i, high, packed)
        packed = jnp.where(index == i + 2, row - high, packed)
    gains[...] = packed.astype(BF16)


def s_backward(place, lengths, rows, hidden, weights, gain, q_gains, axis, span):
    width = weights[0].shape[0]
    units = sum(w.shape[1] for w in weights)
    return call(
        functools.partial(s_backward_kernel, span, axis),
        [SMEM] * 2 + [VMEM] * 2 + [LOAD] + [VMEM] * (len(weights) - 1) + [LOAD, VMEM],
        [
            ((width // 2, units), BF16),
            ((width // 2, units), F32),
            ((GAIN_ROWS, width), BF16),
        ],
        [pltpu.VMEM((width, units), F32), pltpu.VMEM((rows.shape[0], units), F32)],
        flops=6 * 10**9,
        bytes_accessed=3 * 10**6,
    )(place, lengths, rows, hidden, *weights, gain, q_gains)


def score_kernel(
    n_sa, n_pb, width, start, arrive, place, q_ref, s_ref, q_outer, *refs
):
    start(LOAD)
    s_outers = refs[:-5]
    loss_ref, q_grad_ref, s_grad_ref, q_hidden, s_hidden = refs[-5:]
    p, a = place[0], place[1]
    q, s = q_ref[:, :width], s_ref[:, :width]
    positive = q_ref[:, q_ref.shape[1] - 128 : q_ref.shape[1] - 127].astype(jnp.int32)
    count = q.shape[0]
    scale = 1.0 / math.sqrt(width)
    score = scale * lax.dot_general(q, s, CONTRACT_LAST, precision=HIGH, preferred_element_type=F32)
    columns = lax.broadcasted_iota(jnp.int32, (count, count), 1)
    match = (positive == columns).astype(F32)
    row_max = jnp.max(score, axis=1, keepdims=True)
    col_max = jnp.max(score, axis=0, keepdims=True)
    row_lse = row_max + jnp.log(jnp.sum(jnp.exp(score - row_max), axis=1, keepdims=True))
    col_lse = col_max + jnp.log(jnp.sum(jnp.exp(score - col_max), axis=0, keepdims=True))
    matched = jnp.sum(match * score, axis=1, keepdims=True)
    row_part = jnp.sum(row_lse - matched, axis=0, keepdims=True)
    col_part = jnp.sum(col_lse, axis=1, keepdims=True) - jnp.sum(matched, axis=0, keepdims=True)
    loss_ref[...] = (row_part + col_part) / (2.0 * count)
    dscore = 0.5 * (jnp.exp(score - row_lse) + jnp.exp(score - col_lse) - 2.0 * match)
    q_grad = scale * jnp.dot(dscore, s, precision=HIGH, preferred_element_type=F32)
    s_grad = scale * lax.dot_general(
        dscore, q, CONTRACT_FIRST, precision=HIGH, preferred_element_type=F32
    )
    q_grad_ref[...] = q_grad
    s_grad_ref[...] = s_grad

    def hidden(grad, places, outers, out):
        rows = places.shape[0]
        chosen = lax.broadcasted_iota(jnp.int32, (rows, count), 1) == places
        picked = jnp.dot(chosen.astype(F32), grad, precision=HIGH, preferred_element_type=F32)
        high = picked.astype(BF16)
        low = (picked - high.astype(F32)).astype(BF16)
        base = 0
        for outer in outers:
            weight = outer[...]
            result = lax.dot_general(high, weight, CONTRACT_LAST, preferred_element_type=F32)
            result += lax.dot_general(low, weight, CONTRACT_LAST, preferred_element_type=F32)
            out[:, base : base + weight.shape[0]] = result
            base += weight.shape[0]

    index = lax.broadcasted_iota(jnp.int32, (2 * n_sa, 1), 0)
    pair = (index >= n_sa).astype(jnp.int32)
    hidden(q_grad, (p ^ pair) * n_sa + (a ^ (index - pair * n_sa)), [q_outer], q_hidden)
    index = lax.broadcasted_iota(jnp.int32, (8, 1), 0)
    arrive(LOAD)
    hidden(s_grad, a * n_pb + (p ^ index), s_outers, s_hidden)


def scores(place, q_all, s_all, q_outer, s_outers, n_sa, n_pb, width):
    shape = (q_all.shape[0], width)
    units = sum(w.shape[0] for w in s_outers)
    return call(
        functools.partial(score_kernel, n_sa, n_pb, width),
        [SMEM] + [VMEM] * 3 + [LOAD] + [VMEM] * (len(s_outers) - 1),
        [
            ((1, 1), F32),
            (shape, F32),
            (shape, F32),
            ((2 * n_sa, q_outer.shape[0]), F32),
            ((8, units), F32),
        ],
        staged=True,
    )(place, q_all, s_all, q_outer, *s_outers)


def assemble_kernel(first, own_rows, packed, continued, place, *refs):
    out, buffer, sems = refs[-3:]
    refs = refs[1:-3] if continued else refs[:-3]
    count = len(refs) - 1 if packed else len(refs) // 2
    chunks, others = refs[:count], refs[count:]
    mine = place[0] // 2
    even = place[0] % 2 == 0
    copies = []
    for k in range(count):
        half = chunks[k].shape[1]
        a = chunks[k][:own_rows, :].astype(F32)
        b = others[0][k * own_rows : (k + 1) * own_rows, :] if packed else others[k][...]
        b = b.astype(F32)
        buffer[k, :, :half] = jnp.where(even, a, b)
        buffer[k, :, half:] = jnp.where(even, b, a)
        place_of = pl.multiple_of((mine ^ (first + k)) * own_rows, 8)
        copies.append(
            pltpu.make_async_copy(buffer.at[k], out.at[pl.ds(place_of, own_rows), :], sems.at[k])
        )
        copies[-1].start()
    for copy in copies:
        copy.wait()


def assemble(place, chunks, others, first, rows, shape, packed=False, earlier=None):
    before = [] if earlier is None else [earlier]
    return call(
        functools.partial(assemble_kernel, first, rows, packed, bool(before)),
        [SMEM] + [HBM] * len(before) + [LOAD] * (len(chunks) + len(others)),
        [(shape, F32)],
        [
            pltpu.VMEM((len(chunks), rows, shape[1]), F32),
            pltpu.SemaphoreType.DMA((len(chunks),)),
        ],
        flops=2 * 10**9,
        bytes_accessed=3 * 10**6,
        outs=[HBM],
        aliases={1: 0} if before else {},
    )(place, *before, *chunks, *others)[0]


def per_device(
    question_states,
    question_ids,
    q_inner_weight,
    q_outer_weight,
    q_norm_gain,
    sql_states,
    sql_ids,
    s_inner_weight,
    s_outer_weight,
    s_norm_gain,
    positive_column,
):
    n_pb, n_sa = lax.axis_size("pb"), lax.axis_size("sa")
    p, a = lax.axis_index("pb"), lax.axis_index("sa")
    width, length = question_states.shape[-1], question_states.shape[-2]
    block = s_inner_weight.shape[1]
    units = q_inner_weight.shape[1]
    half = units // 2
    pairs = n_pb // 2
    far = range(GROUP, n_pb, GROUP)
    y, core = bit_at(a, 2), bit_at(a, 1)
    place = jnp.stack([p, a, core * 2 + y, y, core]).astype(jnp.int32)

    own_q, own_s = question_states[0, 0], sql_states[0, 0]
    q_normed, s_normed, piece = prepare(
        place, own_q, own_s, q_norm_gain, s_norm_gain, s_inner_weight, s_outer_weight
    )
    top = n_sa // 2
    mine = [swap(piece, "pb", k) for k in far]
    beside = [swap(piece, "sa", 1) for piece in mine]
    from_x, from_z = swap(s_normed, "pb", 1), swap(s_normed, "pb", 2)
    q_far = swap(q_normed, "sa", top)
    pair_bit = bit_at(p, 1)
    q_inner_half = lax.dynamic_slice_in_dim(q_inner_weight, pair_bit * half, half, 1)
    q_outer_half = lax.dynamic_slice_in_dim(q_outer_weight, pair_bit * half, half, 0)
    q_lengths = jnp.sum((question_ids[0] > 0).astype(jnp.int32), axis=-1)
    s_lengths = jnp.sum((sql_ids[0] > 0).astype(jnp.int32), axis=-1)
    (
        from_x,
        from_z,
        mine,
        beside,
        q_far,
        q_late,
        q_inner_half,
        q_outer_half,
        q_lengths,
        s_lengths,
    ) = together(
        from_x,
        from_z,
        mine,
        beside,
        q_far,
        q_normed,
        q_inner_half,
        q_outer_half,
        q_lengths,
        s_lengths,
    )

    across = [swap(piece, "sa", 2) for piece in mine]
    from_xz = swap(from_x, "pb", 2)
    pair_token = swap(q_late, "pb", 1)
    q_tokens = [q_normed] + [None] * (n_sa - 1)
    q_tokens[top] = q_far
    for step in reversed(bits_of(n_sa)):
        for k in range(0, n_sa, 2 * step):
            if q_tokens[k + step] is None:
                q_tokens[k + step] = swap(q_tokens[k], "sa", step)

    q_all, q_rows = forward(
        place, q_lengths, positive_column, own_q, q_tokens, q_inner_weight, q_outer_weight, [], 1
    )
    in_part = jnp.arange(q_all.shape[1], dtype=jnp.int32)[None, :] < width

    def add_part(x, step):
        return jnp.where(in_part, x + swap(x, "sa", step), x)

    (own_slope,) = slopes(place, q_lengths, [q_rows], [q_inner_half], 1, length)
    q_steps = list(reversed(bits_of(n_sa)))
    for step in q_steps[:-1]:
        q_all = add_part(q_all, step)
    from_xz, across, q_all, own_slope, pair_token = together(
        from_xz, across, q_all, own_slope, pair_token
    )
    pair_far = swap(pair_token, "sa", top)

    pieces = []
    for one, two, three in zip(mine, across, beside):
        pieces += [one, two, three, swap(two, "sa", 1)]
    s_tokens = [s_normed, from_x, from_z, from_xz]
    q_all = add_part(q_all, q_steps[-1])
    s_part, *s_rest = forward(
        place, s_lengths, None, own_s, s_tokens, s_inner_weight, s_outer_weight, pieces, 0
    )
    s_pooled, s_rows, far_weights = (
        s_rest[: 1 + len(far)],
        s_rest[1 + len(far)],
        s_rest[2 + len(far) :],
    )
    s_inners = [s_inner_weight] + far_weights[0::2]
    s_outers = [s_outer_weight] + far_weights[1::2]

    s_others = [swap(s_part, "pb", k) for k in range(1, GROUP)]
    pair_meta, s_part = together(swap(q_all, "pb", 1), s_part)
    q_all = ordered(q_all, pair_meta, pair_bit)
    pair_lengths = pair_meta[:, width + units + 1].astype(jnp.int32)
    q_all = ordered(q_all, swap(q_all, "pb", 2), bit_at(p, 2))
    s_part = (s_part + s_others[0]) + (s_others[1] + s_others[2])
    pair_tokens = [pair_token] + [None] * (n_sa - 1)
    pair_tokens[top] = pair_far
    for step in reversed(bits_of(n_sa)):
        for k in range(0, n_sa, 2 * step):
            if pair_tokens[k + step] is None:
                pair_tokens[k + step] = swap(pair_tokens[k], "sa", step)
    s_part, q_all, pair_lengths, pair_tokens = together(s_part, q_all, pair_lengths, pair_tokens)

    s_sent = [jnp.concatenate([s_part, s_pooled[0]], 1)]
    for i, k in enumerate(far, 1):
        s_sent.append(swap(jnp.concatenate([s_part, s_pooled[i]], 1), "pb", k))
    s_all = canonical(s_sent, p // GROUP)[None]
    for step in bits_of(n_pb)[2:]:
        q_all = ordered(q_all, swap(q_all, "pb", step), bit_at(p, step))
    pair_slope, pair_rows = slopes(place, pair_lengths, pair_tokens, [q_inner_half], 1, length)
    for step in reversed(bits_of(n_sa)):
        if step == 1:
            s_all, pair_slope = together(s_all, pair_slope)
        s_all = ordered(s_all, swap(s_all, "sa", step), bit_at(a, step))
    order = [
        sum(((i >> b) & 1) << (n_sa.bit_length() - 2 - b) for b in range(n_sa.bit_length() - 1))
        for i in range(n_sa)
    ]
    s_all = jnp.concatenate([s_all[order[i]] for i in range(n_sa)], 0)
    loss, q_grad, s_grad, q_hidden, s_hidden = scores(
        place, q_all, s_all, q_outer_half, s_outers, n_sa, n_pb, width
    )

    *q_sends, q_keep, q_gains = q_backward(
        place,
        q_rows,
        own_slope,
        pair_rows,
        pair_slope,
        q_hidden,
        q_inner_half,
        q_norm_gain,
        pairs,
        length,
    )
    q_arrived = [swap(x, "pb", 2 * k) for k, x in enumerate(q_sends, 1)]
    s_hidden, q_gains = together(s_hidden, q_gains)
    s_send, s_keep, packed = s_backward(
        place, s_lengths, s_rows, s_hidden, s_inners, s_norm_gain, q_gains, 0, length
    )

    def outer_gradient(pooled, grad):
        high = lax.reduce_precision(pooled, 8, 7)
        top = lax.reduce_precision(grad, 8, 7)
        left = jnp.concatenate([high, pooled - high, high], 0).astype(BF16)
        right = jnp.concatenate([top, top, grad - top], 0).astype(BF16)
        return lax.dot_general(left, right, CONTRACT_FIRST, preferred_element_type=F32)

    q_outer_grad = outer_gradient(q_all[:, width : width + units], q_grad)
    s_outer_grad = outer_gradient(s_all[:, width:], s_grad)
    strips = 6
    strip = s_send.shape[0] // strips
    s_beside = [swap(s_send[i * strip : (i + 1) * strip], "sa", 1) for i in range(strips)]
    s_total = s_keep + jnp.concatenate(s_beside, 0).astype(F32)
    q_arrived, s_total, packed, q_outer_grad, s_outer_grad = together(
        q_arrived, s_total, packed, q_outer_grad, s_outer_grad
    )

    q_total = q_keep
    for x in q_arrived:
        q_total = q_total + x.astype(F32)
    q_total = q_total.astype(BF16)
    rows = q_total.shape[0]

    def with_gains(x, gains):
        packed = pack(gains, x.shape[1])
        return jnp.concatenate([x, packed], 0), unpack(packed, width)

    def arrived_gains(x, rows):
        return x[:rows], unpack(x[rows:], width)

    gains = packed[:2].astype(F32) + packed[2:4].astype(F32)
    sent, gains = with_gains(q_total, gains)
    arrivals = [swap(sent, "pb", 2 * k) for k in range(1, pairs)]
    own_other = swap(q_total, "pb", 1)
    first = swap(arrivals[0][:rows], "pb", 1)
    size = width // 2
    for step in bits_of(n_sa)[1:]:
        size = size // 2
        bit = bit_at(a, step)
        away = lax.dynamic_slice_in_dim(s_total, (1 - bit) * size, size, 0).astype(BF16)
        arrived = swap(away, "sa", step)
        s_total = lax.dynamic_slice_in_dim(s_total, bit * size, size, 0)
        s_total = s_total + arrived.astype(F32)
    arrivals, own_other, first, s_total = together(arrivals, own_other, first, s_total)

    sums = [gains] + [arrived_gains(x, rows)[1] for x in arrivals]
    while len(sums) > 1:
        sums = [sums[i] + sums[i + 1] for i in range(0, len(sums), 2)]
    gains = sums[0] + swap(sums[0], "pb", 1)
    chunks = [q_total] + list(arrivals)
    rest = swap(jnp.concatenate([x[:rows] for x in chunks[2:]], 0), "pb", 1)
    shape = (width, 2 * half)
    q_inner_grad = assemble(place, chunks[:2], [own_other, first], 0, rows, shape)
    s_sum = s_total[:, :block]
    for i, k in enumerate(far):
        far_part = s_total[:, (i + 1) * block : (i + 2) * block].astype(BF16)
        s_sum = s_sum + swap(far_part, "pb", k).astype(F32)
    s_sum, gains, q_inner_grad, rest = together(s_sum.astype(BF16), gains, q_inner_grad, rest)
    q_inner_grad = assemble(place, chunks[2:], [rest], 2, rows, shape, True, q_inner_grad)

    for step in reversed(bits_of(n_sa)):
        size = s_sum.shape[0]
        if step == 1:
            s_sum, q_inner_grad = together(s_sum, q_inner_grad)
        sent, gains = with_gains(s_sum, gains)
        arrived, more = arrived_gains(swap(sent, "sa", step), size)
        gains = gains + more
        s_sum = ordered(s_sum, arrived, bit_at(a, step))
    s_inner_grad = s_sum.astype(F32)

    return (
        loss[0, 0],
        q_inner_grad,
        q_outer_grad,
        gains[0],
        s_inner_grad,
        s_outer_grad,
        gains[1],
    )


def solution(mesh):
    placed = (
        P("pb", "sa", None, None),
        P("pb", None, None),
        P(None, "sa"),
        P("sa", None),
        P(),
        P("sa", "pb", None, None),
        P("sa", None, None),
        P(None, "pb"),
        P("pb", None),
        P(),
        P("pb"),
    )
    return jax.shard_map(
        per_device,
        mesh=mesh,
        in_specs=placed,
        out_specs=(P(), P(None, "sa"), P("sa", None), P(), P(None, "pb"), P("pb", None), P()),
        check_vma=False,
    )
```

```python
import functools
import math

import jax
import jax.numpy as jnp
from jax import lax
from jax.experimental import pallas as pl
from jax.experimental.pallas import tpu as pltpu
from jax.sharding import PartitionSpec as P

HIGH = lax.Precision.HIGHEST
F32 = jnp.float32
BF16 = jnp.bfloat16
CONTRACT_FIRST = (((0,), (0,)), ((), ()))
CONTRACT_LAST = (((1,), (1,)), ((), ()))
GROUP = 4
PARTS = 4
GAIN_ROWS = 16
ROOT_HALF = 1.0 / math.sqrt(2.0)
VMEM = pl.BlockSpec(memory_space=pltpu.VMEM)
SMEM = pl.BlockSpec(memory_space=pltpu.SMEM)
HBM = pl.BlockSpec(memory_space=pltpu.HBM)
LOAD = "load"
LATE = "late"


def call(body, in_specs, out_shape, scratch=(), limit=16, flops=0, bytes_accessed=0, outs=None, aliases=None, staged=False):
    loads = [i for i, spec in enumerate(in_specs) if spec in (LOAD, LATE)]
    n_in, n_own = len(in_specs), len(out_shape) + len(scratch)

    def kernel(*refs):
        ins, rest = list(refs[:n_in]), refs[n_in:]
        copies = {}
        for j, i in enumerate(loads):
            buffer = rest[n_own + j]
            copies[i] = pltpu.make_async_copy(ins[i], buffer, rest[-1].at[j])
            ins[i] = buffer

        def start(wanted):
            for i in loads:
                if in_specs[i] is wanted:
                    copies[i].start()

        def arrive(wanted):
            for i in loads:
                if in_specs[i] is wanted:
                    copies[i].wait()

        if staged:
            body(start, arrive, *ins, *rest[:n_own])
        else:
            start(LOAD)
            arrive(LOAD)
            body(*ins, *rest[:n_own])

    def run(*args):
        buffers = [pltpu.VMEM(args[i].shape, args[i].dtype) for i in loads]
        if loads:
            buffers.append(pltpu.SemaphoreType.DMA((len(loads),)))
        return pl.pallas_call(
            kernel,
            in_specs=[HBM if spec in (LOAD, LATE) else spec for spec in in_specs],
            out_shape=tuple(jax.ShapeDtypeStruct(s, t) for s, t in out_shape),
            out_specs=tuple(outs or [VMEM] * len(out_shape)),
            scratch_shapes=list(scratch) + buffers,
            input_output_aliases=aliases or {},
            cost_estimate=pl.CostEstimate(
                flops=flops, bytes_accessed=bytes_accessed, transcendentals=0
            ),
            compiler_params=pltpu.CompilerParams(vmem_limit_bytes=limit * 1024 * 1024),
        )(*args)

    return run


def gelu_value(v):
    return 0.5 * v * (1.0 + lax.erf(v * ROOT_HALF))


def gelu_slope(v):
    return 0.5 * (1.0 + lax.erf(v * ROOT_HALF)) + v * jnp.exp(-0.5 * v * v) * (
        1.0 / math.sqrt(2.0 * math.pi)
    )


def swap(x, axis, step):
    size = lax.axis_size(axis)
    return lax.ppermute(x, axis, [(i, i ^ step) for i in range(size)])


def ordered(mine, other, bit, axis=0):
    return jnp.where(
        bit == 0,
        jnp.concatenate([mine, other], axis),
        jnp.concatenate([other, mine], axis),
    )


def bits_of(size):
    return [1 << i for i in range(size.bit_length() - 1)]


def bit_at(place, step):
    return jnp.where((place & step) != 0, 1, 0)


def canonical(rows, place):
    rows = list(rows)
    for step in bits_of(len(rows)):
        odd = (place & step) != 0
        for k in range(len(rows)):
            if not k & step:
                first, second = rows[k], rows[k + step]
                rows[k] = jnp.where(odd, second, first)
                rows[k + step] = jnp.where(odd, first, second)
    return jnp.concatenate(rows, 0)


def together(*values):
    return lax.optimization_barrier(values)


def pack(gains, columns):
    high = lax.reduce_precision(gains, 8, 7)
    parts = jnp.concatenate([high, gains - high], 0).astype(BF16).reshape(-1, columns)
    return jnp.concatenate([parts, jnp.zeros((-parts.shape[0] % 16, columns), BF16)], 0)


def unpack(rows, width):
    parts = rows[: 4 * width // rows.shape[1]].reshape(4, width).astype(F32)
    return parts[:2] + parts[2:]


def column_tiles(size):
    tile = 256 if size % 256 == 0 else size
    return [slice(c, c + tile) for c in range(0, size, tile)]


def run_mask(rows, offset, length):
    return lax.broadcasted_iota(jnp.int32, (rows, 1), 0) + offset < length


def product(x, weight):
    return jnp.dot(x, weight, preferred_element_type=F32)


def rms_rows(x_ref, gain, out):
    x = x_ref[...].astype(F32)
    xhat = x * lax.rsqrt(jnp.mean(x * x, axis=-1, keepdims=True) + 1e-06)
    out[...] = (xhat * gain[...][None, :]).astype(BF16)


def prepare_kernel(
    fold,
    start,
    arrive,
    place,
    q_hbm,
    s_hbm,
    q_gain,
    s_gain,
    inner,
    outer,
    q_out,
    s_out,
    piece,
    q_ref,
    s_ref,
    sems,
):
    thin = inner.shape[0] // PARTS // fold
    block = inner.shape[1]
    rows = outer.shape[0] // PARTS
    index = place[2]
    tokens = [
        pltpu.make_async_copy(s_hbm, s_ref, sems.at[0]),
        pltpu.make_async_copy(q_hbm, q_ref, sems.at[1]),
    ]
    copies = []
    for i in range(fold):
        first = pl.multiple_of(index * (thin * fold) + i * thin, 16)
        copies.append(
            pltpu.make_async_copy(
                inner.at[pl.ds(first, thin), :],
                piece.at[pl.ds(0, thin), pl.ds(i * block, block)],
                sems.at[2 + i],
            )
        )
    copies.append(
        pltpu.make_async_copy(
            outer.at[pl.ds(pl.multiple_of(index * rows, 16), rows), :],
            piece.at[pl.ds(thin, rows), :],
            sems.at[2 + fold],
        )
    )
    for copy in tokens:
        copy.start()
    start(LOAD)
    for copy in copies:
        copy.start()
    arrive(LOAD)
    tokens[0].wait()
    rms_rows(s_ref, s_gain, s_out)
    tokens[1].wait()
    x = q_ref[...].astype(F32)
    x = x - jnp.mean(x, axis=-1, keepdims=True)
    xhat = x * lax.rsqrt(jnp.mean(x * x, axis=-1, keepdims=True) + 1e-05)
    q_out[...] = (xhat * q_gain[...][None, :]).astype(BF16)
    for copy in copies:
        copy.wait()


def norm_only_kernel(q_ref, s_ref, q_gain, s_gain, q_out, s_out):
    rms_rows(s_ref, s_gain, s_out)
    x = q_ref[...].astype(F32)
    x = x - jnp.mean(x, axis=-1, keepdims=True)
    xhat = x * lax.rsqrt(jnp.mean(x * x, axis=-1, keepdims=True) + 1e-05)
    q_out[...] = (xhat * q_gain[...][None, :]).astype(BF16)


def prepare(place, own_q, own_s, q_gain, s_gain, inner, outer):
    width, block = inner.shape
    fold = width // block
    thin = width // PARTS // fold
    rows = block // PARTS
    if block % 128 == 0:
        return call(
            functools.partial(prepare_kernel, fold),
            [SMEM] + [HBM] * 2 + [LOAD] * 2 + [HBM] * 2,
            [(own_q.shape, BF16), (own_s.shape, BF16), ((thin + rows, width), BF16)],
            [
                pltpu.VMEM(own_q.shape, BF16),
                pltpu.VMEM(own_s.shape, BF16),
                pltpu.SemaphoreType.DMA((fold + 3,)),
            ],
            limit=60,
            staged=True,
        )(place, own_q, own_s, q_gain, s_gain, inner, outer)
    piece = lax.dynamic_slice_in_dim(inner, place[2] * (thin * fold), thin * fold, 0)
    piece = jnp.concatenate([piece[i * thin : (i + 1) * thin] for i in range(fold)], 1)
    other = lax.dynamic_slice_in_dim(outer, place[2] * rows, rows, 0)
    normed = call(norm_only_kernel, [VMEM] * 4, [(own_q.shape, BF16), (own_s.shape, BF16)])(
        own_q, own_s, q_gain, s_gain
    )
    return *normed, jnp.concatenate([piece, other], 0)


def gather_rows(token_refs, rows, sems):
    copies = []
    first = 0
    for i, token in enumerate(token_refs):
        count = token.shape[0]
        copies.append(pltpu.make_async_copy(token, rows.at[pl.ds(first, count), :], sems.at[i]))
        first += count
    for copy in copies:
        copy.start()
    return copies


def forward_kernel(n, far, axis, start, arrive, place, lengths, positive, own, *refs):
    token_refs, refs = refs[:n], refs[n:]
    inners, outers = [refs[0]], [refs[1]]
    pieces = refs[2 : 2 + PARTS * far]
    refs = refs[2 + PARTS * far :]
    width = own.shape[1]
    if far:
        part, *outs = refs[: 2 + far]
        refs = refs[2 + far :]
    else:
        part, outs, refs = refs[0], [refs[0]], refs[1:]
    offset = 0 if far else width
    results, buffers, sems = refs[: 1 + 2 * far], refs[1 + 2 * far : -1], refs[-1]
    rows = buffers[0]
    start(LOAD)
    gathered = gather_rows(token_refs, rows, sems)
    start(LATE)
    leaving = [
        pltpu.make_async_copy(x, y, sems.at[i]) for i, (x, y) in enumerate(zip(buffers, results))
    ]
    arrive(LOAD)
    for copy in gathered:
        copy.wait()
    leaving[0].start()
    me = place[axis]
    span = own.shape[0]
    total = rows.shape[0] // span
    index = lax.broadcasted_iota(jnp.int32, (total, 1), 0)

    def pool(inner, out):
        for columns in column_tiles(inner.shape[1]):
            weight = inner[:, columns]
            tile = jnp.zeros((total, weight.shape[1]), F32)
            for k in range(total):
                length = lengths[me ^ k]
                value = gelu_value(product(rows[k * span : (k + 1) * span, :], weight))
                value = jnp.where(run_mask(span, 0, length), value, 0.0)
                row = jnp.sum(value, axis=0, keepdims=True) / length.astype(F32)
                tile = jnp.where(index == ((me ^ k) & (total - 1)), row, tile)
            out[:, offset + columns.start : offset + columns.stop] = tile

    pool(inners[0], outs[0])
    arrive(LATE)
    y, core = place[3], place[4]
    places = (
        core * 2 + y,
        core * 2 + (1 - y),
        (1 - core) * 2 + y,
        (1 - core) * 2 + (1 - y),
    )
    for f in range(far):
        inner, outer = buffers[1 + 2 * f : 3 + 2 * f]
        block = inner.shape[1]
        fold = inner.shape[0] // block
        thin = inner.shape[0] // PARTS // fold
        deep = block // PARTS
        for j in range(PARTS):
            piece = pieces[PARTS * f + j]
            for i in range(fold):
                first = pl.multiple_of(places[j] * (thin * fold) + i * thin, 16)
                inner[pl.ds(first, thin), :] = piece[:thin, i * block : (i + 1) * block]
            first = pl.multiple_of(places[j] * deep, 16)
            outer[pl.ds(first, deep), :] = piece[thin:, :]
        inners.append(inner)
        outers.append(outer)
    for copy in leaving[1:]:
        copy.start()
    for inner, out in zip(inners[1:], outs[1:]):
        pool(inner, out)
    x = own[...].astype(F32)
    length = lengths[me]
    x = jnp.where(run_mask(span, 0, length), x, 0.0)
    own_row = jnp.sum(x, axis=0, keepdims=True) / length.astype(F32)
    result = jnp.where(index == (me & (total - 1)), own_row, 0.0)
    for outer, out in zip(outers, outs):
        units = out[:, offset : offset + outer.shape[0]]
        high = units.astype(BF16)
        rest = units - high.astype(F32)
        middle = rest.astype(BF16)
        low = (rest - middle.astype(F32)).astype(BF16)
        weight = outer[...]
        result = result + (
            product(high, weight) + (product(middle, weight) + product(low, weight))
        )
    part[:, :width] = result
    if positive is not None:
        lane = lax.broadcasted_iota(jnp.int32, (total, 128), 1)
        row = lax.broadcasted_iota(jnp.int32, (total, 128), 0)
        meta = jnp.zeros((total, 128), F32)
        for k in range(total):
            pair = jnp.where(lane == 0, positive[k], jnp.where(lane == 1, lengths[k], 0))
            meta = jnp.where(row == k, pair.astype(F32), meta)
        part[:, part.shape[1] - 128 :] = meta
    for copy in leaving:
        copy.wait()


def forward(place, lengths, positive, own, tokens, inner, outer, pieces, axis):
    width, units = inner.shape
    far = len(pieces) // PARTS
    rows = sum(t.shape[0] for t in tokens)
    count = rows // own.shape[0]
    large = [(rows, width)] + [(width, units), (units, width)] * far
    columns = width + units + 128
    body = functools.partial(forward_kernel, len(tokens), far, axis)
    if far:
        return call(
            lambda start, arrive, place, lengths, *refs: body(
                start, arrive, place, lengths, None, *refs
            ),
            [SMEM] * 2 + [LATE] + [HBM] * len(tokens) + [LOAD, LATE] + [LATE] * len(pieces),
            [((count, width), F32)]
            + [((count, units), F32)] * (1 + far)
            + [(x, BF16) for x in large],
            [pltpu.VMEM(x, BF16) for x in large]
            + [pltpu.SemaphoreType.DMA((max(len(tokens), len(large)),))],
            flops=3 * 10**9,
            bytes_accessed=3 * 10**6,
            limit=62,
            outs=[VMEM] * (2 + far) + [HBM] * len(large),
            staged=True,
        )(place, lengths, own, *tokens, inner, outer, *pieces)
    return call(
        body,
        [SMEM] * 3 + [LATE] + [HBM] * len(tokens) + [LOAD, LATE],
        [((count, columns), F32)] + [(x, BF16) for x in large],
        [pltpu.VMEM(x, BF16) for x in large] + [pltpu.SemaphoreType.DMA((len(tokens),))],
        flops=3 * 10**9,
        bytes_accessed=3 * 10**6,
        limit=24,
        outs=[VMEM] + [HBM] * len(large),
        staged=True,
    )(place, lengths, positive, own, *tokens, inner, outer)


def slope_kernel(n, axis, span, gathered, place, lengths, *refs):
    token_refs = refs[:n]
    if gathered:
        weights, out, rows = refs[n:-3], refs[-3], refs[-2]
        for copy in gather_rows(token_refs, rows, refs[-1]):
            copy.wait()
    else:
        weights, out, rows = refs[n:-1], refs[-1], token_refs[0]
    me = place[axis] & (lengths.shape[0] - 1)
    base = 0
    for weight in weights:
        for columns in column_tiles(weight.shape[1]):
            w = weight[:, columns]
            for k in range(out.shape[0] // span):
                length = lengths[me ^ k]
                part = slice(k * span, (k + 1) * span)
                value = gelu_slope(product(rows[part, :], w)) * (1.0 / length.astype(F32))
                value = jnp.where(run_mask(span, 0, length), value, 0.0)
                out[part, base + columns.start : base + columns.stop] = value
        base += weight.shape[1]


def slopes(place, lengths, tokens, weights, axis, span):
    gathered = len(tokens) > 1
    rows = sum(t.shape[0] for t in tokens)
    width, units = weights[0].shape[0], sum(w.shape[1] for w in weights)
    return call(
        functools.partial(slope_kernel, len(tokens), axis, span, gathered),
        [SMEM] * 2 + [HBM if gathered else VMEM] * len(tokens) + [VMEM] * len(weights),
        [((rows, units), F32)] + [((rows, width), BF16)] * gathered,
        [pltpu.SemaphoreType.DMA((len(tokens),))] * gathered,
        flops=3 * rows * units * width,
        bytes_accessed=3 * 10**6,
    )(place, lengths, *tokens, *weights)


def inner_gradient(row_refs, slope_refs, hidden, weights, gain, total, span, arrive=None):
    base = 0
    gains = jnp.zeros((total.shape[0], 128), F32)
    for weight in weights:
        for columns in column_tiles(weight.shape[1]):
            part = slice(base + columns.start, base + columns.stop)
            result = 0.0
            k = 0
            for rows, slope in zip(row_refs, slope_refs):
                for first in range(0, rows.shape[0], span):
                    dpre = slope[first : first + span, part] * hidden[k : k + 1, part]
                    result = result + lax.dot_general(
                        rows[first : first + span, :],
                        dpre.astype(BF16),
                        CONTRACT_FIRST,
                        preferred_element_type=F32,
                    )
                    k += 1
            total[:, part] = result
            shares = result * weight[:, columns].astype(F32)
            lanes = shares.shape[1]
            if lanes % 128:
                shares = jnp.concatenate(
                    [shares, jnp.zeros((shares.shape[0], -lanes % 128), F32)], 1
                )
            for c in range(0, shares.shape[1], 128):
                gains = gains + shares[:, c : c + 128]
        base += weight.shape[1]
    if arrive is not None:
        arrive(LOAD)
    return jnp.sum(gains.T, axis=0, keepdims=True) / gain[...][None, :]


def q_backward_kernel(pairs, span, start, arrive, place, *refs):
    start(LOAD)
    rows, pair_rows, own_slope, pair_slope, hidden, weight, gain = refs[:7]
    sends, (keep, gains, total) = refs[7 : 6 + pairs], refs[6 + pairs :]
    gains[...] = inner_gradient(
        [rows, pair_rows], [own_slope, pair_slope], hidden, [weight], gain, total, span, arrive
    )
    mine = place[0] // 2
    size = keep.shape[0]
    keep[...] = total[pl.ds(pl.multiple_of(mine * size, 16), size), :]
    for k in range(1, pairs):
        first = pl.multiple_of((mine ^ k) * size, 16)
        sends[k - 1][...] = total[pl.ds(first, size), :].astype(BF16)


def q_backward(place, rows, slope, pair_rows, pair_slope, hidden, weight, gain, pairs, span):
    width, units = weight.shape
    size = width // pairs
    return call(
        functools.partial(q_backward_kernel, pairs, span),
        [SMEM] + [VMEM] * 6 + [LOAD],
        [((size, units), BF16)] * (pairs - 1) + [((size, units), F32), ((1, width), F32)],
        [pltpu.VMEM((width, units), F32)],
        flops=4 * 10**9,
        bytes_accessed=3 * 10**6,
        staged=True,
    )(place, rows, pair_rows, slope, pair_slope, hidden, weight, gain)


def s_backward_kernel(span, axis, place, lengths, *refs):
    rows, hidden = refs[:2]
    weights = refs[2:-7]
    gain, q_gains, send, keep, gains, total, slope = refs[-7:]
    slope_kernel(1, axis, span, False, place, lengths, rows, *weights, slope)
    s_gains = inner_gradient([rows], [slope], hidden, weights, gain, total, span)
    core = place[4]
    size = keep.shape[0]
    keep[...] = total[pl.ds(pl.multiple_of(core * size, 16), size), :]
    first = pl.multiple_of((1 - core) * size, 16)
    send[...] = total[pl.ds(first, size), :].astype(BF16)
    index = lax.broadcasted_iota(jnp.int32, (GAIN_ROWS, 1), 0)
    packed = jnp.zeros((GAIN_ROWS, total.shape[0]), F32)
    for i, row in enumerate((q_gains[...], s_gains)):
        high = row.astype(BF16).astype(F32)
        packed = jnp.where(index == i, high, packed)
        packed = jnp.where(index == i + 2, row - high, packed)
    gains[...] = packed.astype(BF16)


def s_backward(place, lengths, rows, hidden, weights, gain, q_gains, axis, span):
    width = weights[0].shape[0]
    units = sum(w.shape[1] for w in weights)
    return call(
        functools.partial(s_backward_kernel, span, axis),
        [SMEM] * 2 + [VMEM] * 2 + [LOAD] + [VMEM] * (len(weights) - 1) + [LOAD, VMEM],
        [
            ((width // 2, units), BF16),
            ((width // 2, units), F32),
            ((GAIN_ROWS, width), BF16),
        ],
        [pltpu.VMEM((width, units), F32), pltpu.VMEM((rows.shape[0], units), F32)],
        flops=6 * 10**9,
        bytes_accessed=3 * 10**6,
    )(place, lengths, rows, hidden, *weights, gain, q_gains)


def score_kernel(
    n_sa, n_pb, width, start, arrive, place, q_ref, s_ref, q_outer, *refs
):
    start(LOAD)
    s_outers = refs[:-5]
    loss_ref, q_grad_ref, s_grad_ref, q_hidden, s_hidden = refs[-5:]
    p, a = place[0], place[1]
    q, s = q_ref[:, :width], s_ref[:, :width]
    positive = q_ref[:, q_ref.shape[1] - 128 : q_ref.shape[1] - 127].astype(jnp.int32)
    count = q.shape[0]
    scale = 1.0 / math.sqrt(width)
    score = scale * lax.dot_general(q, s, CONTRACT_LAST, precision=HIGH, preferred_element_type=F32)
    columns = lax.broadcasted_iota(jnp.int32, (count, count), 1)
    match = (positive == columns).astype(F32)
    row_max = jnp.max(score, axis=1, keepdims=True)
    col_max = jnp.max(score, axis=0, keepdims=True)
    row_lse = row_max + jnp.log(jnp.sum(jnp.exp(score - row_max), axis=1, keepdims=True))
    col_lse = col_max + jnp.log(jnp.sum(jnp.exp(score - col_max), axis=0, keepdims=True))
    matched = jnp.sum(match * score, axis=1, keepdims=True)
    row_part = jnp.sum(row_lse - matched, axis=0, keepdims=True)
    col_part = jnp.sum(col_lse, axis=1, keepdims=True) - jnp.sum(matched, axis=0, keepdims=True)
    loss_ref[...] = (row_part + col_part) / (2.0 * count)
    dscore = 0.5 * (jnp.exp(score - row_lse) + jnp.exp(score - col_lse) - 2.0 * match)
    q_grad = scale * jnp.dot(dscore, s, precision=HIGH, preferred_element_type=F32)
    s_grad = scale * lax.dot_general(
        dscore, q, CONTRACT_FIRST, precision=HIGH, preferred_element_type=F32
    )
    q_grad_ref[...] = q_grad
    s_grad_ref[...] = s_grad

    def hidden(grad, places, outers, out):
        rows = places.shape[0]
        chosen = lax.broadcasted_iota(jnp.int32, (rows, count), 1) == places
        picked = jnp.dot(chosen.astype(F32), grad, precision=HIGH, preferred_element_type=F32)
        high = picked.astype(BF16)
        low = (picked - high.astype(F32)).astype(BF16)
        base = 0
        for outer in outers:
            weight = outer[...]
            result = lax.dot_general(high, weight, CONTRACT_LAST, preferred_element_type=F32)
            result += lax.dot_general(low, weight, CONTRACT_LAST, preferred_element_type=F32)
            out[:, base : base + weight.shape[0]] = result
            base += weight.shape[0]

    index = lax.broadcasted_iota(jnp.int32, (2 * n_sa, 1), 0)
    pair = (index >= n_sa).astype(jnp.int32)
    hidden(q_grad, (p ^ pair) * n_sa + (a ^ (index - pair * n_sa)), [q_outer], q_hidden)
    index = lax.broadcasted_iota(jnp.int32, (8, 1), 0)
    arrive(LOAD)
    hidden(s_grad, a * n_pb + (p ^ index), s_outers, s_hidden)


def scores(place, q_all, s_all, q_outer, s_outers, n_sa, n_pb, width):
    shape = (q_all.shape[0], width)
    units = sum(w.shape[0] for w in s_outers)
    return call(
        functools.partial(score_kernel, n_sa, n_pb, width),
        [SMEM] + [VMEM] * 3 + [LOAD] + [VMEM] * (len(s_outers) - 1),
        [
            ((1, 1), F32),
            (shape, F32),
            (shape, F32),
            ((2 * n_sa, q_outer.shape[0]), F32),
            ((8, units), F32),
        ],
        staged=True,
    )(place, q_all, s_all, q_outer, *s_outers)


def assemble_kernel(first, own_rows, packed, continued, place, *refs):
    out, buffer, sems = refs[-3:]
    refs = refs[1:-3] if continued else refs[:-3]
    count = len(refs) - 1 if packed else len(refs) // 2
    chunks, others = refs[:count], refs[count:]
    mine = place[0] // 2
    even = place[0] % 2 == 0
    copies = []
    for k in range(count):
        half = chunks[k].shape[1]
        a = chunks[k][:own_rows, :].astype(F32)
        b = others[0][k * own_rows : (k + 1) * own_rows, :] if packed else others[k][...]
        b = b.astype(F32)
        buffer[k, :, :half] = jnp.where(even, a, b)
        buffer[k, :, half:] = jnp.where(even, b, a)
        place_of = pl.multiple_of((mine ^ (first + k)) * own_rows, 8)
        copies.append(
            pltpu.make_async_copy(buffer.at[k], out.at[pl.ds(place_of, own_rows), :], sems.at[k])
        )
        copies[-1].start()
    for copy in copies:
        copy.wait()


def assemble(place, chunks, others, first, rows, shape, packed=False, earlier=None):
    before = [] if earlier is None else [earlier]
    return call(
        functools.partial(assemble_kernel, first, rows, packed, bool(before)),
        [SMEM] + [HBM] * len(before) + [LOAD] * (len(chunks) + len(others)),
        [(shape, F32)],
        [
            pltpu.VMEM((len(chunks), rows, shape[1]), F32),
            pltpu.SemaphoreType.DMA((len(chunks),)),
        ],
        flops=2 * 10**9,
        bytes_accessed=3 * 10**6,
        outs=[HBM],
        aliases={1: 0} if before else {},
    )(place, *before, *chunks, *others)[0]


def per_device(
    question_states,
    question_ids,
    q_inner_weight,
    q_outer_weight,
    q_norm_gain,
    sql_states,
    sql_ids,
    s_inner_weight,
    s_outer_weight,
    s_norm_gain,
    positive_column,
):
    n_pb, n_sa = lax.axis_size("pb"), lax.axis_size("sa")
    p, a = lax.axis_index("pb"), lax.axis_index("sa")
    width, length = question_states.shape[-1], question_states.shape[-2]
    block = s_inner_weight.shape[1]
    units = q_inner_weight.shape[1]
    half = units // 2
    pairs = n_pb // 2
    far = range(GROUP, n_pb, GROUP)
    y, core = bit_at(a, 2), bit_at(a, 1)
    place = jnp.stack([p, a, core * 2 + y, y, core]).astype(jnp.int32)

    own_q, own_s = question_states[0, 0], sql_states[0, 0]
    q_normed, s_normed, piece = prepare(
        place, own_q, own_s, q_norm_gain, s_norm_gain, s_inner_weight, s_outer_weight
    )
    top = n_sa // 2
    mine = [swap(piece, "pb", k) for k in far]
    beside = [swap(piece, "sa", 1) for piece in mine]
    from_x, from_z = swap(s_normed, "pb", 1), swap(s_normed, "pb", 2)
    q_far = swap(q_normed, "sa", top)
    pair_bit = bit_at(p, 1)
    q_inner_half = lax.dynamic_slice_in_dim(q_inner_weight, pair_bit * half, half, 1)
    q_outer_half = lax.dynamic_slice_in_dim(q_outer_weight, pair_bit * half, half, 0)
    q_lengths = jnp.sum((question_ids[0] > 0).astype(jnp.int32), axis=-1)
    s_lengths = jnp.sum((sql_ids[0] > 0).astype(jnp.int32), axis=-1)
    (
        from_x,
        from_z,
        mine,
        beside,
        q_far,
        q_late,
        q_inner_half,
        q_outer_half,
        q_lengths,
        s_lengths,
    ) = together(
        from_x,
        from_z,
        mine,
        beside,
        q_far,
        q_normed,
        q_inner_half,
        q_outer_half,
        q_lengths,
        s_lengths,
    )

    across = [swap(piece, "sa", 2) for piece in mine]
    from_xz = swap(from_x, "pb", 2)
    pair_token = swap(q_late, "pb", 1)
    q_tokens = [q_normed] + [None] * (n_sa - 1)
    q_tokens[top] = q_far
    for step in reversed(bits_of(n_sa)):
        for k in range(0, n_sa, 2 * step):
            if q_tokens[k + step] is None:
                q_tokens[k + step] = swap(q_tokens[k], "sa", step)

    q_all, q_rows = forward(
        place, q_lengths, positive_column, own_q, q_tokens, q_inner_weight, q_outer_weight, [], 1
    )
    in_part = jnp.arange(q_all.shape[1], dtype=jnp.int32)[None, :] < width

    def add_part(x, step):
        return jnp.where(in_part, x + swap(x, "sa", step), x)

    (own_slope,) = slopes(place, q_lengths, [q_rows], [q_inner_half], 1, length)
    q_steps = list(reversed(bits_of(n_sa)))
    for step in q_steps[:-1]:
        q_all = add_part(q_all, step)
    from_xz, across, q_all, own_slope, pair_token = together(
        from_xz, across, q_all, own_slope, pair_token
    )
    pair_far = swap(pair_token, "sa", top)

    pieces = []
    for one, two, three in zip(mine, across, beside):
        pieces += [one, two, three, swap(two, "sa", 1)]
    s_tokens = [s_normed, from_x, from_z, from_xz]
    q_all = add_part(q_all, q_steps[-1])
    s_part, *s_rest = forward(
        place, s_lengths, None, own_s, s_tokens, s_inner_weight, s_outer_weight, pieces, 0
    )
    s_pooled, s_rows, far_weights = (
        s_rest[: 1 + len(far)],
        s_rest[1 + len(far)],
        s_rest[2 + len(far) :],
    )
    s_inners = [s_inner_weight] + far_weights[0::2]
    s_outers = [s_outer_weight] + far_weights[1::2]

    s_others = [swap(s_part, "pb", k) for k in range(1, GROUP)]
    pair_meta, s_part = together(swap(q_all, "pb", 1), s_part)
    q_all = ordered(q_all, pair_meta, pair_bit)
    pair_lengths = pair_meta[:, width + units + 1].astype(jnp.int32)
    q_all = ordered(q_all, swap(q_all, "pb", 2), bit_at(p, 2))
    s_part = (s_part + s_others[0]) + (s_others[1] + s_others[2])
    pair_tokens = [pair_token] + [None] * (n_sa - 1)
    pair_tokens[top] = pair_far
    for step in reversed(bits_of(n_sa)):
        for k in range(0, n_sa, 2 * step):
            if pair_tokens[k + step] is None:
                pair_tokens[k + step] = swap(pair_tokens[k], "sa", step)
    s_part, q_all, pair_lengths, pair_tokens = together(s_part, q_all, pair_lengths, pair_tokens)

    s_sent = [jnp.concatenate([s_part, s_pooled[0]], 1)]
    for i, k in enumerate(far, 1):
        s_sent.append(swap(jnp.concatenate([s_part, s_pooled[i]], 1), "pb", k))
    s_all = canonical(s_sent, p // GROUP)[None]
    for step in bits_of(n_pb)[2:]:
        q_all = ordered(q_all, swap(q_all, "pb", step), bit_at(p, step))
    pair_slope, pair_rows = slopes(place, pair_lengths, pair_tokens, [q_inner_half], 1, length)
    for step in reversed(bits_of(n_sa)):
        if step == 1:
            s_all, pair_slope = together(s_all, pair_slope)
        s_all = ordered(s_all, swap(s_all, "sa", step), bit_at(a, step))
    order = [
        sum(((i >> b) & 1) << (n_sa.bit_length() - 2 - b) for b in range(n_sa.bit_length() - 1))
        for i in range(n_sa)
    ]
    s_all = jnp.concatenate([s_all[order[i]] for i in range(n_sa)], 0)
    loss, q_grad, s_grad, q_hidden, s_hidden = scores(
        place, q_all, s_all, q_outer_half, s_outers, n_sa, n_pb, width
    )

    *q_sends, q_keep, q_gains = q_backward(
        place,
        q_rows,
        own_slope,
        pair_rows,
        pair_slope,
        q_hidden,
        q_inner_half,
        q_norm_gain,
        pairs,
        length,
    )
    q_arrived = [swap(x, "pb", 2 * k) for k, x in enumerate(q_sends, 1)]
    s_hidden, q_gains = together(s_hidden, q_gains)
    s_send, s_keep, packed = s_backward(
        place, s_lengths, s_rows, s_hidden, s_inners, s_norm_gain, q_gains, 0, length
    )

    def outer_gradient(pooled, grad):
        high = lax.reduce_precision(pooled, 8, 7)
        top = lax.reduce_precision(grad, 8, 7)
        left = jnp.concatenate([high, pooled - high, high], 0).astype(BF16)
        right = jnp.concatenate([top, top, grad - top], 0).astype(BF16)
        return lax.dot_general(left, right, CONTRACT_FIRST, preferred_element_type=F32)

    q_outer_grad = outer_gradient(q_all[:, width : width + units], q_grad)
    s_outer_grad = outer_gradient(s_all[:, width:], s_grad)
    strips = 6
    strip = s_send.shape[0] // strips
    s_beside = [swap(s_send[i * strip : (i + 1) * strip], "sa", 1) for i in range(strips)]
    s_total = s_keep + jnp.concatenate(s_beside, 0).astype(F32)
    q_arrived, s_total, packed, q_outer_grad, s_outer_grad = together(
        q_arrived, s_total, packed, q_outer_grad, s_outer_grad
    )

    q_total = q_keep
    for x in q_arrived:
        q_total = q_total + x.astype(F32)
    q_total = q_total.astype(BF16)
    rows = q_total.shape[0]

    def with_gains(x, gains):
        packed = pack(gains, x.shape[1])
        return jnp.concatenate([x, packed], 0), unpack(packed, width)

    def arrived_gains(x, rows):
        return x[:rows], unpack(x[rows:], width)

    gains = packed[:2].astype(F32) + packed[2:4].astype(F32)
    sent, gains = with_gains(q_total, gains)
    arrivals = [swap(sent, "pb", 2 * k) for k in range(1, pairs)]
    own_other = swap(q_total, "pb", 1)
    first = swap(arrivals[0][:rows], "pb", 1)
    size = width // 2
    for step in bits_of(n_sa)[1:]:
        size = size // 2
        bit = bit_at(a, step)
        away = lax.dynamic_slice_in_dim(s_total, (1 - bit) * size, size, 0).astype(BF16)
        arrived = swap(away, "sa", step)
        s_total = lax.dynamic_slice_in_dim(s_total, bit * size, size, 0)
        s_total = s_total + arrived.astype(F32)
    arrivals, own_other, first, s_total = together(arrivals, own_other, first, s_total)

    sums = [gains] + [arrived_gains(x, rows)[1] for x in arrivals]
    while len(sums) > 1:
        sums = [sums[i] + sums[i + 1] for i in range(0, len(sums), 2)]
    chunks = [q_total] + list(arrivals)
    sent, gains = with_gains(jnp.concatenate([x[:rows] for x in chunks[2:]], 0), sums[0])
    rest = swap(sent, "pb", 1)
    gains = gains + arrived_gains(rest, rows * (pairs - 2))[1]
    shape = (width, 2 * half)
    q_inner_grad = assemble(place, chunks[:2], [own_other, first], 0, rows, shape)
    s_sum = s_total[:, :block]
    for i, k in enumerate(far):
        far_part = s_total[:, (i + 1) * block : (i + 2) * block].astype(BF16)
        s_sum = s_sum + swap(far_part, "pb", k).astype(F32)
    s_sum, gains, q_inner_grad, rest = together(s_sum.astype(BF16), gains, q_inner_grad, rest)
    q_inner_grad = assemble(place, chunks[2:], [rest], 2, rows, shape, True, q_inner_grad)

    for step in reversed(bits_of(n_sa)):
        size = s_sum.shape[0]
        if step == 1:
            s_sum, q_inner_grad = together(s_sum, q_inner_grad)
        sent, gains = with_gains(s_sum, gains)
        arrived, more = arrived_gains(swap(sent, "sa", step), size)
        gains = gains + more
        s_sum = ordered(s_sum, arrived, bit_at(a, step))
    s_inner_grad = s_sum.astype(F32)

    return (
        loss[0, 0],
        q_inner_grad,
        q_outer_grad,
        gains[0],
        s_inner_grad,
        s_outer_grad,
        gains[1],
    )


def solution(mesh):
    placed = (
        P("pb", "sa", None, None),
        P("pb", None, None),
        P(None, "sa"),
        P("sa", None),
        P(),
        P("sa", "pb", None, None),
        P("sa", None, None),
        P(None, "pb"),
        P("pb", None),
        P(),
        P("pb"),
    )
    return jax.shard_map(
        per_device,
        mesh=mesh,
        in_specs=placed,
        out_specs=(P(), P(None, "sa"), P("sa", None), P(), P(None, "pb"), P("pb", None), P()),
        check_vma=False,
    )
```

```python
import functools
import math

import jax
import jax.numpy as jnp
from jax import lax
from jax.experimental import pallas as pl
from jax.experimental.pallas import tpu as pltpu
from jax.sharding import PartitionSpec as P

HIGH = lax.Precision.HIGHEST
F32 = jnp.float32
BF16 = jnp.bfloat16
CONTRACT_FIRST = (((0,), (0,)), ((), ()))
CONTRACT_LAST = (((1,), (1,)), ((), ()))
GROUP = 4
PARTS = 4
GAIN_ROWS = 16
ROOT_HALF = 1.0 / math.sqrt(2.0)
VMEM = pl.BlockSpec(memory_space=pltpu.VMEM)
SMEM = pl.BlockSpec(memory_space=pltpu.SMEM)
HBM = pl.BlockSpec(memory_space=pltpu.HBM)
LOAD = "load"
LATE = "late"


def call(body, in_specs, out_shape, scratch=(), limit=16, flops=0, bytes_accessed=0, outs=None, aliases=None, staged=False):
    loads = [i for i, spec in enumerate(in_specs) if spec in (LOAD, LATE)]
    n_in, n_own = len(in_specs), len(out_shape) + len(scratch)

    def kernel(*refs):
        ins, rest = list(refs[:n_in]), refs[n_in:]
        copies = {}
        for j, i in enumerate(loads):
            buffer = rest[n_own + j]
            copies[i] = pltpu.make_async_copy(ins[i], buffer, rest[-1].at[j])
            ins[i] = buffer

        def start(wanted):
            for i in loads:
                if in_specs[i] is wanted:
                    copies[i].start()

        def arrive(wanted):
            for i in loads:
                if in_specs[i] is wanted:
                    copies[i].wait()

        if staged:
            body(start, arrive, *ins, *rest[:n_own])
        else:
            start(LOAD)
            arrive(LOAD)
            body(*ins, *rest[:n_own])

    def run(*args):
        buffers = [pltpu.VMEM(args[i].shape, args[i].dtype) for i in loads]
        if loads:
            buffers.append(pltpu.SemaphoreType.DMA((len(loads),)))
        return pl.pallas_call(
            kernel,
            in_specs=[HBM if spec in (LOAD, LATE) else spec for spec in in_specs],
            out_shape=tuple(jax.ShapeDtypeStruct(s, t) for s, t in out_shape),
            out_specs=tuple(outs or [VMEM] * len(out_shape)),
            scratch_shapes=list(scratch) + buffers,
            input_output_aliases=aliases or {},
            cost_estimate=pl.CostEstimate(
                flops=flops, bytes_accessed=bytes_accessed, transcendentals=0
            ),
            compiler_params=pltpu.CompilerParams(vmem_limit_bytes=limit * 1024 * 1024),
        )(*args)

    return run


def gelu_value(v):
    return 0.5 * v * (1.0 + lax.erf(v * ROOT_HALF))


def gelu_slope(v):
    return 0.5 * (1.0 + lax.erf(v * ROOT_HALF)) + v * jnp.exp(-0.5 * v * v) * (
        1.0 / math.sqrt(2.0 * math.pi)
    )


def swap(x, axis, step):
    size = lax.axis_size(axis)
    return lax.ppermute(x, axis, [(i, i ^ step) for i in range(size)])


def ordered(mine, other, bit, axis=0):
    return jnp.where(
        bit == 0,
        jnp.concatenate([mine, other], axis),
        jnp.concatenate([other, mine], axis),
    )


def bits_of(size):
    return [1 << i for i in range(size.bit_length() - 1)]


def bit_at(place, step):
    return jnp.where((place & step) != 0, 1, 0)


def canonical(rows, place):
    rows = list(rows)
    for step in bits_of(len(rows)):
        odd = (place & step) != 0
        for k in range(len(rows)):
            if not k & step:
                first, second = rows[k], rows[k + step]
                rows[k] = jnp.where(odd, second, first)
                rows[k + step] = jnp.where(odd, first, second)
    return jnp.concatenate(rows, 0)


def together(*values):
    return lax.optimization_barrier(values)


def pack(gains, columns):
    high = lax.reduce_precision(gains, 8, 7)
    parts = jnp.concatenate([high, gains - high], 0).astype(BF16).reshape(-1, columns)
    return jnp.concatenate([parts, jnp.zeros((-parts.shape[0] % 16, columns), BF16)], 0)


def unpack(rows, width):
    parts = rows[: 4 * width // rows.shape[1]].reshape(4, width).astype(F32)
    return parts[:2] + parts[2:]


def column_tiles(size):
    tile = 256 if size % 256 == 0 else size
    return [slice(c, c + tile) for c in range(0, size, tile)]


def run_mask(rows, offset, length):
    return lax.broadcasted_iota(jnp.int32, (rows, 1), 0) + offset < length


def product(x, weight):
    return jnp.dot(x, weight, preferred_element_type=F32)


def rms_rows(x_ref, gain, out):
    x = x_ref[...].astype(F32)
    xhat = x * lax.rsqrt(jnp.mean(x * x, axis=-1, keepdims=True) + 1e-06)
    out[...] = (xhat * gain[...][None, :]).astype(BF16)


def prepare_kernel(
    fold,
    start,
    arrive,
    place,
    q_hbm,
    s_hbm,
    q_gain,
    s_gain,
    inner,
    outer,
    q_out,
    s_out,
    piece,
    q_ref,
    s_ref,
    sems,
):
    thin = inner.shape[0] // PARTS // fold
    block = inner.shape[1]
    rows = outer.shape[0] // PARTS
    index = place[2]
    tokens = [
        pltpu.make_async_copy(s_hbm, s_ref, sems.at[0]),
        pltpu.make_async_copy(q_hbm, q_ref, sems.at[1]),
    ]
    copies = []
    for i in range(fold):
        first = pl.multiple_of(index * (thin * fold) + i * thin, 16)
        copies.append(
            pltpu.make_async_copy(
                inner.at[pl.ds(first, thin), :],
                piece.at[pl.ds(0, thin), pl.ds(i * block, block)],
                sems.at[2 + i],
            )
        )
    copies.append(
        pltpu.make_async_copy(
            outer.at[pl.ds(pl.multiple_of(index * rows, 16), rows), :],
            piece.at[pl.ds(thin, rows), :],
            sems.at[2 + fold],
        )
    )
    for copy in tokens:
        copy.start()
    start(LOAD)
    for copy in copies:
        copy.start()
    arrive(LOAD)
    tokens[0].wait()
    rms_rows(s_ref, s_gain, s_out)
    tokens[1].wait()
    x = q_ref[...].astype(F32)
    x = x - jnp.mean(x, axis=-1, keepdims=True)
    xhat = x * lax.rsqrt(jnp.mean(x * x, axis=-1, keepdims=True) + 1e-05)
    q_out[...] = (xhat * q_gain[...][None, :]).astype(BF16)
    for copy in copies:
        copy.wait()


def norm_only_kernel(q_ref, s_ref, q_gain, s_gain, q_out, s_out):
    rms_rows(s_ref, s_gain, s_out)
    x = q_ref[...].astype(F32)
    x = x - jnp.mean(x, axis=-1, keepdims=True)
    xhat = x * lax.rsqrt(jnp.mean(x * x, axis=-1, keepdims=True) + 1e-05)
    q_out[...] = (xhat * q_gain[...][None, :]).astype(BF16)


def prepare(place, own_q, own_s, q_gain, s_gain, inner, outer):
    width, block = inner.shape
    fold = width // block
    thin = width // PARTS // fold
    rows = block // PARTS
    if block % 128 == 0:
        return call(
            functools.partial(prepare_kernel, fold),
            [SMEM] + [HBM] * 2 + [LOAD] * 2 + [HBM] * 2,
            [(own_q.shape, BF16), (own_s.shape, BF16), ((thin + rows, width), BF16)],
            [
                pltpu.VMEM(own_q.shape, BF16),
                pltpu.VMEM(own_s.shape, BF16),
                pltpu.SemaphoreType.DMA((fold + 3,)),
            ],
            limit=60,
            staged=True,
        )(place, own_q, own_s, q_gain, s_gain, inner, outer)
    piece = lax.dynamic_slice_in_dim(inner, place[2] * (thin * fold), thin * fold, 0)
    piece = jnp.concatenate([piece[i * thin : (i + 1) * thin] for i in range(fold)], 1)
    other = lax.dynamic_slice_in_dim(outer, place[2] * rows, rows, 0)
    normed = call(norm_only_kernel, [VMEM] * 4, [(own_q.shape, BF16), (own_s.shape, BF16)])(
        own_q, own_s, q_gain, s_gain
    )
    return *normed, jnp.concatenate([piece, other], 0)


def gather_rows(token_refs, rows, sems):
    copies = []
    first = 0
    for i, token in enumerate(token_refs):
        count = token.shape[0]
        copies.append(pltpu.make_async_copy(token, rows.at[pl.ds(first, count), :], sems.at[i]))
        first += count
    for copy in copies:
        copy.start()
    return copies


def forward_kernel(n, far, axis, start, arrive, place, lengths, positive, own, *refs):
    token_refs, refs = refs[:n], refs[n:]
    inners, outers = [refs[0]], [refs[1]]
    pieces = refs[2 : 2 + PARTS * far]
    refs = refs[2 + PARTS * far :]
    width = own.shape[1]
    if far:
        part, *outs = refs[: 2 + far]
        refs = refs[2 + far :]
    else:
        part, outs, refs = refs[0], [refs[0]], refs[1:]
    offset = 0 if far else width
    results, buffers, sems = refs[: 1 + 2 * far], refs[1 + 2 * far : -1], refs[-1]
    rows = buffers[0]
    start(LOAD)
    gathered = gather_rows(token_refs, rows, sems)
    start(LATE)
    leaving = [
        pltpu.make_async_copy(x, y, sems.at[i]) for i, (x, y) in enumerate(zip(buffers, results))
    ]
    arrive(LOAD)
    for copy in gathered:
        copy.wait()
    leaving[0].start()
    me = place[axis]
    span = own.shape[0]
    total = rows.shape[0] // span
    index = lax.broadcasted_iota(jnp.int32, (total, 1), 0)

    def pool(inner, out):
        for columns in column_tiles(inner.shape[1]):
            weight = inner[:, columns]
            tile = jnp.zeros((total, weight.shape[1]), F32)
            for k in range(total):
                length = lengths[me ^ k]
                value = gelu_value(product(rows[k * span : (k + 1) * span, :], weight))
                value = jnp.where(run_mask(span, 0, length), value, 0.0)
                row = jnp.sum(value, axis=0, keepdims=True) / length.astype(F32)
                tile = jnp.where(index == ((me ^ k) & (total - 1)), row, tile)
            out[:, offset + columns.start : offset + columns.stop] = tile

    pool(inners[0], outs[0])
    arrive(LATE)
    y, core = place[3], place[4]
    places = (
        core * 2 + y,
        core * 2 + (1 - y),
        (1 - core) * 2 + y,
        (1 - core) * 2 + (1 - y),
    )
    for f in range(far):
        inner, outer = buffers[1 + 2 * f : 3 + 2 * f]
        block = inner.shape[1]
        fold = inner.shape[0] // block
        thin = inner.shape[0] // PARTS // fold
        deep = block // PARTS
        for j in range(PARTS):
            piece = pieces[PARTS * f + j]
            for i in range(fold):
                first = pl.multiple_of(places[j] * (thin * fold) + i * thin, 16)
                inner[pl.ds(first, thin), :] = piece[:thin, i * block : (i + 1) * block]
            first = pl.multiple_of(places[j] * deep, 16)
            outer[pl.ds(first, deep), :] = piece[thin:, :]
        inners.append(inner)
        outers.append(outer)
    for copy in leaving[1:]:
        copy.start()
    for inner, out in zip(inners[1:], outs[1:]):
        pool(inner, out)
    x = own[...].astype(F32)
    length = lengths[me]
    x = jnp.where(run_mask(span, 0, length), x, 0.0)
    own_row = jnp.sum(x, axis=0, keepdims=True) / length.astype(F32)
    result = jnp.where(index == (me & (total - 1)), own_row, 0.0)
    for outer, out in zip(outers, outs):
        units = out[:, offset : offset + outer.shape[0]]
        high = units.astype(BF16)
        rest = units - high.astype(F32)
        middle = rest.astype(BF16)
        low = (rest - middle.astype(F32)).astype(BF16)
        weight = outer[...]
        result = result + (
            product(high, weight) + (product(middle, weight) + product(low, weight))
        )
    part[:, :width] = result
    if positive is not None:
        lane = lax.broadcasted_iota(jnp.int32, (total, 128), 1)
        row = lax.broadcasted_iota(jnp.int32, (total, 128), 0)
        meta = jnp.zeros((total, 128), F32)
        for k in range(total):
            pair = jnp.where(lane == 0, positive[k], jnp.where(lane == 1, lengths[k], 0))
            meta = jnp.where(row == k, pair.astype(F32), meta)
        part[:, part.shape[1] - 128 :] = meta
    for copy in leaving:
        copy.wait()


def forward(place, lengths, positive, own, tokens, inner, outer, pieces, axis):
    width, units = inner.shape
    far = len(pieces) // PARTS
    rows = sum(t.shape[0] for t in tokens)
    count = rows // own.shape[0]
    large = [(rows, width)] + [(width, units), (units, width)] * far
    columns = width + units + 128
    body = functools.partial(forward_kernel, len(tokens), far, axis)
    if far:
        return call(
            lambda start, arrive, place, lengths, *refs: body(
                start, arrive, place, lengths, None, *refs
            ),
            [SMEM] * 2 + [LATE] + [HBM] * len(tokens) + [LOAD, LATE] + [LATE] * len(pieces),
            [((count, width), F32)]
            + [((count, units), F32)] * (1 + far)
            + [(x, BF16) for x in large],
            [pltpu.VMEM(x, BF16) for x in large]
            + [pltpu.SemaphoreType.DMA((max(len(tokens), len(large)),))],
            flops=3 * 10**9,
            bytes_accessed=3 * 10**6,
            limit=62,
            outs=[VMEM] * (2 + far) + [HBM] * len(large),
            staged=True,
        )(place, lengths, own, *tokens, inner, outer, *pieces)
    return call(
        body,
        [SMEM] * 3 + [LATE] + [HBM] * len(tokens) + [LOAD, LATE],
        [((count, columns), F32)] + [(x, BF16) for x in large],
        [pltpu.VMEM(x, BF16) for x in large] + [pltpu.SemaphoreType.DMA((len(tokens),))],
        flops=3 * 10**9,
        bytes_accessed=3 * 10**6,
        limit=24,
        outs=[VMEM] + [HBM] * len(large),
        staged=True,
    )(place, lengths, positive, own, *tokens, inner, outer)


def slope_kernel(n, axis, span, gathered, place, lengths, *refs):
    token_refs = refs[:n]
    if gathered:
        weights, out, rows = refs[n:-3], refs[-3], refs[-2]
        for copy in gather_rows(token_refs, rows, refs[-1]):
            copy.wait()
    else:
        weights, out, rows = refs[n:-1], refs[-1], token_refs[0]
    me = place[axis] & (lengths.shape[0] - 1)
    base = 0
    for weight in weights:
        for columns in column_tiles(weight.shape[1]):
            w = weight[:, columns]
            for k in range(out.shape[0] // span):
                length = lengths[me ^ k]
                part = slice(k * span, (k + 1) * span)
                value = gelu_slope(product(rows[part, :], w)) * (1.0 / length.astype(F32))
                value = jnp.where(run_mask(span, 0, length), value, 0.0)
                out[part, base + columns.start : base + columns.stop] = value
        base += weight.shape[1]


def slopes(place, lengths, tokens, weights, axis, span):
    gathered = len(tokens) > 1
    rows = sum(t.shape[0] for t in tokens)
    width, units = weights[0].shape[0], sum(w.shape[1] for w in weights)
    return call(
        functools.partial(slope_kernel, len(tokens), axis, span, gathered),
        [SMEM] * 2 + [HBM if gathered else VMEM] * len(tokens) + [VMEM] * len(weights),
        [((rows, units), F32)] + [((rows, width), BF16)] * gathered,
        [pltpu.SemaphoreType.DMA((len(tokens),))] * gathered,
        flops=3 * rows * units * width,
        bytes_accessed=3 * 10**6,
    )(place, lengths, *tokens, *weights)


def inner_gradient(row_refs, slope_refs, hidden, weights, gain, total, span, arrive=None):
    base = 0
    gains = jnp.zeros((total.shape[0], 128), F32)
    for weight in weights:
        for columns in column_tiles(weight.shape[1]):
            part = slice(base + columns.start, base + columns.stop)
            result = 0.0
            k = 0
            for rows, slope in zip(row_refs, slope_refs):
                for first in range(0, rows.shape[0], span):
                    dpre = slope[first : first + span, part] * hidden[k : k + 1, part]
                    result = result + lax.dot_general(
                        rows[first : first + span, :],
                        dpre.astype(BF16),
                        CONTRACT_FIRST,
                        preferred_element_type=F32,
                    )
                    k += 1
            total[:, part] = result
            shares = result * weight[:, columns].astype(F32)
            lanes = shares.shape[1]
            if lanes % 128:
                shares = jnp.concatenate(
                    [shares, jnp.zeros((shares.shape[0], -lanes % 128), F32)], 1
                )
            for c in range(0, shares.shape[1], 128):
                gains = gains + shares[:, c : c + 128]
        base += weight.shape[1]
    if arrive is not None:
        arrive(LOAD)
    return jnp.sum(gains.T, axis=0, keepdims=True) / gain[...][None, :]


def q_backward_kernel(pairs, span, start, arrive, place, *refs):
    start(LOAD)
    arrive(LOAD)
    rows, pair_rows, own_slope, pair_slope, hidden, weight, gain = refs[:7]
    sends, (keep, gains, total) = refs[7 : 6 + pairs], refs[6 + pairs :]
    gains[...] = inner_gradient(
        [rows, pair_rows], [own_slope, pair_slope], hidden, [weight], gain, total, span
    )
    mine = place[0] // 2
    size = keep.shape[0]
    keep[...] = total[pl.ds(pl.multiple_of(mine * size, 16), size), :]
    for k in range(1, pairs):
        first = pl.multiple_of((mine ^ k) * size, 16)
        sends[k - 1][...] = total[pl.ds(first, size), :].astype(BF16)


def q_backward(place, rows, slope, pair_rows, pair_slope, hidden, weight, gain, pairs, span):
    width, units = weight.shape
    size = width // pairs
    return call(
        functools.partial(q_backward_kernel, pairs, span),
        [SMEM] + [VMEM] * 6 + [LOAD],
        [((size, units), BF16)] * (pairs - 1) + [((size, units), F32), ((1, width), F32)],
        [pltpu.VMEM((width, units), F32)],
        flops=4 * 10**9,
        bytes_accessed=3 * 10**6,
        staged=True,
    )(place, rows, pair_rows, slope, pair_slope, hidden, weight, gain)


def s_backward_kernel(span, axis, place, lengths, *refs):
    rows, hidden = refs[:2]
    weights = refs[2:-7]
    gain, q_gains, send, keep, gains, total, slope = refs[-7:]
    slope_kernel(1, axis, span, False, place, lengths, rows, *weights, slope)
    s_gains = inner_gradient([rows], [slope], hidden, weights, gain, total, span)
    core = place[4]
    size = keep.shape[0]
    keep[...] = total[pl.ds(pl.multiple_of(core * size, 16), size), :]
    first = pl.multiple_of((1 - core) * size, 16)
    send[...] = total[pl.ds(first, size), :].astype(BF16)
    index = lax.broadcasted_iota(jnp.int32, (GAIN_ROWS, 1), 0)
    packed = jnp.zeros((GAIN_ROWS, total.shape[0]), F32)
    for i, row in enumerate((q_gains[...], s_gains)):
        high = row.astype(BF16).astype(F32)
        packed = jnp.where(index == i, high, packed)
        packed = jnp.where(index == i + 2, row - high, packed)
    gains[...] = packed.astype(BF16)


def s_backward(place, lengths, rows, hidden, weights, gain, q_gains, axis, span):
    width = weights[0].shape[0]
    units = sum(w.shape[1] for w in weights)
    return call(
        functools.partial(s_backward_kernel, span, axis),
        [SMEM] * 2 + [VMEM] * 2 + [LOAD] + [VMEM] * (len(weights) - 1) + [LOAD, VMEM],
        [
            ((width // 2, units), BF16),
            ((width // 2, units), F32),
            ((GAIN_ROWS, width), BF16),
        ],
        [pltpu.VMEM((width, units), F32), pltpu.VMEM((rows.shape[0], units), F32)],
        flops=6 * 10**9,
        bytes_accessed=3 * 10**6,
    )(place, lengths, rows, hidden, *weights, gain, q_gains)


def score_kernel(
    n_sa, n_pb, width, start, arrive, place, q_ref, s_ref, q_outer, *refs
):
    start(LOAD)
    arrive(LOAD)
    s_outers = refs[:-5]
    loss_ref, q_grad_ref, s_grad_ref, q_hidden, s_hidden = refs[-5:]
    p, a = place[0], place[1]
    q, s = q_ref[:, :width], s_ref[:, :width]
    positive = q_ref[:, q_ref.shape[1] - 128 : q_ref.shape[1] - 127].astype(jnp.int32)
    count = q.shape[0]
    scale = 1.0 / math.sqrt(width)
    score = scale * lax.dot_general(q, s, CONTRACT_LAST, precision=HIGH, preferred_element_type=F32)
    columns = lax.broadcasted_iota(jnp.int32, (count, count), 1)
    match = (positive == columns).astype(F32)
    row_max = jnp.max(score, axis=1, keepdims=True)
    col_max = jnp.max(score, axis=0, keepdims=True)
    row_lse = row_max + jnp.log(jnp.sum(jnp.exp(score - row_max), axis=1, keepdims=True))
    col_lse = col_max + jnp.log(jnp.sum(jnp.exp(score - col_max), axis=0, keepdims=True))
    matched = jnp.sum(match * score, axis=1, keepdims=True)
    row_part = jnp.sum(row_lse - matched, axis=0, keepdims=True)
    col_part = jnp.sum(col_lse, axis=1, keepdims=True) - jnp.sum(matched, axis=0, keepdims=True)
    loss_ref[...] = (row_part + col_part) / (2.0 * count)
    dscore = 0.5 * (jnp.exp(score - row_lse) + jnp.exp(score - col_lse) - 2.0 * match)
    q_grad = scale * jnp.dot(dscore, s, precision=HIGH, preferred_element_type=F32)
    s_grad = scale * lax.dot_general(
        dscore, q, CONTRACT_FIRST, precision=HIGH, preferred_element_type=F32
    )
    q_grad_ref[...] = q_grad
    s_grad_ref[...] = s_grad

    def hidden(grad, places, outers, out):
        rows = places.shape[0]
        chosen = lax.broadcasted_iota(jnp.int32, (rows, count), 1) == places
        picked = jnp.dot(chosen.astype(F32), grad, precision=HIGH, preferred_element_type=F32)
        high = picked.astype(BF16)
        low = (picked - high.astype(F32)).astype(BF16)
        base = 0
        for outer in outers:
            weight = outer[...]
            result = lax.dot_general(high, weight, CONTRACT_LAST, preferred_element_type=F32)
            result += lax.dot_general(low, weight, CONTRACT_LAST, preferred_element_type=F32)
            out[:, base : base + weight.shape[0]] = result
            base += weight.shape[0]

    index = lax.broadcasted_iota(jnp.int32, (2 * n_sa, 1), 0)
    pair = (index >= n_sa).astype(jnp.int32)
    hidden(q_grad, (p ^ pair) * n_sa + (a ^ (index - pair * n_sa)), [q_outer], q_hidden)
    index = lax.broadcasted_iota(jnp.int32, (8, 1), 0)
    hidden(s_grad, a * n_pb + (p ^ index), s_outers, s_hidden)


def scores(place, q_all, s_all, q_outer, s_outers, n_sa, n_pb, width):
    shape = (q_all.shape[0], width)
    units = sum(w.shape[0] for w in s_outers)
    return call(
        functools.partial(score_kernel, n_sa, n_pb, width),
        [SMEM] + [VMEM] * 3 + [LOAD] + [VMEM] * (len(s_outers) - 1),
        [
            ((1, 1), F32),
            (shape, F32),
            (shape, F32),
            ((2 * n_sa, q_outer.shape[0]), F32),
            ((8, units), F32),
        ],
        staged=True,
    )(place, q_all, s_all, q_outer, *s_outers)


def assemble_kernel(first, own_rows, packed, continued, place, *refs):
    out, buffer, sems = refs[-3:]
    refs = refs[1:-3] if continued else refs[:-3]
    count = len(refs) - 1 if packed else len(refs) // 2
    chunks, others = refs[:count], refs[count:]
    mine = place[0] // 2
    even = place[0] % 2 == 0
    copies = []
    for k in range(count):
        half = chunks[k].shape[1]
        a = chunks[k][:own_rows, :].astype(F32)
        b = others[0][k * own_rows : (k + 1) * own_rows, :] if packed else others[k][...]
        b = b.astype(F32)
        buffer[k, :, :half] = jnp.where(even, a, b)
        buffer[k, :, half:] = jnp.where(even, b, a)
        place_of = pl.multiple_of((mine ^ (first + k)) * own_rows, 8)
        copies.append(
            pltpu.make_async_copy(buffer.at[k], out.at[pl.ds(place_of, own_rows), :], sems.at[k])
        )
        copies[-1].start()
    for copy in copies:
        copy.wait()


def assemble(place, chunks, others, first, rows, shape, packed=False, earlier=None):
    before = [] if earlier is None else [earlier]
    return call(
        functools.partial(assemble_kernel, first, rows, packed, bool(before)),
        [SMEM] + [HBM] * len(before) + [LOAD] * (len(chunks) + len(others)),
        [(shape, F32)],
        [
            pltpu.VMEM((len(chunks), rows, shape[1]), F32),
            pltpu.SemaphoreType.DMA((len(chunks),)),
        ],
        flops=2 * 10**9,
        bytes_accessed=3 * 10**6,
        outs=[HBM],
        aliases={1: 0} if before else {},
    )(place, *before, *chunks, *others)[0]


def per_device(
    question_states,
    question_ids,
    q_inner_weight,
    q_outer_weight,
    q_norm_gain,
    sql_states,
    sql_ids,
    s_inner_weight,
    s_outer_weight,
    s_norm_gain,
    positive_column,
):
    n_pb, n_sa = lax.axis_size("pb"), lax.axis_size("sa")
    p, a = lax.axis_index("pb"), lax.axis_index("sa")
    width, length = question_states.shape[-1], question_states.shape[-2]
    block = s_inner_weight.shape[1]
    units = q_inner_weight.shape[1]
    half = units // 2
    pairs = n_pb // 2
    far = range(GROUP, n_pb, GROUP)
    y, core = bit_at(a, 2), bit_at(a, 1)
    place = jnp.stack([p, a, core * 2 + y, y, core]).astype(jnp.int32)

    own_q, own_s = question_states[0, 0], sql_states[0, 0]
    q_normed, s_normed, piece = prepare(
        place, own_q, own_s, q_norm_gain, s_norm_gain, s_inner_weight, s_outer_weight
    )
    top = n_sa // 2
    mine = [swap(piece, "pb", k) for k in far]
    beside = [swap(piece, "sa", 1) for piece in mine]
    from_x, from_z = swap(s_normed, "pb", 1), swap(s_normed, "pb", 2)
    q_far = swap(q_normed, "sa", top)
    pair_bit = bit_at(p, 1)
    q_inner_half = lax.dynamic_slice_in_dim(q_inner_weight, pair_bit * half, half, 1)
    q_outer_half = lax.dynamic_slice_in_dim(q_outer_weight, pair_bit * half, half, 0)
    q_lengths = jnp.sum((question_ids[0] > 0).astype(jnp.int32), axis=-1)
    s_lengths = jnp.sum((sql_ids[0] > 0).astype(jnp.int32), axis=-1)
    (
        from_x,
        from_z,
        mine,
        beside,
        q_far,
        q_late,
        q_inner_half,
        q_outer_half,
        q_lengths,
        s_lengths,
    ) = together(
        from_x,
        from_z,
        mine,
        beside,
        q_far,
        q_normed,
        q_inner_half,
        q_outer_half,
        q_lengths,
        s_lengths,
    )

    across = [swap(piece, "sa", 2) for piece in mine]
    from_xz = swap(from_x, "pb", 2)
    pair_token = swap(q_late, "pb", 1)
    q_tokens = [q_normed] + [None] * (n_sa - 1)
    q_tokens[top] = q_far
    for step in reversed(bits_of(n_sa)):
        for k in range(0, n_sa, 2 * step):
            if q_tokens[k + step] is None:
                q_tokens[k + step] = swap(q_tokens[k], "sa", step)

    q_all, q_rows = forward(
        place, q_lengths, positive_column, own_q, q_tokens, q_inner_weight, q_outer_weight, [], 1
    )
    in_part = jnp.arange(q_all.shape[1], dtype=jnp.int32)[None, :] < width

    def add_part(x, step):
        return jnp.where(in_part, x + swap(x, "sa", step), x)

    (own_slope,) = slopes(place, q_lengths, [q_rows], [q_inner_half], 1, length)
    q_steps = list(reversed(bits_of(n_sa)))
    for step in q_steps[:-1]:
        q_all = add_part(q_all, step)
    from_xz, across, q_all, own_slope, pair_token = together(
        from_xz, across, q_all, own_slope, pair_token
    )
    pair_far = swap(pair_token, "sa", top)

    pieces = []
    for one, two, three in zip(mine, across, beside):
        pieces += [one, two, three, swap(two, "sa", 1)]
    s_tokens = [s_normed, from_x, from_z, from_xz]
    q_all = add_part(q_all, q_steps[-1])
    s_part, *s_rest = forward(
        place, s_lengths, None, own_s, s_tokens, s_inner_weight, s_outer_weight, pieces, 0
    )
    s_pooled, s_rows, far_weights = (
        s_rest[: 1 + len(far)],
        s_rest[1 + len(far)],
        s_rest[2 + len(far) :],
    )
    s_inners = [s_inner_weight] + far_weights[0::2]
    s_outers = [s_outer_weight] + far_weights[1::2]

    s_others = [swap(s_part, "pb", k) for k in range(1, GROUP)]
    pair_meta, s_part = together(swap(q_all, "pb", 1), s_part)
    q_all = ordered(q_all, pair_meta, pair_bit)
    pair_lengths = pair_meta[:, width + units + 1].astype(jnp.int32)
    q_all = ordered(q_all, swap(q_all, "pb", 2), bit_at(p, 2))
    s_part = (s_part + s_others[0]) + (s_others[1] + s_others[2])
    pair_tokens = [pair_token] + [None] * (n_sa - 1)
    pair_tokens[top] = pair_far
    for step in reversed(bits_of(n_sa)):
        for k in range(0, n_sa, 2 * step):
            if pair_tokens[k + step] is None:
                pair_tokens[k + step] = swap(pair_tokens[k], "sa", step)
    s_part, q_all, pair_lengths, pair_tokens = together(s_part, q_all, pair_lengths, pair_tokens)

    s_sent = [jnp.concatenate([s_part, s_pooled[0]], 1)]
    for i, k in enumerate(far, 1):
        s_sent.append(swap(jnp.concatenate([s_part, s_pooled[i]], 1), "pb", k))
    s_all = canonical(s_sent, p // GROUP)[None]
    for step in bits_of(n_pb)[2:]:
        q_all = ordered(q_all, swap(q_all, "pb", step), bit_at(p, step))
    pair_slope, pair_rows = slopes(place, pair_lengths, pair_tokens, [q_inner_half], 1, length)
    for step in reversed(bits_of(n_sa)):
        if step == 1:
            s_all, pair_slope = together(s_all, pair_slope)
        s_all = ordered(s_all, swap(s_all, "sa", step), bit_at(a, step))
    order = [
        sum(((i >> b) & 1) << (n_sa.bit_length() - 2 - b) for b in range(n_sa.bit_length() - 1))
        for i in range(n_sa)
    ]
    s_all = jnp.concatenate([s_all[order[i]] for i in range(n_sa)], 0)
    loss, q_grad, s_grad, q_hidden, s_hidden = scores(
        place, q_all, s_all, q_outer_half, s_outers, n_sa, n_pb, width
    )

    *q_sends, q_keep, q_gains = q_backward(
        place,
        q_rows,
        own_slope,
        pair_rows,
        pair_slope,
        q_hidden,
        q_inner_half,
        q_norm_gain,
        pairs,
        length,
    )
    q_arrived = [swap(x, "pb", 2 * k) for k, x in enumerate(q_sends, 1)]
    s_hidden, q_gains = together(s_hidden, q_gains)
    s_send, s_keep, packed = s_backward(
        place, s_lengths, s_rows, s_hidden, s_inners, s_norm_gain, q_gains, 0, length
    )

    def outer_gradient(pooled, grad):
        high = lax.reduce_precision(pooled, 8, 7)
        top = lax.reduce_precision(grad, 8, 7)
        left = jnp.concatenate([high, pooled - high, high], 0).astype(BF16)
        right = jnp.concatenate([top, top, grad - top], 0).astype(BF16)
        return lax.dot_general(left, right, CONTRACT_FIRST, preferred_element_type=F32)

    q_outer_grad = outer_gradient(q_all[:, width : width + units], q_grad)
    s_outer_grad = outer_gradient(s_all[:, width:], s_grad)
    strips = 6
    strip = s_send.shape[0] // strips
    s_beside = [swap(s_send[i * strip : (i + 1) * strip], "sa", 1) for i in range(strips)]
    s_total = s_keep + jnp.concatenate(s_beside, 0).astype(F32)
    q_arrived, s_total, packed, q_outer_grad, s_outer_grad = together(
        q_arrived, s_total, packed, q_outer_grad, s_outer_grad
    )

    q_total = q_keep
    for x in q_arrived:
        q_total = q_total + x.astype(F32)
    q_total = q_total.astype(BF16)
    rows = q_total.shape[0]

    def with_gains(x, gains):
        packed = pack(gains, x.shape[1])
        return jnp.concatenate([x, packed], 0), unpack(packed, width)

    def arrived_gains(x, rows):
        return x[:rows], unpack(x[rows:], width)

    gains = packed[:2].astype(F32) + packed[2:4].astype(F32)
    sent, gains = with_gains(q_total, gains)
    arrivals = [swap(sent, "pb", 2 * k) for k in range(1, pairs)]
    own_other = swap(q_total, "pb", 1)
    first = swap(arrivals[0][:rows], "pb", 1)
    size = width // 2
    for step in bits_of(n_sa)[1:]:
        size = size // 2
        bit = bit_at(a, step)
        away = lax.dynamic_slice_in_dim(s_total, (1 - bit) * size, size, 0).astype(BF16)
        arrived = swap(away, "sa", step)
        s_total = lax.dynamic_slice_in_dim(s_total, bit * size, size, 0)
        s_total = s_total + arrived.astype(F32)
    arrivals, own_other, first, s_total = together(arrivals, own_other, first, s_total)

    sums = [gains] + [arrived_gains(x, rows)[1] for x in arrivals]
    while len(sums) > 1:
        sums = [sums[i] + sums[i + 1] for i in range(0, len(sums), 2)]
    chunks = [q_total] + list(arrivals)
    sent, gains = with_gains(jnp.concatenate([x[:rows] for x in chunks[2:]], 0), sums[0])
    rest = swap(sent, "pb", 1)
    gains = gains + arrived_gains(rest, rows * (pairs - 2))[1]
    shape = (width, 2 * half)
    q_inner_grad = assemble(place, chunks[:2], [own_other, first], 0, rows, shape)
    s_sum = s_total[:, :block]
    for i, k in enumerate(far):
        far_part = s_total[:, (i + 1) * block : (i + 2) * block].astype(BF16)
        s_sum = s_sum + swap(far_part, "pb", k).astype(F32)
    s_sum, gains, q_inner_grad, rest = together(s_sum.astype(BF16), gains, q_inner_grad, rest)
    q_inner_grad = assemble(place, chunks[2:], [rest], 2, rows, shape, True, q_inner_grad)

    for step in reversed(bits_of(n_sa)):
        size = s_sum.shape[0]
        if step == 1:
            s_sum, q_inner_grad = together(s_sum, q_inner_grad)
        sent, gains = with_gains(s_sum, gains)
        arrived, more = arrived_gains(swap(sent, "sa", step), size)
        gains = gains + more
        s_sum = ordered(s_sum, arrived, bit_at(a, step))
    s_inner_grad = s_sum.astype(F32)

    return (
        loss[0, 0],
        q_inner_grad,
        q_outer_grad,
        gains[0],
        s_inner_grad,
        s_outer_grad,
        gains[1],
    )


def solution(mesh):
    placed = (
        P("pb", "sa", None, None),
        P("pb", None, None),
        P(None, "sa"),
        P("sa", None),
        P(),
        P("sa", "pb", None, None),
        P("sa", None, None),
        P(None, "pb"),
        P("pb", None),
        P(),
        P("pb"),
    )
    return jax.shard_map(
        per_device,
        mesh=mesh,
        in_specs=placed,
        out_specs=(P(), P(None, "sa"), P("sa", None), P(), P(None, "pb"), P("pb", None), P()),
        check_vma=False,
    )
```
